256 devices in a mesh: dp: 32 (over z, y_hi, core), tensor: 8 (over y_lo, x).
Axes of the slice: x: 4, y: 4 (y_hi: 2, y_lo: 2; y = y_hi * 2 + y_lo), z: 8, core: 2. Of those that a mesh axis runs over, the one named last changes fastest.
Arguments:
- x_ckpt: bfloat16 [10240, 5120], P('dp', 'tensor'), may hold values from -6 to 6
- norm_gain_vector: float32 [5120], replicated, may hold values from 0.25 to 1.75
- w_qkv: bfloat16 [5120, 3, 3072], P(None, None, 'tensor'), may hold values from -4 to 4
- segments: int32 [10240], P('dp'), may hold values from 0 to 212, never falling along the last dimension, each value on 1 to 96 neighbouring positions
- d_context: bfloat16 [10240, 3072], P('dp', 'tensor'), may hold values from -6 to 6
Outputs:
- input_gradient: bfloat16 [10240, 5120], P('dp', 'tensor')
- gain_gradient: float32 [5120], P('tensor')
- d_weight: bfloat16 [5120, 3, 3072], P('dp', None, 'tensor')
The draws below stay inside these ranges and needn't reach their ends.
Inputs may be any that keep to these rules, and one draw needn't show every extreme that they name: `segments`: segment numbers never fall along the tokens.
All inputs are finite; a program needn't handle non-finite values.
Results may differ from the reference program's by a relative error of at most 0.022.
Values may be sent and summed in bfloat16 or wider, within the bound.
No kernel may reach another device: no remote copies, remote signals or barrier semaphores. Data moves between devices by JAX's collectives and lax.ppermute only.
A program may use at most 192 MiB of HBM per device.

```python
import math
import jax
import jax.numpy as jnp
import numpy as np
from jax import lax

D = 5120
H = 24
HD = 128
TOK_DEV = 320
TOKENS = 10240
N_DP = 32


def draw_w_qkv(key, part):
    key = jax.random.fold_in(key, 11)
    base = jax.random.normal(key, (D, 3, H * HD), jnp.float32) / math.sqrt(D)
    return jnp.clip(base, -4.0, 4.0).astype(jnp.bfloat16)


def level_of(rng, dims, cuts, smallest, high):
    gain, own = 1.0, jax.random.fold_in(rng, 6)
    for axis_at, shards_of in cuts:
        steps = jnp.exp(jax.random.uniform(jax.random.fold_in(own, axis_at), (shards_of,), jnp.float32, smallest / len(cuts), high / len(cuts)))
        gain = gain * jnp.repeat(steps, dims[axis_at] // shards_of).reshape([-1 if axis == axis_at else 1 for axis in range(len(dims))])
    return gain


def length_profile(count, total, reach, slope):
    weights = [(1 << 20) // math.isqrt(grade ** slope) + 1 for grade in range(2, count + 1)]
    spare, given = total - reach - (count - 1), [1] * (count - 1)
    while spare > 0:
        free = [i for i in range(count - 1) if given[i] < reach]
        pool, budget = sum([weights[i] for i in free]), spare
        for i in free:
            extra = min(reach - given[i], max(1, budget * weights[i] // pool), spare)
            given[i] = given[i] + extra
            spare = spare - extra
    return np.array([reach] + given)


def uneven(rng, number_of, total, most, lean):
    if number_of == 2:
        one = jax.random.randint(rng, (), max(1, total - most), min(most, total - 1) + 1)
        return jnp.stack([one, total - one])
    sizes = jnp.asarray(length_profile(number_of, total, most, lean), jnp.int32)
    twos = (number_of - 1) // 2
    donor, receiver = sizes[1:1 + 2 * twos:2], sizes[2:2 + 2 * twos:2]
    slack = jnp.minimum(donor - 1, most - receiver)
    shifted = jax.random.randint(jax.random.fold_in(rng, 1), (twos,), 0, 1 << 20) % (slack + 1)
    sizes = sizes.at[1:1 + 2 * twos:2].set(donor - shifted).at[2:2 + 2 * twos:2].set(receiver + shifted)
    return sizes[jax.random.permutation(jax.random.fold_in(rng, 2), number_of)]


def scatter_about(key, dims, spread, limit, cuts=(), held_as=jnp.bfloat16):
    entries = jax.random.normal(key, dims, jnp.float32) * spread
    if len(cuts) > 0:
        entries = level_of(key, dims, cuts, -0.22, 0.18) * entries
    return jnp.clip(entries, min=-limit, max=limit).astype(held_as)


def setup_inputs(seed: int = 0) -> dict:
    streams_of = jax.random.split(jax.random.key(seed), 6)
    x_ckpt = scatter_about(streams_of[0], (TOKENS, D), 1.0, 6.0, ((0, 32), (1, 8)))
    norm_gain_vector = jnp.clip(1.0 + 0.15 * jax.random.normal(streams_of[1], (D,), jnp.float32), 0.25, 1.75)
    w_qkv = draw_w_qkv(jax.random.fold_in(streams_of[5], 71), 0)
    segments = jnp.searchsorted(jnp.cumsum(uneven(streams_of[3], TOKENS // 48, TOKENS, 96, 1)), jnp.arange(TOKENS), side="right").astype(jnp.int32)
    d_context = scatter_about(streams_of[4], (TOKENS, H * HD), 1.0, 6.0, ((0, 32), (1, 8)))
    return {"x_ckpt": x_ckpt, "norm_gain_vector": norm_gain_vector, "w_qkv": w_qkv, "segments": segments, "d_context": d_context}


def rotate(values, cosines, sines):
    half_size = values.shape[-1] // 2
    first = values[..., :half_size]
    second = values[..., half_size:]
    return jnp.concatenate([first * cosines - second * sines, second * cosines + first * sines], axis=-1)

def rope_tables(length, head_size):
    half_size = head_size // 2
    positions = jnp.arange(length, dtype=jnp.float32)[:, None, None]
    inv_freq = 10000.0 ** (-(2.0 * jnp.arange(half_size, dtype=jnp.float32)) / head_size)
    angles = positions * inv_freq[None, None, :]
    return (jnp.cos(angles), jnp.sin(angles))

def attend(queries, key_rows, values, allowed, cosines, sines):
    rotated_q = rotate(queries, cosines, sines)
    rotated_k = rotate(key_rows, cosines, sines)
    scale = queries.shape[-1] ** (-0.5)
    scores = jnp.einsum('qhd,khd->hqk', rotated_q, rotated_k, precision=lax.Precision.HIGHEST) * scale
    scores = jnp.where(allowed[None], scores, -1e+30)
    weights = jax.nn.softmax(scores, axis=-1)
    return jnp.einsum('hqk,khd->qhd', weights, values, precision=lax.Precision.HIGHEST)

def reference(x_ckpt, norm_gain_vector, w_qkv, segments, d_context):
    weight_flat = w_qkv.reshape(D, 3 * H * HD)
    cosines, sines = rope_tables(TOK_DEV, HD)
    row_ids = jnp.arange(TOK_DEV, dtype=jnp.int32)

    def one_rank(block):
        x_rows, seg_rows, cot_rows = block
        input_rows = x_rows.astype(jnp.float32)
        row_inverse_scale = jnp.sqrt(lax.optimization_barrier(jnp.mean(input_rows * input_rows, axis=1, keepdims=True)) + 1e-05)
        unit_rows = input_rows / row_inverse_scale
        normalized_rows = (unit_rows * norm_gain_vector).astype(jnp.bfloat16)
        packed = jnp.dot(normalized_rows, weight_flat, preferred_element_type=jnp.float32).astype(jnp.bfloat16)
        heads_data = packed.astype(jnp.float32).reshape(TOK_DEV, 3, H, HD)
        allowed = (seg_rows[:, None] == seg_rows[None, :]) & (row_ids[None, :] <= row_ids[:, None])

        def attend_local(queries, key_rows, values):
            return attend(queries, key_rows, values, allowed, cosines, sines)
        _, pullback = jax.vjp(attend_local, heads_data[:, 0], heads_data[:, 1], heads_data[:, 2])
        pulled = pullback(cot_rows.astype(jnp.float32).reshape(TOK_DEV, H, HD))
        d_packed = jnp.stack(pulled, axis=1).reshape(TOK_DEV, 3 * H * HD).astype(jnp.bfloat16)
        normalized_gradient = lax.dot_general(d_packed, weight_flat, (((1,), (1,)), ((), ())), preferred_element_type=jnp.float32)
        rescaled_rows = normalized_gradient * norm_gain_vector
        row_inner_product = lax.optimization_barrier(jnp.mean(rescaled_rows * unit_rows, axis=1, keepdims=True))
        input_gradient = ((rescaled_rows - unit_rows * row_inner_product) / row_inverse_scale).astype(jnp.bfloat16)
        gain_contribution = lax.optimization_barrier(jnp.sum(normalized_gradient * unit_rows, axis=0))
        return (normalized_rows, d_packed, input_gradient, gain_contribution)
    blocks = (x_ckpt.reshape(N_DP, TOK_DEV, D), segments.reshape(N_DP, TOK_DEV), d_context.reshape(N_DP, TOK_DEV, H * HD))
    normalized_rows, d_packed, input_gradient, gain_terms = lax.map(one_rank, blocks)
    d_weight = lax.dot_general(normalized_rows.reshape(TOKENS, D), d_packed.reshape(TOKENS, 3 * H * HD), (((0,), (0,)), ((), ())), preferred_element_type=jnp.float32)
    gain_gradient = lax.optimization_barrier(jnp.sum(gain_terms, axis=0))
    return (input_gradient.reshape(TOKENS, D), gain_gradient, d_weight.reshape(D, 3, H * HD).astype(jnp.bfloat16))
```

```python
import jax
import jax.numpy as jnp
from jax import lax
from jax.experimental import pallas as pl
from jax.experimental.pallas import tpu as pltpu
from jax.sharding import Mesh, PartitionSpec as P

HD = 128
HEADS = 3
TOK = 320
D = 5120
COLS = 1152
SHARE = 640
PW = 256
QW = 384
BF = jnp.bfloat16
F32 = jnp.float32
VMEM_LIMIT = 44 * 1024 * 1024


def dot(a, b, dims):
    return lax.dot_general(a, b, (dims, ((), ())), preferred_element_type=F32)


NN = ((1,), (0,))
NT = ((1,), (1,))
TN = ((0,), (0,))


def cost(flops, nbytes):
    return pl.CostEstimate(flops=flops, bytes_accessed=nbytes, transcendentals=0)


def square_sum(values):
    width = values.shape[1]
    squares = values * values
    total = squares[:, :128]
    for start in range(128, width, 128):
        total = total + squares[:, start : start + 128]
    return total


def absorb(x, gain_ref, places, w_slot, sums):
    width = x.shape[1] // len(places)
    values = x.astype(F32)
    gains = jnp.concatenate([gain_ref[t] for t in places], axis=1)
    sums = square_sum(values) if sums is None else sums + square_sum(values)
    return dot((values * gains).astype(BF), w_slot, NN), sums


def project_first(place_ref, p_ref, q_ref, gp_ref, gq_ref, w_ref, acc_ref, sq_ref, wp, wq, sems):
    places_p = [place_ref[k] for k in range(4)]
    places_q = [place_ref[0], place_ref[4]]
    copies = []
    for i, t in enumerate(places_p):
        copies.append(
            pltpu.make_async_copy(w_ref.at[t, pl.ds(0, PW)], wp.at[pl.ds(i * PW, PW)], sems.at[i])
        )
    for i, t in enumerate(places_q):
        copies.append(
            pltpu.make_async_copy(
                w_ref.at[t, pl.ds(PW, QW)], wq.at[pl.ds(i * QW, QW)], sems.at[4 + i]
            )
        )
    for c in copies:
        c.start()
    for c in copies[:4]:
        c.wait()
    part, sums = absorb(p_ref[...], gp_ref, places_p, wp[...], None)
    acc_ref[...] = part
    for c in copies[4:]:
        c.wait()
    part, sums = absorb(q_ref[...], gq_ref, places_q, wq[...], sums)
    acc_ref[...] += part
    sq_ref[...] = sums


def split(values):
    high = values.astype(BF)
    return high, (values - high.astype(F32)).astype(BF)


def attention(
    place_ref, acc0_ref, sq0_ref, p_ref, q1_ref, q2_ref, q3_ref, gp_ref, gq_ref,
    cos_ref, sin_ref, seg_col_ref, seg_row_ref, dctx_ref, w_ref,
    dp_ref, stat_ref, acc, wp, wq, sems,
):
    places_p = [place_ref[4 + k] for k in range(4)]
    places_q = [[place_ref[k], place_ref[4 + k]] for k in range(1, 4)]
    copies_p, copies_q = [], []
    for i, t in enumerate(places_p):
        copies_p.append(
            pltpu.make_async_copy(w_ref.at[t, pl.ds(0, PW)], wp.at[pl.ds(i * PW, PW)], sems.at[i])
        )
    for g, pair in enumerate(places_q):
        for i, t in enumerate(pair):
            copies_q.append(
                pltpu.make_async_copy(
                    w_ref.at[t, pl.ds(PW, QW)],
                    wq.at[g, pl.ds(i * QW, QW)],
                    sems.at[4 + 2 * g + i],
                )
            )
    for c in copies_p + copies_q:
        c.start()
    sums = sq0_ref[...]
    for c in copies_p:
        c.wait()
    part, sums = absorb(p_ref[...], gp_ref, places_p, wp[...], sums)
    acc[...] = acc0_ref[...] + part
    for g, x_ref in enumerate((q1_ref, q2_ref, q3_ref)):
        copies_q[2 * g].wait()
        copies_q[2 * g + 1].wait()
        part, sums = absorb(x_ref[...], gq_ref, places_q[g], wq[g], sums)
        acc[...] += part
    mean_square = jnp.sum(sums, axis=1, keepdims=True) * (1.0 / D) + 1e-05
    inverse = lax.rsqrt(mean_square)
    cosines, sines = cos_ref[...], sin_ref[...]
    queries_at = lax.broadcasted_iota(jnp.int32, (TOK, TOK), 0)
    keys_at = lax.broadcasted_iota(jnp.int32, (TOK, TOK), 1)
    allowed = (seg_col_ref[...] == seg_row_ref[...]) & (keys_at <= queries_at)
    scale = HD ** (-0.5)
    row_dot = jnp.zeros((TOK, HD), F32)
    for h in range(HEADS):
        at = [slice(n * HEADS * HD + h * HD, n * HEADS * HD + (h + 1) * HD) for n in range(3)]
        raw = [acc[:, s] * inverse for s in at]
        q, k, v = (r.astype(BF) for r in raw)
        qf, kf = q.astype(F32), k.astype(F32)
        qr = qf * cosines + pltpu.roll(qf, HD // 2, 1) * sines
        kr = kf * cosines + pltpu.roll(kf, HD // 2, 1) * sines
        qh, ql = split(qr)
        kh, kl = split(kr)
        scores = (dot(qh, kh, NT) + (dot(qh, kl, NT) + dot(ql, kh, NT))) * scale
        scores = jnp.where(allowed, scores, -1e30)
        weights = jnp.exp(scores - jnp.max(scores, axis=1, keepdims=True))
        weights = weights / jnp.sum(weights, axis=1, keepdims=True)
        cotangent = dctx_ref[:, h * HD : (h + 1) * HD]
        d_weights = dot(cotangent, v, NT)
        d_scores = weights * (
            d_weights - jnp.sum(weights * d_weights, axis=1, keepdims=True)
        )
        d_scores = (d_scores * scale).astype(BF)
        dv = dot(weights.astype(BF), cotangent, TN)
        dqr = dot(d_scores, kh, NN)
        dkr = dot(d_scores, qh, TN)
        dq = dqr * cosines + pltpu.roll(dqr * sines, HD // 2, 1)
        dk = dkr * cosines + pltpu.roll(dkr * sines, HD // 2, 1)
        for s, r, g in zip(at, raw, (dq, dk, dv)):
            row_dot += r * g
            dp_ref[:, s] = (g * inverse).astype(BF)
    total = jnp.sum(row_dot, axis=1, keepdims=True) * (1.0 / D)
    lane = lax.broadcasted_iota(jnp.int32, (TOK, HD), 1)
    stat_ref[...] = jnp.where(lane == 0, total, inverse * inverse)


def feature_gradient(place_ref, dp_ref, w_ref, *rest):
    outs, (ws, sems, qs, ps, out_sems) = rest[:6], rest[6:]
    order = [(k, dy) for k in (2, 1, 3, 0) for dy in (1, 0)]
    copies = []
    for n, (k, dy) in enumerate(order):
        copies.append(
            pltpu.make_async_copy(w_ref.at[place_ref[dy * 4 + k]], ws.at[n], sems.at[n])
        )
    for c in copies:
        c.start()
    left = []
    dp = dp_ref[...]
    for n, (k, dy) in enumerate(order):
        copies[n].wait()
        out = dot(dp, ws[n], NT).astype(BF)
        ps[dy, :, k * PW : (k + 1) * PW] = out[:, :PW]
        qs[k, :, dy * QW : (dy + 1) * QW] = out[:, PW:]
        if dy == 0:
            c = pltpu.make_async_copy(qs.at[k], outs[k], out_sems.at[k])
            c.start()
            left.append(c)
    for dy in (1, 0):
        c = pltpu.make_async_copy(ps.at[dy], outs[4 + dy], out_sems.at[4 + dy])
        c.start()
        left.append(c)
    for c in left:
        c.wait()


def weight_gradient(x_ref, d0, d1, d2, d3, out_ref, rhs, sems):
    @pl.when(pl.program_id(0) == 0)
    def _():
        copies = [
            pltpu.make_async_copy(d, rhs.at[pl.ds(i * TOK, TOK)], sems.at[i])
            for i, d in enumerate((d0, d1, d2, d3))
        ]
        for c in copies:
            c.start()
        for c in copies:
            c.wait()

    out_ref[...] = dot(x_ref[...], rhs[...], NN).astype(BF)


VM = pl.BlockSpec(memory_space=pltpu.VMEM)
SM = pl.BlockSpec(memory_space=pltpu.SMEM)
ANY = pl.BlockSpec(memory_space=pl.ANY)
PARAMS = pltpu.CompilerParams(vmem_limit_bytes=VMEM_LIMIT)


def shift(values, axis, by, size):
    return lax.ppermute(values, axis, [(i, (i + by) % size) for i in range(size)])


def swap(values, axis, bit, size):
    return lax.ppermute(values, axis, [(i, i ^ bit) for i in range(size)])


def body(x_own, gain, w_qkv, segments, d_context):
    yh, core = lax.axis_index("yh"), lax.axis_index("core")
    yl, x_at = lax.axis_index("yl"), lax.axis_index("x")
    ks = jnp.arange(4, dtype=jnp.int32)
    rows = [yl, 1 - yl]
    sources = jnp.concatenate([r * 4 + (x_at - ks) % 4 for r in rows]).astype(jnp.int32)
    targets = jnp.concatenate([r * 4 + (x_at + ks) % 4 for r in rows]).astype(jnp.int32)
    gain_own = lax.dynamic_slice_in_dim(gain, (yl * 4 + x_at) * SHARE, SHARE, 0)

    xp, xq = x_own[:, :PW], x_own[:, PW:]
    got_p = [shift(xp, "x", k, 4) for k in (1, 2, 3)]
    got_q = swap(xq, "yl", 1, 2)
    p_here = jnp.concatenate([xp] + got_p, axis=1)
    q_here = jnp.concatenate([xq, got_q], axis=1)
    p_there = swap(p_here, "yl", 1, 2)
    q_there = [shift(q_here, "x", k, 4) for k in (1, 2, 3)]

    scaled = (x_own.astype(F32) * gain_own).astype(BF).T.reshape(2, 2, 160, TOK)
    to_core = lax.dynamic_index_in_dim(scaled, 1 - core, 1, False)
    mine = lax.dynamic_index_in_dim(scaled, core, 1, False)
    pair = jnp.stack([mine, swap(to_core, "core", 1, 2)], axis=2)
    kept = lax.dynamic_index_in_dim(pair, yh, 0, False)
    got = swap(lax.dynamic_index_in_dim(pair, 1 - yh, 0, False), "yh", 1, 2)
    quarter = jnp.concatenate([kept, got], axis=1).reshape(160, 4 * TOK)
    group_x = lax.all_gather(quarter, ("yl", "x"), axis=0, tiled=True)

    weight = w_qkv.reshape(8, SHARE, COLS)
    gains = gain.reshape(8, 1, SHARE)
    gain_p, gain_q = gains[:, :, :PW], gains[:, :, PW:]
    acc, squares = pl.pallas_call(
        project_first,
        out_shape=(
            jax.ShapeDtypeStruct((TOK, COLS), F32),
            jax.ShapeDtypeStruct((TOK, 128), F32),
        ),
        in_specs=[SM, VM, VM, VM, VM, ANY],
        out_specs=(VM, VM),
        scratch_shapes=[
            pltpu.VMEM((4 * PW, COLS), BF),
            pltpu.VMEM((2 * QW, COLS), BF),
            pltpu.SemaphoreType.DMA((6,)),
        ],
        compiler_params=PARAMS,
        cost_estimate=cost(2 * TOK * 1792 * COLS, 8_000_000),
        name="project_first",
    )(sources, p_here, q_here, gain_p, gain_q, weight)

    half = HD // 2
    angles = jnp.arange(TOK, dtype=F32)[:, None] * (
        10000.0 ** (-(2.0 * jnp.arange(half, dtype=F32)) / HD)
    )
    cosines, sines = jnp.cos(angles), jnp.sin(angles)
    cosines = jnp.concatenate([cosines, cosines], axis=1)
    sines = jnp.concatenate([-sines, sines], axis=1)
    d_packed, stats = pl.pallas_call(
        attention,
        out_shape=(
            jax.ShapeDtypeStruct((TOK, COLS), BF),
            jax.ShapeDtypeStruct((TOK, HD), F32),
        ),
        in_specs=[SM] + [VM] * 13 + [ANY],
        out_specs=(VM, VM),
        scratch_shapes=[
            pltpu.VMEM((TOK, COLS), F32),
            pltpu.VMEM((4 * PW, COLS), BF),
            pltpu.VMEM((3, 2 * QW, COLS), BF),
            pltpu.SemaphoreType.DMA((10,)),
        ],
        compiler_params=PARAMS,
        cost_estimate=cost(2 * TOK * 3328 * COLS + 4_000_000_000, 14_000_000),
        name="attention",
    )(
        sources, acc, squares, p_there, *q_there, gain_p, gain_q, cosines, sines,
        segments[:, None], segments[None, :], d_context, weight,
    )

    from_yh = swap(d_packed, "yh", 1, 2)
    from_core = swap(d_packed, "core", 1, 2)
    from_both = swap(from_yh, "core", 1, 2)

    wide, narrow = 2 * QW, 4 * PW
    pieces = pl.pallas_call(
        feature_gradient,
        out_shape=tuple(
            [jax.ShapeDtypeStruct((TOK, wide), BF)] * 4
            + [jax.ShapeDtypeStruct((TOK, narrow), BF)] * 2
        ),
        in_specs=[SM, VM, ANY],
        out_specs=(ANY,) * 6,
        scratch_shapes=[
            pltpu.VMEM((8, SHARE, COLS), BF),
            pltpu.SemaphoreType.DMA((8,)),
            pltpu.VMEM((4, TOK, wide), BF),
            pltpu.VMEM((2, TOK, narrow), BF),
            pltpu.SemaphoreType.DMA((6,)),
        ],
        compiler_params=PARAMS,
        cost_estimate=cost(2 * TOK * D * COLS, 16_000_000),
        name="feature_gradient",
    )(targets, d_packed, weight)
    along_x = [shift(pieces[k], "x", k, 4) for k in (1, 2, 3)]
    along_y = swap(pieces[5], "yl", 1, 2)
    row_dots = lax.all_gather(stats[:, 0], ("yl", "x"), axis=0)
    sum_q = sum((a.astype(F32) for a in along_x), pieces[0].astype(F32))
    sum_p = pieces[4].astype(F32) + along_y.astype(F32)
    sent_q = swap(sum_q[:, QW:].astype(BF), "yl", 1, 2)
    sent_p = [
        shift(sum_p[:, k * PW : (k + 1) * PW].astype(BF), "x", k, 4) for k in (1, 2, 3)
    ]
    own_q = sum_q[:, :QW] + sent_q.astype(F32)
    own_p = sum((a.astype(F32) for a in sent_p), sum_p[:, :PW])
    d_normed = jnp.concatenate([own_p, own_q], axis=1)
    features = x_own.astype(F32)
    row_dot = jnp.sum(row_dots, axis=0) * stats[:, 1]
    input_gradient = (d_normed * gain_own - features * row_dot[:, None]).astype(BF)
    gain_gradient = jnp.sum(d_normed * features, axis=0).reshape(5, 128)
    for axis, bit, size in (
        ("core", 1, 2), ("yh", 1, 2), ("z", 1, 8), ("z", 2, 8), ("z", 4, 8),
    ):
        gain_gradient = gain_gradient + swap(gain_gradient, axis, bit, size)

    partial_weight = pl.pallas_call(
        weight_gradient,
        grid=(4,),
        out_shape=jax.ShapeDtypeStruct((1280, COLS), BF),
        in_specs=[pl.BlockSpec((320, 4 * TOK), lambda i: (i, 0))] + [ANY] * 4,
        out_specs=pl.BlockSpec((320, COLS), lambda i: (i, 0)),
        scratch_shapes=[pltpu.VMEM((4 * TOK, COLS), BF), pltpu.SemaphoreType.DMA((4,))],
        compiler_params=PARAMS,
        cost_estimate=cost(2 * 1280 * 1280 * COLS, 10_000_000),
        name="weight_gradient",
    )(group_x, d_packed, from_core, from_yh, from_both)
    d_weight = lax.psum_scatter(partial_weight, "z", scatter_dimension=0, tiled=True)
    return (
        input_gradient,
        gain_gradient.reshape(SHARE),
        d_weight.reshape(160, 3, HEADS * HD),
    )


def solution(mesh):
    fine = Mesh(mesh.devices.reshape(8, 2, 2, 2, 4), ("z", "yh", "core", "yl", "x"))
    dp, tensor = ("z", "yh", "core"), ("yl", "x")
    in_specs = (P(dp, tensor), P(), P(None, None, tensor), P(dp), P(dp, tensor))
    out_specs = (P(dp, tensor), P(tensor), P(dp, None, tensor))
    return jax.shard_map(
        body, mesh=fine, in_specs=in_specs, out_specs=out_specs, check_vma=False
    )
```

```python
import jax
import jax.numpy as jnp
from jax import lax
from jax.experimental import pallas as pl
from jax.experimental.pallas import tpu as pltpu
from jax.sharding import Mesh, PartitionSpec as P

HD = 128
HEADS = 3
TOK = 320
D = 5120
COLS = 1152
SHARE = 640
PW = 256
QW = 384
BF = jnp.bfloat16
F32 = jnp.float32
VMEM_LIMIT = 44 * 1024 * 1024


def dot(a, b, dims):
    return lax.dot_general(a, b, (dims, ((), ())), preferred_element_type=F32)


NN = ((1,), (0,))
NT = ((1,), (1,))
TN = ((0,), (0,))


def cost(flops, nbytes):
    return pl.CostEstimate(flops=flops, bytes_accessed=nbytes, transcendentals=0)


def square_sum(values):
    width = values.shape[1]
    squares = values * values
    total = squares[:, :128]
    for start in range(128, width, 128):
        total = total + squares[:, start : start + 128]
    return total


def absorb(x, gain_ref, places, w_slot, sums):
    width = x.shape[1] // len(places)
    values = x.astype(F32)
    gains = jnp.concatenate([gain_ref[t] for t in places], axis=1)
    sums = square_sum(values) if sums is None else sums + square_sum(values)
    return dot((values * gains).astype(BF), w_slot, NN), sums


def fetch(w_ref, place, first, count, slot, start, sems):
    return [
        pltpu.make_async_copy(
            w_ref.at[n, pl.ds(place * SHARE + first, count)],
            slot.at[pl.ds(start, count), pl.ds(n * HEADS * HD, HEADS * HD)],
            sems.at[n],
        )
        for n in range(3)
    ]


def project_first(place_ref, p_ref, q_ref, gp_ref, gq_ref, w_ref, acc_ref, sq_ref, wp, wq, sems):
    places_p = [place_ref[k] for k in range(4)]
    places_q = [place_ref[0], place_ref[4]]
    copies = []
    for i, t in enumerate(places_p):
        copies += fetch(w_ref, t, 0, PW, wp, i * PW, sems.at[i])
    for i, t in enumerate(places_q):
        copies += fetch(w_ref, t, PW, QW, wq, i * QW, sems.at[4 + i])
    for c in copies:
        c.start()
    for c in copies[:12]:
        c.wait()
    part, sums = absorb(p_ref[...], gp_ref, places_p, wp[...], None)
    acc_ref[...] = part
    for c in copies[12:]:
        c.wait()
    part, sums = absorb(q_ref[...], gq_ref, places_q, wq[...], sums)
    acc_ref[...] += part
    sq_ref[...] = sums


def split(values):
    high = values.astype(BF)
    return high, (values - high.astype(F32)).astype(BF)


def attention(
    place_ref, acc0_ref, sq0_ref, p_ref, q1_ref, q2_ref, q3_ref, gp_ref, gq_ref,
    cos_ref, sin_ref, seg_col_ref, seg_row_ref, dctx_ref, w_ref,
    dp_ref, stat_ref, acc, wp, wq, sems,
):
    places_p = [place_ref[4 + k] for k in range(4)]
    places_q = [[place_ref[k], place_ref[4 + k]] for k in range(1, 4)]
    copies_p, copies_q = [], []
    for i, t in enumerate(places_p):
        copies_p += fetch(w_ref, t, 0, PW, wp, i * PW, sems.at[i])
    for g, pair in enumerate(places_q):
        for i, t in enumerate(pair):
            copies_q += fetch(w_ref, t, PW, QW, wq.at[g], i * QW, sems.at[4 + 2 * g + i])
    for c in copies_p + copies_q:
        c.start()
    sums = sq0_ref[...]
    for c in copies_p:
        c.wait()
    part, sums = absorb(p_ref[...], gp_ref, places_p, wp[...], sums)
    acc[...] = acc0_ref[...] + part
    for g, x_ref in enumerate((q1_ref, q2_ref, q3_ref)):
        for c in copies_q[6 * g : 6 * g + 6]:
            c.wait()
        part, sums = absorb(x_ref[...], gq_ref, places_q[g], wq[g], sums)
        acc[...] += part
    mean_square = jnp.sum(sums, axis=1, keepdims=True) * (1.0 / D) + 1e-05
    inverse = lax.rsqrt(mean_square)
    cosines, sines = cos_ref[...], sin_ref[...]
    queries_at = lax.broadcasted_iota(jnp.int32, (TOK, TOK), 0)
    keys_at = lax.broadcasted_iota(jnp.int32, (TOK, TOK), 1)
    allowed = (seg_col_ref[...] == seg_row_ref[...]) & (keys_at <= queries_at)
    scale = HD ** (-0.5)
    row_dot = jnp.zeros((TOK, HD), F32)
    for h in range(HEADS):
        at = [slice(n * HEADS * HD + h * HD, n * HEADS * HD + (h + 1) * HD) for n in range(3)]
        raw = [acc[:, s] * inverse for s in at]
        q, k, v = (r.astype(BF) for r in raw)
        qf, kf = q.astype(F32), k.astype(F32)
        qr = qf * cosines + pltpu.roll(qf, HD // 2, 1) * sines
        kr = kf * cosines + pltpu.roll(kf, HD // 2, 1) * sines
        qh, ql = split(qr)
        kh, kl = split(kr)
        scores = (dot(qh, kh, NT) + (dot(qh, kl, NT) + dot(ql, kh, NT))) * scale
        scores = jnp.where(allowed, scores, -1e30)
        weights = jnp.exp(scores - jnp.max(scores, axis=1, keepdims=True))
        weights = weights / jnp.sum(weights, axis=1, keepdims=True)
        cotangent = dctx_ref[:, h * HD : (h + 1) * HD]
        d_weights = dot(cotangent, v, NT)
        d_scores = weights * (
            d_weights - jnp.sum(weights * d_weights, axis=1, keepdims=True)
        )
        d_scores = (d_scores * scale).astype(BF)
        dv = dot(weights.astype(BF), cotangent, TN)
        dqr = dot(d_scores, kh, NN)
        dkr = dot(d_scores, qh, TN)
        dq = dqr * cosines + pltpu.roll(dqr * sines, HD // 2, 1)
        dk = dkr * cosines + pltpu.roll(dkr * sines, HD // 2, 1)
        for s, r, g in zip(at, raw, (dq, dk, dv)):
            row_dot += r * g
            dp_ref[:, s] = (g * inverse).astype(BF)
    total = jnp.sum(row_dot, axis=1, keepdims=True) * (1.0 / D)
    lane = lax.broadcasted_iota(jnp.int32, (TOK, HD), 1)
    stat_ref[...] = jnp.where(lane == 0, total, inverse * inverse)


def feature_gradient(place_ref, dp_ref, w_ref, *rest):
    outs, (ws, sems, qs, ps, out_sems) = rest[:6], rest[6:]
    order = [(k, dy) for k in (2, 1, 3, 0) for dy in (1, 0)]
    copies = []
    for n, (k, dy) in enumerate(order):
        copies.append(fetch(w_ref, place_ref[dy * 4 + k], 0, SHARE, ws.at[n], 0, sems.at[n]))
    for group in copies:
        for c in group:
            c.start()
    left = []
    dp = dp_ref[...]
    for n, (k, dy) in enumerate(order):
        for c in copies[n]:
            c.wait()
        out = dot(dp, ws[n], NT).astype(BF)
        ps[dy, :, k * PW : (k + 1) * PW] = out[:, :PW]
        qs[k, :, dy * QW : (dy + 1) * QW] = out[:, PW:]
        if dy == 0:
            c = pltpu.make_async_copy(qs.at[k], outs[k], out_sems.at[k])
            c.start()
            left.append(c)
    for dy in (1, 0):
        c = pltpu.make_async_copy(ps.at[dy], outs[4 + dy], out_sems.at[4 + dy])
        c.start()
        left.append(c)
    for c in left:
        c.wait()


def weight_gradient(x_ref, d0, d1, d2, d3, out_ref, rhs, sems):
    @pl.when(pl.program_id(0) == 0)
    def _():
        copies = [
            pltpu.make_async_copy(d, rhs.at[pl.ds(i * TOK, TOK)], sems.at[i])
            for i, d in enumerate((d0, d1, d2, d3))
        ]
        for c in copies:
            c.start()
        for c in copies:
            c.wait()

    out_ref[...] = dot(x_ref[...], rhs[...], NN).astype(BF)


VM = pl.BlockSpec(memory_space=pltpu.VMEM)
SM = pl.BlockSpec(memory_space=pltpu.SMEM)
ANY = pl.BlockSpec(memory_space=pl.ANY)
PARAMS = pltpu.CompilerParams(vmem_limit_bytes=VMEM_LIMIT)


def shift(values, axis, by, size):
    return lax.ppermute(values, axis, [(i, (i + by) % size) for i in range(size)])


def swap(values, axis, bit, size):
    return lax.ppermute(values, axis, [(i, i ^ bit) for i in range(size)])


def body(x_own, gain, w_qkv, segments, d_context):
    yh, core = lax.axis_index("yh"), lax.axis_index("core")
    yl, x_at = lax.axis_index("yl"), lax.axis_index("x")
    ks = jnp.arange(4, dtype=jnp.int32)
    rows = [yl, 1 - yl]
    sources = jnp.concatenate([r * 4 + (x_at - ks) % 4 for r in rows]).astype(jnp.int32)
    targets = jnp.concatenate([r * 4 + (x_at + ks) % 4 for r in rows]).astype(jnp.int32)
    gain_own = lax.dynamic_slice_in_dim(gain, (yl * 4 + x_at) * SHARE, SHARE, 0)

    xp, xq = x_own[:, :PW], x_own[:, PW:]
    got_p = [shift(xp, "x", k, 4) for k in (1, 2, 3)]
    got_q = swap(xq, "yl", 1, 2)
    scaled = (x_own.astype(F32) * gain_own).astype(BF).T.reshape(2, 2, 160, TOK)
    to_core = lax.dynamic_index_in_dim(scaled, 1 - core, 1, False)
    mine = lax.dynamic_index_in_dim(scaled, core, 1, False)
    pair = jnp.stack([mine, swap(to_core, "core", 1, 2)], axis=2)
    kept = lax.dynamic_index_in_dim(pair, yh, 0, False)
    got = swap(lax.dynamic_index_in_dim(pair, 1 - yh, 0, False), "yh", 1, 2)
    quarter = jnp.concatenate([kept, got], axis=1).reshape(160, 4 * TOK)
    quarter, got_p, got_q = lax.optimization_barrier((quarter, got_p, got_q))
    group_x = lax.all_gather(quarter, ("yl", "x"), axis=0, tiled=True)

    p_here = jnp.concatenate([xp] + got_p, axis=1)
    q_here = jnp.concatenate([xq, got_q], axis=1)
    p_there = swap(p_here, "yl", 1, 2)
    q_there = [shift(q_here, "x", k, 4) for k in (1, 2, 3)]

    weight = w_qkv.transpose(1, 0, 2)
    gains = gain.reshape(8, 1, SHARE)
    gain_p, gain_q = gains[:, :, :PW], gains[:, :, PW:]
    acc, squares = pl.pallas_call(
        project_first,
        out_shape=(
            jax.ShapeDtypeStruct((TOK, COLS), F32),
            jax.ShapeDtypeStruct((TOK, 128), F32),
        ),
        in_specs=[SM, VM, VM, VM, VM, ANY],
        out_specs=(VM, VM),
        scratch_shapes=[
            pltpu.VMEM((4 * PW, COLS), BF),
            pltpu.VMEM((2 * QW, COLS), BF),
            pltpu.SemaphoreType.DMA((6, 3)),
        ],
        compiler_params=PARAMS,
        cost_estimate=cost(2 * TOK * 1792 * COLS, 8_000_000),
        name="project_first",
    )(sources, p_here, q_here, gain_p, gain_q, weight)

    half = HD // 2
    angles = jnp.arange(TOK, dtype=F32)[:, None] * (
        10000.0 ** (-(2.0 * jnp.arange(half, dtype=F32)) / HD)
    )
    cosines, sines = jnp.cos(angles), jnp.sin(angles)
    cosines = jnp.concatenate([cosines, cosines], axis=1)
    sines = jnp.concatenate([-sines, sines], axis=1)
    d_packed, stats = pl.pallas_call(
        attention,
        out_shape=(
            jax.ShapeDtypeStruct((TOK, COLS), BF),
            jax.ShapeDtypeStruct((TOK, HD), F32),
        ),
        in_specs=[SM] + [VM] * 13 + [ANY],
        out_specs=(VM, VM),
        scratch_shapes=[
            pltpu.VMEM((TOK, COLS), F32),
            pltpu.VMEM((4 * PW, COLS), BF),
            pltpu.VMEM((3, 2 * QW, COLS), BF),
            pltpu.SemaphoreType.DMA((10, 3)),
        ],
        compiler_params=PARAMS,
        cost_estimate=cost(2 * TOK * 3328 * COLS + 4_000_000_000, 14_000_000),
        name="attention",
    )(
        sources, acc, squares, p_there, *q_there, gain_p, gain_q, cosines, sines,
        segments[:, None], segments[None, :], d_context, weight,
    )

    from_yh = swap(d_packed, "yh", 1, 2)
    from_core = swap(d_packed, "core", 1, 2)
    wide, narrow = 2 * QW, 4 * PW
    pieces = pl.pallas_call(
        feature_gradient,
        out_shape=tuple(
            [jax.ShapeDtypeStruct((TOK, wide), BF)] * 4
            + [jax.ShapeDtypeStruct((TOK, narrow), BF)] * 2
        ),
        in_specs=[SM, VM, ANY],
        out_specs=(ANY,) * 6,
        scratch_shapes=[
            pltpu.VMEM((8, SHARE, COLS), BF),
            pltpu.SemaphoreType.DMA((8, 3)),
            pltpu.VMEM((4, TOK, wide), BF),
            pltpu.VMEM((2, TOK, narrow), BF),
            pltpu.SemaphoreType.DMA((6,)),
        ],
        compiler_params=PARAMS,
        cost_estimate=cost(2 * TOK * D * COLS, 16_000_000),
        name="feature_gradient",
    )(targets, d_packed, weight)
    along_x = [shift(pieces[k], "x", k, 4) for k in (1, 2, 3)]

    from_yh, from_core, along_x[0], along_x[2] = lax.optimization_barrier(
        (from_yh, from_core, along_x[0], along_x[2])
    )
    from_both = swap(from_yh, "core", 1, 2)
    partial_weight = pl.pallas_call(
        weight_gradient,
        grid=(4,),
        out_shape=jax.ShapeDtypeStruct((1280, COLS), BF),
        in_specs=[pl.BlockSpec((320, 4 * TOK), lambda i: (i, 0))] + [ANY] * 4,
        out_specs=pl.BlockSpec((320, COLS), lambda i: (i, 0)),
        scratch_shapes=[pltpu.VMEM((4 * TOK, COLS), BF), pltpu.SemaphoreType.DMA((4,))],
        compiler_params=PARAMS,
        cost_estimate=cost(2 * 1280 * 1280 * COLS, 10_000_000),
        name="weight_gradient",
    )(group_x, d_packed, from_core, from_yh, from_both)
    d_weight = lax.psum_scatter(partial_weight, "z", scatter_dimension=0, tiled=True)
    along_y = swap(pieces[5], "yl", 1, 2)
    row_dot = stats[:, 0]
    for axis, bit, size in (("x", 1, 4), ("x", 2, 4), ("yl", 1, 2)):
        row_dot = row_dot + swap(row_dot, axis, bit, size)
    sum_q = sum((a.astype(F32) for a in along_x), pieces[0].astype(F32))
    sum_p = pieces[4].astype(F32) + along_y.astype(F32)
    sent_q = swap(sum_q[:, QW:].astype(BF), "yl", 1, 2)
    sent_p = [
        shift(sum_p[:, k * PW : (k + 1) * PW].astype(BF), "x", k, 4) for k in (1, 2, 3)
    ]
    own_q = sum_q[:, :QW] + sent_q.astype(F32)
    own_p = sum((a.astype(F32) for a in sent_p), sum_p[:, :PW])
    d_normed = jnp.concatenate([own_p, own_q], axis=1)
    features = x_own.astype(F32)
    row_dot = row_dot * stats[:, 1]
    input_gradient = (d_normed * gain_own - features * row_dot[:, None]).astype(BF)
    gain_gradient = jnp.sum(d_normed * features, axis=0).reshape(5, 128)
    for axis, bit, size in (
        ("core", 1, 2), ("yh", 1, 2), ("z", 1, 8), ("z", 2, 8), ("z", 4, 8),
    ):
        gain_gradient = gain_gradient + swap(gain_gradient, axis, bit, size)

    return (
        input_gradient,
        gain_gradient.reshape(SHARE),
        d_weight.reshape(160, 3, HEADS * HD),
    )


def solution(mesh):
    fine = Mesh(mesh.devices.reshape(8, 2, 2, 2, 4), ("z", "yh", "core", "yl", "x"))
    dp, tensor = ("z", "yh", "core"), ("yl", "x")
    in_specs = (P(dp, tensor), P(), P(None, None, tensor), P(dp), P(dp, tensor))
    out_specs = (P(dp, tensor), P(tensor), P(dp, None, tensor))
    return jax.shard_map(
        body, mesh=fine, in_specs=in_specs, out_specs=out_specs, check_vma=False
    )
```

```python
import jax
import jax.numpy as jnp
from jax import lax
from jax.experimental import pallas as pl
from jax.experimental.pallas import tpu as pltpu
from jax.sharding import Mesh, PartitionSpec as P

HD = 128
HEADS = 3
TOK = 320
D = 5120
COLS = 1152
SHARE = 640
PW = 256
QW = 384
BF = jnp.bfloat16
F32 = jnp.float32
VMEM_LIMIT = 44 * 1024 * 1024


def dot(a, b, dims):
    return lax.dot_general(a, b, (dims, ((), ())), preferred_element_type=F32)


NN = ((1,), (0,))
NT = ((1,), (1,))
TN = ((0,), (0,))


def square_sum(values):
    width = values.shape[1]
    squares = values * values
    total = squares[:, :128]
    for start in range(128, width, 128):
        total = total + squares[:, start : start + 128]
    return total


def absorb(x, gain_ref, places, w_slot, sums):
    width = x.shape[1] // len(places)
    values = x.astype(F32)
    gains = jnp.concatenate([gain_ref[t] for t in places], axis=1)
    sums = square_sum(values) if sums is None else sums + square_sum(values)
    return dot((values * gains).astype(BF), w_slot, NN), sums


def fetch(w_ref, place, first, count, slot, start, sems):
    return [
        pltpu.make_async_copy(
            w_ref.at[n, pl.ds(place * SHARE + first, count)],
            slot.at[pl.ds(start, count), pl.ds(n * HEADS * HD, HEADS * HD)],
            sems.at[n],
        )
        for n in range(3)
    ]


def project_first(place_ref, p_ref, q_ref, gp_ref, gq_ref, w_ref, acc_ref, sq_ref, wp, wq, sems):
    places_p = [place_ref[k] for k in range(4)]
    places_q = [place_ref[0], place_ref[4]]
    copies = []
    for i, t in enumerate(places_p):
        copies += fetch(w_ref, t, 0, PW, wp, i * PW, sems.at[i])
    for i, t in enumerate(places_q):
        copies += fetch(w_ref, t, PW, QW, wq, i * QW, sems.at[4 + i])
    for c in copies:
        c.start()
    for c in copies[:12]:
        c.wait()
    part, sums = absorb(p_ref[...], gp_ref, places_p, wp[...], None)
    acc_ref[...] = part
    for c in copies[12:]:
        c.wait()
    part, sums = absorb(q_ref[...], gq_ref, places_q, wq[...], sums)
    acc_ref[...] += part
    sq_ref[...] = sums


def split(values):
    high = values.astype(BF)
    return high, (values - high.astype(F32)).astype(BF)


def attention(
    place_ref, acc0_ref, sq0_ref, p_ref, q1_ref, q2_ref, q3_ref, gp_ref, gq_ref,
    cos_ref, sin_ref, seg_col_ref, seg_row_ref, dctx_ref, w_ref,
    dp_ref, stat_ref, acc, wp, wq, sems,
):
    places_p = [place_ref[4 + k] for k in range(4)]
    places_q = [[place_ref[k], place_ref[4 + k]] for k in range(1, 4)]
    copies_p, copies_q = [], []
    for i, t in enumerate(places_p):
        copies_p += fetch(w_ref, t, 0, PW, wp, i * PW, sems.at[i])
    for g, pair in enumerate(places_q):
        for i, t in enumerate(pair):
            copies_q += fetch(w_ref, t, PW, QW, wq.at[g], i * QW, sems.at[4 + 2 * g + i])
    for c in copies_p + copies_q:
        c.start()
    sums = sq0_ref[...]
    for c in copies_p:
        c.wait()
    part, sums = absorb(p_ref[...], gp_ref, places_p, wp[...], sums)
    acc[...] = acc0_ref[...] + part
    for g, x_ref in enumerate((q1_ref, q2_ref, q3_ref)):
        for c in copies_q[6 * g : 6 * g + 6]:
            c.wait()
        part, sums = absorb(x_ref[...], gq_ref, places_q[g], wq[g], sums)
        acc[...] += part
    mean_square = jnp.sum(sums, axis=1, keepdims=True) * (1.0 / D) + 1e-05
    inverse = lax.rsqrt(mean_square)
    cosines, sines = cos_ref[...], sin_ref[...]
    queries_at = lax.broadcasted_iota(jnp.int32, (TOK, TOK), 0)
    keys_at = lax.broadcasted_iota(jnp.int32, (TOK, TOK), 1)
    allowed = (seg_col_ref[...] == seg_row_ref[...]) & (keys_at <= queries_at)
    scale = HD ** (-0.5)
    row_dot = jnp.zeros((TOK, HD), F32)
    for h in range(HEADS):
        at = [slice(n * HEADS * HD + h * HD, n * HEADS * HD + (h + 1) * HD) for n in range(3)]
        raw = [acc[:, s] * inverse for s in at]
        q, k, v = (r.astype(BF) for r in raw)
        qf, kf = q.astype(F32), k.astype(F32)
        qr = qf * cosines + pltpu.roll(qf, HD // 2, 1) * sines
        kr = kf * cosines + pltpu.roll(kf, HD // 2, 1) * sines
        qh, ql = split(qr)
        kh, kl = split(kr)
        scores = (dot(qh, kh, NT) + (dot(qh, kl, NT) + dot(ql, kh, NT))) * scale
        scores = jnp.where(allowed, scores, -1e30)
        weights = jnp.exp(scores - jnp.max(scores, axis=1, keepdims=True))
        weights = weights / jnp.sum(weights, axis=1, keepdims=True)
        cotangent = dctx_ref[:, h * HD : (h + 1) * HD]
        d_weights = dot(cotangent, v, NT)
        d_scores = weights * (
            d_weights - jnp.sum(weights * d_weights, axis=1, keepdims=True)
        )
        d_scores = (d_scores * scale).astype(BF)
        dv = dot(weights.astype(BF), cotangent, TN)
        dqr = dot(d_scores, kh, NN)
        dkr = dot(d_scores, qh, TN)
        dq = dqr * cosines + pltpu.roll(dqr * sines, HD // 2, 1)
        dk = dkr * cosines + pltpu.roll(dkr * sines, HD // 2, 1)
        for s, r, g in zip(at, raw, (dq, dk, dv)):
            row_dot += r * g
            dp_ref[:, s] = (g * inverse).astype(BF)
    total = jnp.sum(row_dot, axis=1, keepdims=True) * (1.0 / D)
    lane = lax.broadcasted_iota(jnp.int32, (TOK, HD), 1)
    stat_ref[...] = jnp.where(lane == 0, total, inverse * inverse)


def pick(place_ref, quarter_ref, xp_refs, xq_refs, gp_ref, gq_ref, mine_ref, theirs_ref):
    wanted = lax.broadcasted_iota(jnp.int32, (320, SHARE), 0)
    wanted = jnp.where(
        wanted < 160, wanted + 160 * quarter_ref[0], wanted - 160 + 160 * quarter_ref[1]
    )
    unit = lax.broadcasted_iota(jnp.int32, (320, SHARE), 1) == wanted
    unit = jnp.where(unit, 1.0, 0.0).astype(BF)
    for dy in range(2):
        for k in range(4):
            t = place_ref[dy * 4 + k]
            xp = xp_refs[dy][:, k * PW : (k + 1) * PW].astype(F32) * gp_ref[t]
            xq = xq_refs[k][:, dy * QW : (dy + 1) * QW].astype(F32) * gq_ref[t]
            rows = dot(unit[:, :PW], xp.astype(BF), NT) + dot(unit[:, PW:], xq.astype(BF), NT)
            rows = rows.astype(BF)
            mine_ref[t, :, :TOK] = rows[:160]
            mine_ref[t, :, TOK:] = jnp.zeros((160, 64), BF)
            theirs_ref[t, :, :TOK] = rows[160:]
            theirs_ref[t, :, TOK:] = jnp.zeros((160, 64), BF)


def feature_gradient(
    place_ref, source_ref, quarter_ref, dp_ref, ph_ref, pt_ref, q0_ref, q1_ref, q2_ref, q3_ref,
    gp_ref, gq_ref, w_ref, *rest,
):
    outs, (gain_ref, mine_ref, theirs_ref), (ws, sems, qs, ps, out_sems) = (
        rest[:6], rest[6:9], rest[9:],
    )
    xp_refs, xq_refs = (ph_ref, pt_ref), (q0_ref, q1_ref, q2_ref, q3_ref)
    order = [(k, dy) for k in (2, 1, 3, 0) for dy in (1, 0)]
    copies = []
    for n, (k, dy) in enumerate(order):
        copies.append(fetch(w_ref, place_ref[dy * 4 + k], 0, SHARE, ws.at[n], 0, sems.at[n]))
    for group in copies:
        for c in group:
            c.start()
    pick(source_ref, quarter_ref, xp_refs, xq_refs, gp_ref, gq_ref, mine_ref, theirs_ref)
    left = []
    dp = dp_ref[...]
    for n, (k, dy) in enumerate(order):
        for c in copies[n]:
            c.wait()
        exact = dot(dp, ws[n], NT)
        back = (4 - k) % 4
        xp = xp_refs[dy][:, back * PW : (back + 1) * PW].astype(F32)
        xq = xq_refs[back][:, dy * QW : (dy + 1) * QW].astype(F32)
        row = pl.ds(place_ref[dy * 4 + k], 1)
        gain_ref[row, :PW] = jnp.sum(exact[:, :PW] * xp, axis=0, keepdims=True)
        gain_ref[row, PW:] = jnp.sum(exact[:, PW:] * xq, axis=0, keepdims=True)
        out = exact.astype(BF)
        ps[dy, :, k * PW : (k + 1) * PW] = out[:, :PW]
        qs[k, :, dy * QW : (dy + 1) * QW] = out[:, PW:]
        if dy == 0:
            c = pltpu.make_async_copy(qs.at[k], outs[k], out_sems.at[k])
            c.start()
            left.append(c)
    for dy in (1, 0):
        c = pltpu.make_async_copy(ps.at[dy], outs[4 + dy], out_sems.at[4 + dy])
        c.start()
        left.append(c)
    for c in left:
        c.wait()


def weight_gradient(
    own_ref, core_ref, x_ref, d0, d1, d2, d3, out_ref, near, far, d_near, d_far, result, sems, x_sems, out_sems
):
    copies = [
        pltpu.make_async_copy(d0, d_near.at[pl.ds(0, TOK)], sems.at[0]),
        pltpu.make_async_copy(d1, d_near.at[pl.ds(384, TOK)], sems.at[1]),
        pltpu.make_async_copy(d2, d_far.at[pl.ds(0, TOK)], sems.at[2]),
        pltpu.make_async_copy(d3, d_far.at[pl.ds(TOK, TOK)], sems.at[3]),
    ]
    x_copies = []
    for i in range(4):
        rows = pl.ds(i * 320, 320)
        x_copies += [
            pltpu.make_async_copy(own_ref.at[rows], near.at[i, :, pl.ds(0, 384)], x_sems.at[i, 0]),
            pltpu.make_async_copy(core_ref.at[rows], near.at[i, :, pl.ds(384, 384)], x_sems.at[i, 1]),
            pltpu.make_async_copy(x_ref.at[rows], far.at[i], x_sems.at[i, 2]),
        ]
    for c in copies[:2] + x_copies[:3] + copies[2:] + x_copies[3:]:
        c.start()
    d_near[TOK:384] = jnp.zeros((64, COLS), BF)
    d_near[384 + TOK :] = jnp.zeros((64, COLS), BF)
    left = []
    for i in range(4):
        for c in x_copies[3 * i : 3 * i + 3] + (copies if i == 0 else []):
            c.wait()
        total = dot(near[i], d_near[...], NN) + dot(far[i], d_far[...], NN)
        result[i] = total.astype(BF)
        left.append(
            pltpu.make_async_copy(result.at[i], out_ref.at[pl.ds(i * 320, 320)], out_sems.at[i])
        )
        left[-1].start()
    for c in left:
        c.wait()


VM = pl.BlockSpec(memory_space=pltpu.VMEM)
SM = pl.BlockSpec(memory_space=pltpu.SMEM)
ANY = pl.BlockSpec(memory_space=pl.ANY)
HBM = pl.BlockSpec(memory_space=pltpu.HBM)
SMALL = pl.CostEstimate(flops=1000, bytes_accessed=1000, transcendentals=0)
PARAMS = pltpu.CompilerParams(vmem_limit_bytes=VMEM_LIMIT)


def shift(values, axis, by, size):
    return lax.ppermute(values, axis, [(i, (i + by) % size) for i in range(size)])


def swap(values, axis, bit, size):
    return lax.ppermute(values, axis, [(i, i ^ bit) for i in range(size)])


def body(x_own, gain, w_qkv, segments, d_context):
    yh, core = lax.axis_index("yh"), lax.axis_index("core")
    yl, x_at = lax.axis_index("yl"), lax.axis_index("x")
    ks = jnp.arange(4, dtype=jnp.int32)
    rows = [yl, 1 - yl]
    sources = jnp.concatenate([r * 4 + (x_at - ks) % 4 for r in rows]).astype(jnp.int32)
    targets = jnp.concatenate([r * 4 + (x_at + ks) % 4 for r in rows]).astype(jnp.int32)
    gain_own = lax.dynamic_slice_in_dim(gain, (yl * 4 + x_at) * SHARE, SHARE, 0)

    xp, xq = x_own[:, :PW], x_own[:, PW:]
    got_p = [shift(xp, "x", k, 4) for k in (1, 2, 3)]
    got_q = swap(xq, "yl", 1, 2)
    scaled = (x_own.astype(F32) * gain_own).astype(BF).T.reshape(2, 2, 160, TOK)
    other = lax.dynamic_index_in_dim(scaled, 1 - yh, 0, False)
    straight = lax.dynamic_index_in_dim(other, core, 0, False)
    across = lax.dynamic_index_in_dim(other, 1 - core, 0, False)
    straight, across, got_p, got_q = lax.optimization_barrier((straight, across, got_p, got_q))
    p_here = jnp.concatenate([xp] + got_p, axis=1)
    q_here = jnp.concatenate([xq, got_q], axis=1)
    p_there = swap(p_here, "yl", 1, 2)
    q_there = [shift(q_here, "x", k, 4) for k in (1, 2, 3)]
    straight = swap(straight, "yh", 1, 2)
    across = lax.ppermute(across, ("yh", "core"), [(i, 3 - i) for i in range(4)])

    weight = w_qkv.transpose(1, 0, 2)
    gains = gain.reshape(8, 1, SHARE)
    gain_p, gain_q = gains[:, :, :PW], gains[:, :, PW:]
    acc, squares = pl.pallas_call(
        project_first,
        out_shape=(
            jax.ShapeDtypeStruct((TOK, COLS), F32),
            jax.ShapeDtypeStruct((TOK, 128), F32),
        ),
        in_specs=[SM, VM, VM, VM, VM, HBM],
        out_specs=(VM, VM),
        scratch_shapes=[
            pltpu.VMEM((4 * PW, COLS), BF),
            pltpu.VMEM((2 * QW, COLS), BF),
            pltpu.SemaphoreType.DMA((6, 3)),
        ],
        compiler_params=PARAMS,
        cost_estimate=SMALL,
        name="project_first",
    )(sources, p_here, q_here, gain_p, gain_q, weight)
    acc, straight, across, p_there, q_there = lax.optimization_barrier(
        (acc, straight, across, p_there, q_there)
    )
    quarter = jnp.concatenate([straight, across], axis=1)
    group_x = lax.all_gather(quarter, ("yl", "x"), axis=0, tiled=True)

    half = HD // 2
    angles = jnp.arange(TOK, dtype=F32)[:, None] * (
        10000.0 ** (-(2.0 * jnp.arange(half, dtype=F32)) / HD)
    )
    cosines, sines = jnp.cos(angles), jnp.sin(angles)
    cosines = jnp.concatenate([cosines, cosines], axis=1)
    sines = jnp.concatenate([-sines, sines], axis=1)
    d_packed, stats = pl.pallas_call(
        attention,
        out_shape=(
            jax.ShapeDtypeStruct((TOK, COLS), BF),
            jax.ShapeDtypeStruct((TOK, HD), F32),
        ),
        in_specs=[SM] + [VM] * 13 + [HBM],
        out_specs=(VM, VM),
        scratch_shapes=[
            pltpu.VMEM((TOK, COLS), F32),
            pltpu.VMEM((4 * PW, COLS), BF),
            pltpu.VMEM((3, 2 * QW, COLS), BF),
            pltpu.SemaphoreType.DMA((10, 3)),
        ],
        compiler_params=PARAMS,
        cost_estimate=SMALL,
        name="attention",
    )(
        sources, acc, squares, p_there, *q_there, gain_p, gain_q, cosines, sines,
        segments[:, None], segments[None, :], d_context, weight,
    )

    from_yh = swap(d_packed, "yh", 1, 2)
    from_core = swap(d_packed, "core", 1, 2)
    quarters = jnp.stack([yh * 2 + core, yh * 2 + 1 - core]).astype(jnp.int32)

    wide, narrow = 2 * QW, 4 * PW
    *pieces, gain_parts, x_mine, x_theirs = pl.pallas_call(
        feature_gradient,
        out_shape=tuple(
            [jax.ShapeDtypeStruct((TOK, wide), BF)] * 4
            + [jax.ShapeDtypeStruct((TOK, narrow), BF)] * 2
            + [jax.ShapeDtypeStruct((8, SHARE), F32)]
            + [jax.ShapeDtypeStruct((8, 160, 384), BF)] * 2
        ),
        in_specs=[SM] * 3 + [VM] * 9 + [HBM],
        out_specs=(ANY,) * 6 + (VM,) * 3,
        scratch_shapes=[
            pltpu.VMEM((8, SHARE, COLS), BF),
            pltpu.SemaphoreType.DMA((8, 3)),
            pltpu.VMEM((4, TOK, wide), BF),
            pltpu.VMEM((2, TOK, narrow), BF),
            pltpu.SemaphoreType.DMA((6,)),
        ],
        compiler_params=PARAMS,
        cost_estimate=SMALL,
        name="feature_gradient",
    )(
        targets, sources, quarters, d_packed, p_here, p_there, q_here, *q_there, gain_p, gain_q, weight,
    )
    from_yh, from_core, group_x, x_theirs, pieces, gain_parts = lax.optimization_barrier(
        (from_yh, from_core, group_x, x_theirs, pieces, gain_parts)
    )
    x_core = swap(x_theirs, "core", 1, 2)
    from_both = swap(from_yh, "core", 1, 2)
    partial_weight = pl.pallas_call(
        weight_gradient,
        out_shape=jax.ShapeDtypeStruct((1280, COLS), BF),
        in_specs=[HBM] * 7,
        out_specs=HBM,
        scratch_shapes=[
            pltpu.VMEM((4, 320, 768), BF),
            pltpu.VMEM((4, 320, 640), BF),
            pltpu.VMEM((768, COLS), BF),
            pltpu.VMEM((640, COLS), BF),
            pltpu.VMEM((4, 320, COLS), BF),
            pltpu.SemaphoreType.DMA((4,)),
            pltpu.SemaphoreType.DMA((4, 3)),
            pltpu.SemaphoreType.DMA((4,)),
        ],
        compiler_params=PARAMS,
        cost_estimate=SMALL,
        name="weight_gradient",
    )(
        x_mine.reshape(1280, 384), x_core.reshape(1280, 384), group_x,
        d_packed, from_core, from_yh, from_both,
    )
    pieces, gain_parts, partial_weight = lax.optimization_barrier(
        (pieces, gain_parts, partial_weight)
    )
    d_weight = lax.psum_scatter(partial_weight, "z", scatter_dimension=0, tiled=True)

    along_x = [shift(pieces[k], "x", k, 4) for k in (1, 2, 3)]
    along_y = swap(pieces[5], "yl", 1, 2)

    def over_tensor(small):
        for axis, bit, size in (("x", 1, 4), ("x", 2, 4), ("yl", 1, 2)):
            small = small + swap(small, axis, bit, size)
        share = lax.dynamic_slice_in_dim(small, TOK + (yl * 4 + x_at) * SHARE, SHARE, 0)
        for axis in ("core", "yh"):
            share = share + swap(share, axis, 1, 2)
        return small[:TOK], share

    def over_z(share):
        for bit in (1, 2, 4):
            share = share + swap(share, "z", bit, 8)
        return share

    small = jnp.concatenate([stats[:, 0], gain_parts.reshape(D)])
    row_dot, gain_gradient = lax.cond(
        segments[0] >= 0, over_tensor, lambda v: (v[:TOK], v[TOK : TOK + SHARE]), small
    )
    along_x, along_y, row_dot, gain_gradient = lax.optimization_barrier(
        (along_x, along_y, row_dot, gain_gradient)
    )
    sum_q = sum((a.astype(F32) for a in along_x), pieces[0].astype(F32))
    sum_p = pieces[4].astype(F32) + along_y.astype(F32)
    sent_q = swap(sum_q[:, QW:].astype(BF), "yl", 1, 2)
    sent_p = [
        shift(sum_p[:, k * PW : (k + 1) * PW].astype(BF), "x", k, 4) for k in (1, 2, 3)
    ]
    gain_gradient = lax.cond(segments[0] >= 0, over_z, lambda v: v, gain_gradient)
    sent_q, sent_p, gain_gradient = lax.optimization_barrier((sent_q, sent_p, gain_gradient))
    own_q = sum_q[:, :QW] + sent_q.astype(F32)
    own_p = sum((a.astype(F32) for a in sent_p), sum_p[:, :PW])
    d_normed = jnp.concatenate([own_p, own_q], axis=1)
    features = x_own.astype(F32)
    row_dot = row_dot * stats[:, 1]
    input_gradient = (d_normed * gain_own - features * row_dot[:, None]).astype(BF)
    return (
        input_gradient,
        gain_gradient,
        d_weight.reshape(160, 3, HEADS * HD),
    )


def solution(mesh):
    fine = Mesh(mesh.devices.reshape(8, 2, 2, 2, 4), ("z", "yh", "core", "yl", "x"))
    dp, tensor = ("z", "yh", "core"), ("yl", "x")
    in_specs = (P(dp, tensor), P(), P(None, None, tensor), P(dp), P(dp, tensor))
    out_specs = (P(dp, tensor), P(tensor), P(dp, None, tensor))
    return jax.shard_map(
        body, mesh=fine, in_specs=in_specs, out_specs=out_specs, check_vma=False
    )
```

```python
import functools

import jax
import jax.numpy as jnp
from jax import lax
from jax.experimental import pallas as pl
from jax.experimental.pallas import tpu as pltpu
from jax.sharding import Mesh, PartitionSpec as P

HD = 128
HEADS = 3
TOK = 320
D = 5120
COLS = 1152
SHARE = 640
PW = 256
WIDE = 768
QW = 384
BF = jnp.bfloat16
F32 = jnp.float32


def dot(a, b, dims):
    return lax.dot_general(a, b, (dims, ((), ())), preferred_element_type=F32)


NN = ((1,), (0,))
NT = ((1,), (1,))
TN = ((0,), (0,))


def square_sum(values):
    width = values.shape[1]
    squares = values * values
    total = squares[:, :128]
    for start in range(128, width, 128):
        total = total + squares[:, start : start + 128]
    return total


def absorb(x, gain_ref, places, w_slot, sums):
    width = x.shape[1] // len(places)
    values = x.astype(F32)
    gains = jnp.concatenate([gain_ref[t] for t in places], axis=1)
    sums = square_sum(values) if sums is None else sums + square_sum(values)
    return dot((values * gains).astype(BF), w_slot, NN), sums


def fetch(w_ref, place, first, count, slot, start, sems):
    return [
        pltpu.make_async_copy(
            w_ref.at[n, pl.ds(place * SHARE + first, count)],
            slot.at[pl.ds(start, count), pl.ds(n * HEADS * HD, HEADS * HD)],
            sems.at[n],
        )
        for n in range(3)
    ]


def project_first(place_ref, p_ref, q_ref, gp_ref, gq_ref, w_ref, acc_ref, sq_ref, wp, wq, sems):
    places_p = [place_ref[k] for k in range(4)]
    places_q = [place_ref[0], place_ref[4]]
    copies = []
    for i, t in enumerate(places_p):
        copies += fetch(w_ref, t, 0, PW, wp, i * PW, sems.at[i])
    for i, t in enumerate(places_q):
        copies += fetch(w_ref, t, PW, QW, wq, i * QW, sems.at[4 + i])
    for c in copies:
        c.start()
    for c in copies[:12]:
        c.wait()
    part, sums = absorb(p_ref[...], gp_ref, places_p, wp[...], None)
    acc_ref[...] = part
    for c in copies[12:]:
        c.wait()
    part, sums = absorb(q_ref[...], gq_ref, places_q, wq[...], sums)
    acc_ref[...] += part
    sq_ref[...] = sums


def split(values):
    high = values.astype(BF)
    return high, (values - high.astype(F32)).astype(BF)


def thirds(values):
    high, low = split(values)
    rest = values - high.astype(F32) - low.astype(F32)
    return high, low, rest.astype(BF)


def attention(
    place_ref, acc0_ref, sq0_ref, p_ref, q1_ref, q2_ref, q3_ref, gp_ref, gq_ref,
    cos_ref, sin_ref, seg_col_ref, seg_row_ref, dctx_ref, w_ref,
    dp_ref, stat_ref, lane_ref, acc, wp, wq, sems,
):
    places_p = [place_ref[4 + k] for k in range(4)]
    places_q = [[place_ref[k], place_ref[4 + k]] for k in range(1, 4)]
    copies_p, copies_q = [], []
    for i, t in enumerate(places_p):
        copies_p += fetch(w_ref, t, 0, PW, wp, i * PW, sems.at[i])
    for g, pair in enumerate(places_q):
        for i, t in enumerate(pair):
            copies_q += fetch(w_ref, t, PW, QW, wq.at[g], i * QW, sems.at[4 + 2 * g + i])
    for c in copies_p + copies_q:
        c.start()
    sums = sq0_ref[...]
    for c in copies_p:
        c.wait()
    part, sums = absorb(p_ref[...], gp_ref, places_p, wp[...], sums)
    acc[...] = acc0_ref[...] + part
    for g, x_ref in enumerate((q1_ref, q2_ref, q3_ref)):
        for c in copies_q[6 * g : 6 * g + 6]:
            c.wait()
        part, sums = absorb(x_ref[...], gq_ref, places_q[g], wq[g], sums)
        acc[...] += part
    mean_square = jnp.sum(sums, axis=1, keepdims=True) * (1.0 / D) + 1e-05
    inverse = lax.rsqrt(mean_square)
    cosines, sines = cos_ref[...], sin_ref[...]
    queries_at = lax.broadcasted_iota(jnp.int32, (TOK, TOK), 0)
    keys_at = lax.broadcasted_iota(jnp.int32, (TOK, TOK), 1)
    allowed = (seg_col_ref[...] == seg_row_ref[...]) & (keys_at <= queries_at)
    scale = HD ** (-0.5)
    row_dot = jnp.zeros((TOK, HD), F32)
    for h in range(HEADS):
        at = [slice(n * HEADS * HD + h * HD, n * HEADS * HD + (h + 1) * HD) for n in range(3)]
        raw = [acc[:, s] * inverse for s in at]
        q, k, v = (r.astype(BF) for r in raw)
        qf, kf = q.astype(F32), k.astype(F32)
        qr = qf * cosines + pltpu.roll(qf, HD // 2, 1) * sines
        kr = kf * cosines + pltpu.roll(kf, HD // 2, 1) * sines
        qh, ql = split(qr)
        kh, kl = split(kr)
        scores = (dot(qh, kh, NT) + (dot(qh, kl, NT) + dot(ql, kh, NT))) * scale
        scores = jnp.where(allowed, scores, -1e30)
        weights = jnp.exp(scores - jnp.max(scores, axis=1, keepdims=True))
        weights = weights / jnp.sum(weights, axis=1, keepdims=True)
        cotangent = dctx_ref[:, h * HD : (h + 1) * HD]
        d_weights = dot(cotangent, v, NT)
        d_scores = weights * (
            d_weights - jnp.sum(weights * d_weights, axis=1, keepdims=True)
        )
        d_scores = (d_scores * scale).astype(BF)
        dv = dot(weights.astype(BF), cotangent, TN)
        dqr = dot(d_scores, kh, NN)
        dkr = dot(d_scores, qh, TN)
        dq = dqr * cosines + pltpu.roll(dqr * sines, HD // 2, 1)
        dk = dkr * cosines + pltpu.roll(dkr * sines, HD // 2, 1)
        for s, r, g in zip(at, raw, (dq, dk, dv)):
            row_dot += r * g
            dp_ref[:, s] = (g * inverse).astype(BF)
    stat_ref[...] = jnp.broadcast_to(inverse * inverse, (TOK, HD))
    ones = jnp.ones((16, HD), BF)
    lane_ref[...] = sum(dot(ones, part, NT) for part in thirds(row_dot * (1.0 / D)))[:8]


def pick(place_ref, quarter_ref, xp_refs, xq_refs, gp_ref, gq_ref, mine_ref, theirs_ref):
    wanted = lax.broadcasted_iota(jnp.int32, (320, SHARE), 0)
    wanted = jnp.where(
        wanted < 160, wanted + 160 * quarter_ref[0], wanted - 160 + 160 * quarter_ref[1]
    )
    unit = lax.broadcasted_iota(jnp.int32, (320, SHARE), 1) == wanted
    unit = jnp.where(unit, 1.0, 0.0).astype(BF)
    for dy in range(2):
        for k in range(4):
            t = place_ref[dy * 4 + k]
            xp = xp_refs[dy][:, k * PW : (k + 1) * PW].astype(F32) * gp_ref[t]
            xq = xq_refs[k][:, dy * QW : (dy + 1) * QW].astype(F32) * gq_ref[t]
            rows = dot(unit[:, :PW], xp.astype(BF), NT) + dot(unit[:, PW:], xq.astype(BF), NT)
            rows = rows.astype(BF)
            mine_ref[t, :, :TOK] = rows[:160]
            mine_ref[t, :, TOK:] = jnp.zeros((160, 64), BF)
            theirs_ref[t, :, :TOK] = rows[160:]
            theirs_ref[t, :, TOK:] = jnp.zeros((160, 64), BF)


def feature_gradient(
    place_ref, source_ref, quarter_ref, dp_ref, lane_ref, ph_ref, pt_ref, q0_ref, q1_ref, q2_ref, q3_ref,
    gp_ref, gq_ref, w_ref, qo0, qo1, qo2, qo3, po0, po1, gain_ref, mine_ref, theirs_ref, ws, sems,
):
    q_outs, p_outs = (qo0, qo1, qo2, qo3), (po0, po1)
    xp_refs, xq_refs = (ph_ref, pt_ref), (q0_ref, q1_ref, q2_ref, q3_ref)
    order = [(k, dy) for k in range(4) for dy in (0, 1)]
    copies = []
    for n, (k, dy) in enumerate(order):
        copies.append(fetch(w_ref, place_ref[dy * 4 + k], 0, SHARE, ws.at[n], 0, sems.at[n]))
    for group in copies:
        for c in group:
            c.start()
    pick(source_ref, quarter_ref, xp_refs, xq_refs, gp_ref, gq_ref, mine_ref, theirs_ref)
    gain_ref[:, 2:, :] = jnp.zeros((4, 6, SHARE), F32)
    for column in range(4):
        gain_ref[column, 2:3, :TOK] = lane_ref[0:1]
    dp = dp_ref[...]
    for n, (k, dy) in enumerate(order):
        for c in copies[n]:
            c.wait()
        exact = dot(dp, ws[n], NT)
        back = (4 - k) % 4
        xp = xp_refs[dy][:, back * PW : (back + 1) * PW].astype(F32)
        xq = xq_refs[back][:, dy * QW : (dy + 1) * QW].astype(F32)
        column = place_ref[dy * 4 + k] & 3
        row = pl.ds(place_ref[dy * 4 + k] >> 2, 1)
        gain_ref[column, row, :PW] = jnp.sum(exact[:, :PW] * xp, axis=0, keepdims=True)
        gain_ref[column, row, PW:] = jnp.sum(exact[:, PW:] * xq, axis=0, keepdims=True)
        p_outs[dy][:, k * PW : (k + 1) * PW] = exact[:, :PW].astype(BF)
        q_outs[k][:, dy * QW : (dy + 1) * QW] = exact[:, PW:].astype(BF)


def add_up(q0, q1, q2, q3, p0, p1, own_q, sent_q, own_p, sent1, sent2, sent3):
    total = (q0[...].astype(F32) + q1[...].astype(F32)) + (q2[...].astype(F32) + q3[...].astype(F32))
    own_q[...] = total[:, :QW]
    sent_q[...] = total[:, QW:].astype(BF)
    total = p0[...].astype(F32) + p1[...].astype(F32)
    own_p[...] = total[:, :PW]
    for k, ref in enumerate((sent1, sent2, sent3)):
        ref[...] = total[:, (k + 1) * PW : (k + 2) * PW].astype(BF)


def weight_gradient(
    distances, owner_ref, slot_ref, own_ref, core_ref, f0, f1, f2, f3, d0, d1, d2, d3, out_ref,
    near, far, d_near, d_far, sems, near_sems, far_sems,
):
    d_copies = [
        pltpu.make_async_copy(d0, d_near.at[pl.ds(0, TOK)], sems.at[0]),
        pltpu.make_async_copy(d1, d_near.at[pl.ds(384, TOK)], sems.at[1]),
        pltpu.make_async_copy(d2, d_far.at[pl.ds(0, TOK)], sems.at[2]),
        pltpu.make_async_copy(d3, d_far.at[pl.ds(TOK, TOK)], sems.at[3]),
    ]
    copies = []
    for i, r in enumerate(distances):
        rows = pl.ds(i * 160, 160)
        t = owner_ref[r]
        copies += [
            pltpu.make_async_copy(own_ref.at[t], near.at[rows, pl.ds(0, 384)], near_sems.at[i, 0]),
            pltpu.make_async_copy(core_ref.at[t], near.at[rows, pl.ds(384, 384)], near_sems.at[i, 1]),
        ]
    for k, f in enumerate((f0, f1, f2, f3)):
        for dy in range(2):
            n = dy * 4 + k
            copies.append(
                pltpu.make_async_copy(f.at[:, pl.ds(dy * 640, 640)], far.at[slot_ref[n]], far_sems.at[n])
            )
    for c in d_copies + copies:
        c.start()
    d_near[TOK:384] = jnp.zeros((64, COLS), BF)
    d_near[384 + TOK :] = jnp.zeros((64, COLS), BF)
    for c in d_copies + copies:
        c.wait()
    at = 0
    while at < len(distances):
        count = min(2, len(distances) - at)
        group = distances[at : at + count]
        x_far = jnp.concatenate([far[r] for r in group], axis=0) if count > 1 else far[group[0]]
        total = dot(near[at * 160 : (at + count) * 160], d_near[...], NN) + dot(x_far, d_far[...], NN)
        for i in range(count):
            out_ref[at + i] = total[i * 160 : (i + 1) * 160].astype(BF)
        at += count


def finish(own_ref, down_ref, up_ref, out_ref):
    total = own_ref[...].astype(F32) + (down_ref[...].astype(F32) + up_ref[...].astype(F32))
    for n in range(3):
        out_ref[n] = total[:, n * HEADS * HD : (n + 1) * HEADS * HD].astype(BF)


VM = pl.BlockSpec(memory_space=pltpu.VMEM)
SM = pl.BlockSpec(memory_space=pltpu.SMEM)
ANY = pl.BlockSpec(memory_space=pl.ANY)
HBM = pl.BlockSpec(memory_space=pltpu.HBM)
SMALL = pl.CostEstimate(flops=1000, bytes_accessed=1000, transcendentals=0)


def limit(mib):
    return pltpu.CompilerParams(vmem_limit_bytes=mib * 1024 * 1024)


def shift(values, axis, by, size):
    return lax.ppermute(values, axis, [(i, (i + by) % size) for i in range(size)])


def swap(values, axis, bit, size):
    return lax.ppermute(values, axis, [(i, i ^ bit) for i in range(size)])


def body(x_own, gain, w_qkv, segments, d_context):
    yh, core = lax.axis_index("yh"), lax.axis_index("core")
    yl, x_at = lax.axis_index("yl"), lax.axis_index("x")
    ks = jnp.arange(4, dtype=jnp.int32)
    rows = [yl, 1 - yl]
    sources = jnp.concatenate([r * 4 + (x_at - ks) % 4 for r in rows]).astype(jnp.int32)
    targets = jnp.concatenate([r * 4 + (x_at + ks) % 4 for r in rows]).astype(jnp.int32)
    gain_own = lax.dynamic_slice_in_dim(gain, (yl * 4 + x_at) * SHARE, SHARE, 0)

    xp, xq = x_own[:, :PW], x_own[:, PW:]
    got_p = [shift(xp, "x", k, 4) for k in (1, 2, 3)]
    got_q = swap(xq, "yl", 1, 2)
    scaled = (x_own.astype(F32) * gain_own).astype(BF).T.reshape(2, 2, 160, TOK)
    other = lax.dynamic_index_in_dim(scaled, 1 - yh, 0, False)
    straight = lax.dynamic_index_in_dim(other, core, 0, False)
    across = lax.dynamic_index_in_dim(other, 1 - core, 0, False)
    straight, across, got_p, got_q = lax.optimization_barrier((straight, across, got_p, got_q))
    p_here = jnp.concatenate([xp] + got_p, axis=1)
    q_here = jnp.concatenate([xq, got_q], axis=1)
    p_there = swap(p_here, "yl", 1, 2)
    q_there = [shift(q_here, "x", k, 4) for k in (1, 2, 3)]
    straight = swap(straight, "yh", 1, 2)
    across = lax.ppermute(across, ("yh", "core"), [(i, 3 - i) for i in range(4)])
    quarter = jnp.concatenate([straight, across], axis=1)

    weight = w_qkv.transpose(1, 0, 2)
    gains = gain.reshape(8, 1, SHARE)
    gain_p, gain_q = gains[:, :, :PW], gains[:, :, PW:]
    acc, squares = pl.pallas_call(
        project_first,
        out_shape=(
            jax.ShapeDtypeStruct((TOK, COLS), F32),
            jax.ShapeDtypeStruct((TOK, 128), F32),
        ),
        in_specs=[SM, VM, VM, VM, VM, HBM],
        out_specs=(VM, VM),
        scratch_shapes=[
            pltpu.VMEM((4 * PW, COLS), BF),
            pltpu.VMEM((2 * QW, COLS), BF),
            pltpu.SemaphoreType.DMA((6, 3)),
        ],
        compiler_params=limit(12),
        cost_estimate=SMALL,
        name="project_first",
    )(sources, p_here, q_here, gain_p, gain_q, weight)

    acc, quarter = lax.optimization_barrier((acc, quarter))
    quarter_there = swap(quarter, "yl", 1, 2)

    half = HD // 2
    angles = jnp.arange(TOK, dtype=F32)[:, None] * (
        10000.0 ** (-(2.0 * jnp.arange(half, dtype=F32)) / HD)
    )
    cosines, sines = jnp.cos(angles), jnp.sin(angles)
    cosines = jnp.concatenate([cosines, cosines], axis=1)
    sines = jnp.concatenate([-sines, sines], axis=1)
    d_packed, stats, row_dots = pl.pallas_call(
        attention,
        out_shape=(
            jax.ShapeDtypeStruct((TOK, COLS), BF),
            jax.ShapeDtypeStruct((TOK, HD), F32),
            jax.ShapeDtypeStruct((8, TOK), F32),
        ),
        in_specs=[SM] + [VM] * 13 + [HBM],
        out_specs=(VM, VM, VM),
        scratch_shapes=[
            pltpu.VMEM((TOK, COLS), F32),
            pltpu.VMEM((4 * PW, COLS), BF),
            pltpu.VMEM((3, 2 * QW, COLS), BF),
            pltpu.SemaphoreType.DMA((10, 3)),
        ],
        compiler_params=limit(22),
        cost_estimate=SMALL,
        name="attention",
    )(
        sources, acc, squares, p_there, *q_there, gain_p, gain_q, cosines, sines,
        segments[:, None], segments[None, :], d_context, weight,
    )

    d_packed, quarter, quarter_there = lax.optimization_barrier((d_packed, quarter, quarter_there))
    far = [jnp.concatenate([quarter, quarter_there], axis=1)]
    from_yh = swap(d_packed, "yh", 1, 2)
    from_core = swap(d_packed, "core", 1, 2)
    far = far + [shift(far[0], "x", k, 4) for k in (1, 2, 3)]
    quarters = jnp.stack([yh * 2 + core, yh * 2 + 1 - core]).astype(jnp.int32)
    *pieces, gains_here, x_mine, x_theirs = pl.pallas_call(
        feature_gradient,
        out_shape=tuple(
            [jax.ShapeDtypeStruct((TOK, WIDE), BF)] * 4
            + [jax.ShapeDtypeStruct((TOK, 4 * PW), BF)] * 2
            + [jax.ShapeDtypeStruct((4, 8, SHARE), F32)]
            + [jax.ShapeDtypeStruct((8, 160, 384), BF)] * 2
        ),
        in_specs=[SM] * 3 + [VM] * 10 + [HBM],
        out_specs=(VM,) * 9,
        scratch_shapes=[
            pltpu.VMEM((8, SHARE, COLS), BF),
            pltpu.SemaphoreType.DMA((8, 3)),
        ],
        compiler_params=limit(30),
        cost_estimate=SMALL,
        name="feature_gradient",
    )(
        targets, sources, quarters, d_packed, row_dots, p_here, p_there, q_here, *q_there, gain_p, gain_q, weight,
    )
    from_yh, from_core, far, x_theirs, gains_here = lax.optimization_barrier(
        (from_yh, from_core, far, x_theirs, gains_here)
    )
    small = [lax.dynamic_index_in_dim(gains_here, x_at ^ bit, 0, False) for bit in range(4)]
    small = small[:1] + [swap(small[bit], "x", bit, 4) for bit in (1, 2, 3)]
    from_both = swap(from_yh, "core", 1, 2)
    x_core = swap(x_theirs, "core", 1, 2)
    from_both, x_core, small, pieces = lax.optimization_barrier((from_both, x_core, small, pieces))
    small = (small[0] + small[1]) + (small[2] + small[3])

    z_at = lax.axis_index("z")
    owners = ((z_at + jnp.arange(8)) % 8).astype(jnp.int32)
    slots = ((sources - z_at) % 8).astype(jnp.int32)
    operands = (owners, slots, x_mine, x_core, *far, d_packed, from_core, from_yh, from_both)

    def rows_for(distances, name):
        return pl.pallas_call(
            functools.partial(weight_gradient, distances),
            out_shape=jax.ShapeDtypeStruct((len(distances), 160, COLS), BF),
            in_specs=[SM, SM] + [ANY] * 10,
            out_specs=VM,
            scratch_shapes=[
                pltpu.VMEM((len(distances) * 160, 768), BF),
                pltpu.VMEM((8, 160, 640), BF),
                pltpu.VMEM((768, COLS), BF),
                pltpu.VMEM((640, COLS), BF),
                pltpu.SemaphoreType.DMA((4,)),
                pltpu.SemaphoreType.DMA((len(distances), 2)),
                pltpu.SemaphoreType.DMA((8,)),
            ],
            compiler_params=limit(18),
            cost_estimate=SMALL,
            name=name,
        )(*operands)

    def plus(a, b):
        return (a.astype(F32) + b.astype(F32)).astype(BF)

    along_x = [shift(pieces[k], "x", k, 4) for k in (1, 2, 3)]
    along_y = swap(pieces[5], "yl", 1, 2)
    down = shift(rows_for((4,), "weight_gradient_far")[0], "z", 1, 8)
    rest = rows_for((3, 5, 2, 6, 1, 7, 0), "weight_gradient_rest")
    heard = [swap(small, "yl", 1, 2), swap(small, "yh", 1, 2)]
    heard.append(lax.ppermute(small, ("yh", "yl"), [(i, 3 - i) for i in range(4)]))
    down, heard, along_x[0], along_x[2], rest = lax.optimization_barrier(
        (down, heard, along_x[0], along_x[2], rest)
    )
    row_dot = small[2, :TOK] + heard[0][2, :TOK]
    shares = [lax.dynamic_index_in_dim(v, yl, 0, False) for v in (small, *heard)]
    share = (shares[0] + shares[1]) + (shares[2] + shares[3])
    down = shift(plus(rest[0], down), "z", 1, 8)
    up = shift(rest[1], "z", -1, 8)
    there = swap(share, "z", 1, 8)
    down, up, there, along_x, along_y = lax.optimization_barrier((down, up, there, along_x, along_y))
    share = share + there
    own_q, sent_q, own_p, *sent_p = pl.pallas_call(
        add_up,
        out_shape=(
            jax.ShapeDtypeStruct((TOK, QW), F32),
            jax.ShapeDtypeStruct((TOK, QW), BF),
            jax.ShapeDtypeStruct((TOK, PW), F32),
            jax.ShapeDtypeStruct((TOK, PW), BF),
            jax.ShapeDtypeStruct((TOK, PW), BF),
            jax.ShapeDtypeStruct((TOK, PW), BF),
        ),
        in_specs=[VM] * 6,
        out_specs=(VM,) * 6,
        compiler_params=limit(16),
        cost_estimate=SMALL,
        name="add_up",
    )(pieces[0], *along_x, pieces[4], along_y)
    down = shift(plus(rest[2], down), "z", 1, 8)
    up = shift(plus(rest[3], up), "z", -1, 8)
    sent_q = swap(sent_q, "yl", 1, 2)
    sent_p = [shift(a, "x", k, 4) for k, a in zip((1, 2, 3), sent_p)]
    there = swap(share, "z", 2, 8)
    down, up, sent_q, sent_p, there = lax.optimization_barrier((down, up, sent_q, sent_p, there))
    share = share + there
    down = shift(plus(rest[4], down), "z", 1, 8)
    up = shift(plus(rest[5], up), "z", -1, 8)
    d_normed = jnp.concatenate(
        [sum((a.astype(F32) for a in sent_p), own_p), own_q + sent_q.astype(F32)], axis=1
    )
    row_dot = row_dot * stats[:, 0]
    input_gradient = (d_normed * gain_own - x_own.astype(F32) * row_dot[:, None]).astype(BF)
    share = share + swap(share, "z", 4, 8)
    gain_gradient = share + swap(share, "core", 1, 2)
    down, up, gain_gradient = lax.optimization_barrier((down, up, gain_gradient))
    d_weight = pl.pallas_call(
        finish,
        out_shape=jax.ShapeDtypeStruct((3, 160, HEADS * HD), BF),
        in_specs=[VM] * 3,
        out_specs=VM,
        compiler_params=limit(12),
        cost_estimate=SMALL,
        name="finish",
    )(rest[6], down, up)
    return input_gradient, gain_gradient, d_weight.transpose(1, 0, 2)


def solution(mesh):
    fine = Mesh(mesh.devices.reshape(8, 2, 2, 2, 4), ("z", "yh", "core", "yl", "x"))
    dp, tensor = ("z", "yh", "core"), ("yl", "x")
    in_specs = (P(dp, tensor), P(), P(None, None, tensor), P(dp), P(dp, tensor))
    out_specs = (P(dp, tensor), P(tensor), P(dp, None, tensor))
    return jax.shard_map(
        body, mesh=fine, in_specs=in_specs, out_specs=out_specs, check_vma=False
    )
```

```python
import functools

import jax
import jax.numpy as jnp
from jax import lax
from jax.experimental import pallas as pl
from jax.experimental.pallas import tpu as pltpu
from jax.sharding import Mesh, PartitionSpec as P

HD = 128
HEADS = 3
TOK = 320
D = 5120
COLS = 1152
SHARE = 640
PW = 256
WIDE = 768
QW = 384
BF = jnp.bfloat16
F32 = jnp.float32


def dot(a, b, dims):
    return lax.dot_general(a, b, (dims, ((), ())), preferred_element_type=F32)


NN = ((1,), (0,))
NT = ((1,), (1,))
TN = ((0,), (0,))


def square_sum(values):
    width = values.shape[1]
    squares = values * values
    total = squares[:, :128]
    for start in range(128, width, 128):
        total = total + squares[:, start : start + 128]
    return total


def absorb(x, gain_ref, places, w_slot, sums):
    width = x.shape[1] // len(places)
    values = x.astype(F32)
    gains = jnp.concatenate([gain_ref[t] for t in places], axis=1)
    sums = square_sum(values) if sums is None else sums + square_sum(values)
    return dot((values * gains).astype(BF), w_slot, NN), sums


def fetch(w_ref, place, first, count, slot, start, sems):
    return [
        pltpu.make_async_copy(
            w_ref.at[n, pl.ds(place * SHARE + first, count)],
            slot.at[pl.ds(start, count), pl.ds(n * HEADS * HD, HEADS * HD)],
            sems.at[n],
        )
        for n in range(3)
    ]


def project_first(place_ref, p_ref, q_ref, gp_ref, gq_ref, w_ref, acc_ref, sq_ref, wp, wq, sems):
    places_p = [place_ref[k] for k in range(4)]
    places_q = [place_ref[0], place_ref[4]]
    copies = []
    for i, t in enumerate(places_p):
        copies += fetch(w_ref, t, 0, PW, wp, i * PW, sems.at[i])
    for i, t in enumerate(places_q):
        copies += fetch(w_ref, t, PW, QW, wq, i * QW, sems.at[4 + i])
    for c in copies:
        c.start()
    for c in copies[:12]:
        c.wait()
    part, sums = absorb(p_ref[...], gp_ref, places_p, wp[...], None)
    acc_ref[...] = part
    for c in copies[12:]:
        c.wait()
    part, sums = absorb(q_ref[...], gq_ref, places_q, wq[...], sums)
    acc_ref[...] += part
    sq_ref[...] = sums


def split(values):
    high = values.astype(BF)
    return high, (values - high.astype(F32)).astype(BF)


def thirds(values):
    high, low = split(values)
    rest = values - high.astype(F32) - low.astype(F32)
    return high, low, rest.astype(BF)


def attention(
    place_ref, acc0_ref, sq0_ref, p_ref, q1_ref, q2_ref, q3_ref, gp_ref, gq_ref,
    cos_ref, sin_ref, seg_col_ref, seg_row_ref, dctx_ref, w_ref,
    dp_ref, stat_ref, lane_ref, acc, acc0, xp, xq, wp, wq, sems, x_sems,
):
    places_p = [place_ref[4 + k] for k in range(4)]
    places_q = [[place_ref[k], place_ref[4 + k]] for k in range(1, 4)]
    copies_p, copies_q = [], []
    for i, t in enumerate(places_p):
        copies_p += fetch(w_ref, t, 0, PW, wp, i * PW, sems.at[i])
    for g, pair in enumerate(places_q):
        for i, t in enumerate(pair):
            copies_q += fetch(w_ref, t, PW, QW, wq.at[g], i * QW, sems.at[4 + 2 * g + i])
    x_copies = [pltpu.make_async_copy(p_ref, xp, x_sems.at[0])]
    for g, x_ref in enumerate((q1_ref, q2_ref, q3_ref)):
        x_copies.append(pltpu.make_async_copy(x_ref, xq.at[g], x_sems.at[1 + g]))
    x_copies.append(pltpu.make_async_copy(acc0_ref, acc0, x_sems.at[4]))
    for c in x_copies[:1] + copies_p + x_copies[1:4] + copies_q + x_copies[4:]:
        c.start()
    sums = sq0_ref[...]
    for c in x_copies[:1] + copies_p:
        c.wait()
    part, sums = absorb(xp[...], gp_ref, places_p, wp[...], sums)
    acc[...] = part
    for g in range(3):
        for c in x_copies[1 + g : 2 + g] + copies_q[6 * g : 6 * g + 6]:
            c.wait()
        part, sums = absorb(xq[g], gq_ref, places_q[g], wq[g], sums)
        acc[...] += part
    x_copies[4].wait()
    acc[...] += acc0[...]
    mean_square = jnp.sum(sums, axis=1, keepdims=True) * (1.0 / D) + 1e-05
    inverse = lax.rsqrt(mean_square)
    cosines, sines = cos_ref[...], sin_ref[...]
    queries_at = lax.broadcasted_iota(jnp.int32, (TOK, TOK), 0)
    keys_at = lax.broadcasted_iota(jnp.int32, (TOK, TOK), 1)
    allowed = (seg_col_ref[...] == seg_row_ref[...]) & (keys_at <= queries_at)
    scale = HD ** (-0.5)
    row_dot = jnp.zeros((TOK, HD), F32)
    for h in range(HEADS):
        at = [slice(n * HEADS * HD + h * HD, n * HEADS * HD + (h + 1) * HD) for n in range(3)]
        raw = [acc[:, s] * inverse for s in at]
        q, k, v = (r.astype(BF) for r in raw)
        qf, kf = q.astype(F32), k.astype(F32)
        qr = qf * cosines + pltpu.roll(qf, HD // 2, 1) * sines
        kr = kf * cosines + pltpu.roll(kf, HD // 2, 1) * sines
        qh, ql = split(qr)
        kh, kl = split(kr)
        scores = (dot(qh, kh, NT) + (dot(qh, kl, NT) + dot(ql, kh, NT))) * scale
        scores = jnp.where(allowed, scores, -1e30)
        weights = jnp.exp(scores - jnp.max(scores, axis=1, keepdims=True))
        weights = weights / jnp.sum(weights, axis=1, keepdims=True)
        cotangent = dctx_ref[:, h * HD : (h + 1) * HD]
        d_weights = dot(cotangent, v, NT)
        d_scores = weights * (
            d_weights - jnp.sum(weights * d_weights, axis=1, keepdims=True)
        )
        d_scores = (d_scores * scale).astype(BF)
        dv = dot(weights.astype(BF), cotangent, TN)
        dqr = dot(d_scores, kh, NN)
        dkr = dot(d_scores, qh, TN)
        dq = dqr * cosines + pltpu.roll(dqr * sines, HD // 2, 1)
        dk = dkr * cosines + pltpu.roll(dkr * sines, HD // 2, 1)
        for s, r, g in zip(at, raw, (dq, dk, dv)):
            row_dot += r * g
            dp_ref[:, s] = (g * inverse).astype(BF)
    stat_ref[...] = jnp.broadcast_to(inverse * inverse, (TOK, HD))
    ones = jnp.ones((16, HD), BF)
    lane_ref[...] = sum(dot(ones, part, NT) for part in thirds(row_dot * (1.0 / D)))[:8]


def pick(place_ref, quarter_ref, xp_ref, xq_ref, gp_ref, gq_ref, mine_ref, theirs_ref):
    wanted = lax.broadcasted_iota(jnp.int32, (320, SHARE), 0)
    wanted = jnp.where(
        wanted < 160, wanted + 160 * quarter_ref[0], wanted - 160 + 160 * quarter_ref[1]
    )
    unit = lax.broadcasted_iota(jnp.int32, (320, SHARE), 1) == wanted
    unit = jnp.where(unit, 1.0, 0.0).astype(BF)
    for dy in range(2):
        for k in range(4):
            t = place_ref[dy * 4 + k]
            xp = xp_ref[dy, :, k * PW : (k + 1) * PW].astype(F32) * gp_ref[t]
            xq = xq_ref[k, :, dy * QW : (dy + 1) * QW].astype(F32) * gq_ref[t]
            rows = dot(unit[:, :PW], xp.astype(BF), NT) + dot(unit[:, PW:], xq.astype(BF), NT)
            rows = rows.astype(BF)
            mine_ref[t, :, :TOK] = rows[:160]
            mine_ref[t, :, TOK:] = jnp.zeros((160, 64), BF)
            theirs_ref[t, :, :TOK] = rows[160:]
            theirs_ref[t, :, TOK:] = jnp.zeros((160, 64), BF)


def feature_gradient(
    place_ref, source_ref, quarter_ref, dp_ref, lane_ref, ph_ref, pt_ref, q0_ref, q1_ref, q2_ref, q3_ref,
    gp_ref, gq_ref, w_ref, qo0, qo1, qo2, qo3, po0, po1, gain_ref, mine_ref, theirs_ref,
    ws, xp, xq, qs, ps, mine, theirs, sems, x_sems, out_sems,
):
    order = [(k, dy) for k in (1, 3, 2, 0) for dy in (0, 1)]
    copies = []
    for n, (k, dy) in enumerate(order):
        copies.append(fetch(w_ref, place_ref[dy * 4 + k], 0, SHARE, ws.at[n], 0, sems.at[n]))
    x_copies = [
        pltpu.make_async_copy(ref, slot, x_sems.at[i])
        for i, (ref, slot) in enumerate(
            (
                (ph_ref, xp.at[0]), (pt_ref, xp.at[1]), (q0_ref, xq.at[0]),
                (q1_ref, xq.at[1]), (q2_ref, xq.at[2]), (q3_ref, xq.at[3]),
            )
        )
    ]
    for c in copies[0] + x_copies + [c for group in copies[1:] for c in group]:
        c.start()
    gain_ref[:, 2:, :] = jnp.zeros((4, 6, SHARE), F32)
    for column in range(4):
        gain_ref[column, 2:3, :TOK] = lane_ref[0:1]
    dp = dp_ref[...]
    left = []

    def send(source, target, n):
        c = pltpu.make_async_copy(source, target, out_sems.at[n])
        c.start()
        left.append(c)

    for n, (k, dy) in enumerate(order):
        for c in copies[n]:
            c.wait()
        exact = dot(dp, ws[n], NT)
        if n == 0:
            for c in x_copies:
                c.wait()
        back = (4 - k) % 4
        column = place_ref[dy * 4 + k] & 3
        row = pl.ds(place_ref[dy * 4 + k] >> 2, 1)
        x_part = xp[dy, :, back * PW : (back + 1) * PW].astype(F32)
        gain_ref[column, row, :PW] = jnp.sum(exact[:, :PW] * x_part, axis=0, keepdims=True)
        x_part = xq[back, :, dy * QW : (dy + 1) * QW].astype(F32)
        gain_ref[column, row, PW:] = jnp.sum(exact[:, PW:] * x_part, axis=0, keepdims=True)
        ps[dy, :, k * PW : (k + 1) * PW] = exact[:, :PW].astype(BF)
        qs[k, :, dy * QW : (dy + 1) * QW] = exact[:, PW:].astype(BF)
        if dy == 1:
            send(qs.at[k], (qo0, qo1, qo2, qo3)[k], k)
        if n == 3:
            pick(source_ref, quarter_ref, xp, xq, gp_ref, gq_ref, mine, theirs)
            send(theirs, theirs_ref, 6)
            send(mine, mine_ref, 7)
    send(ps.at[1], po1, 5)
    send(ps.at[0], po0, 4)
    for c in left:
        c.wait()


def add_up(q0, q1, q2, q3, p0, p1, own_q, sent_q, own_p, sent1, sent2, sent3):
    total = (q0[...].astype(F32) + q1[...].astype(F32)) + (q2[...].astype(F32) + q3[...].astype(F32))
    own_q[...] = total[:, :QW]
    sent_q[...] = total[:, QW:].astype(BF)
    total = p0[...].astype(F32) + p1[...].astype(F32)
    own_p[...] = total[:, :PW]
    for k, ref in enumerate((sent1, sent2, sent3)):
        ref[...] = total[:, (k + 1) * PW : (k + 2) * PW].astype(BF)


def weight_gradient(
    distances, owner_ref, slot_ref, own_ref, core_ref, f0, f1, f2, f3, d0, d1, d2, d3, out_ref,
    near, far, d_near, d_far, result, sems, near_sems, far_sems, out_sems,
):
    d_copies = [
        pltpu.make_async_copy(d0, d_near.at[pl.ds(0, TOK)], sems.at[0]),
        pltpu.make_async_copy(d1, d_near.at[pl.ds(384, TOK)], sems.at[1]),
        pltpu.make_async_copy(d2, d_far.at[pl.ds(0, TOK)], sems.at[2]),
        pltpu.make_async_copy(d3, d_far.at[pl.ds(TOK, TOK)], sems.at[3]),
    ]
    copies = []
    for i, r in enumerate(distances):
        rows = pl.ds(i * 160, 160)
        t = owner_ref[r]
        copies += [
            pltpu.make_async_copy(own_ref.at[t], near.at[rows, pl.ds(0, 384)], near_sems.at[i, 0]),
            pltpu.make_async_copy(core_ref.at[t], near.at[rows, pl.ds(384, 384)], near_sems.at[i, 1]),
        ]
    for k, f in enumerate((f0, f1, f2, f3)):
        for dy in range(2):
            n = dy * 4 + k
            copies.append(
                pltpu.make_async_copy(f.at[:, pl.ds(dy * 640, 640)], far.at[slot_ref[n]], far_sems.at[n])
            )
    for c in d_copies + copies:
        c.start()
    d_near[TOK:384] = jnp.zeros((64, COLS), BF)
    d_near[384 + TOK :] = jnp.zeros((64, COLS), BF)
    for c in d_copies + copies:
        c.wait()
    at, left = 0, []
    while at < len(distances):
        count = min(2, len(distances) - at)
        group = distances[at : at + count]
        x_far = jnp.concatenate([far[r] for r in group], axis=0) if count > 1 else far[group[0]]
        total = dot(near[at * 160 : (at + count) * 160], d_near[...], NN) + dot(x_far, d_far[...], NN)
        for i in range(count):
            result[at + i] = total[i * 160 : (i + 1) * 160].astype(BF)
            c = pltpu.make_async_copy(result.at[at + i], out_ref.at[at + i], out_sems.at[at + i])
            c.start()
            left.append(c)
        at += count
    for c in left:
        c.wait()


def finish(own_ref, down_ref, up_ref, out_ref):
    total = own_ref[...].astype(F32) + (down_ref[...].astype(F32) + up_ref[...].astype(F32))
    for n in range(3):
        out_ref[n] = total[:, n * HEADS * HD : (n + 1) * HEADS * HD].astype(BF)


VM = pl.BlockSpec(memory_space=pltpu.VMEM)
SM = pl.BlockSpec(memory_space=pltpu.SMEM)
ANY = pl.BlockSpec(memory_space=pl.ANY)
SMALL = pl.CostEstimate(flops=1000, bytes_accessed=1000, transcendentals=0)


def rows_of(width):
    return pl.BlockSpec((64, width), lambda i: (i, 0))


def limit(mib):
    return pltpu.CompilerParams(vmem_limit_bytes=mib * 1024 * 1024)


def shift(values, axis, by, size):
    return lax.ppermute(values, axis, [(i, (i + by) % size) for i in range(size)])


def swap(values, axis, bit, size):
    return lax.ppermute(values, axis, [(i, i ^ bit) for i in range(size)])


def body(x_own, gain, w_qkv, segments, d_context):
    yh, core = lax.axis_index("yh"), lax.axis_index("core")
    yl, x_at = lax.axis_index("yl"), lax.axis_index("x")
    ks = jnp.arange(4, dtype=jnp.int32)
    rows = [yl, 1 - yl]
    sources = jnp.concatenate([r * 4 + (x_at - ks) % 4 for r in rows]).astype(jnp.int32)
    targets = jnp.concatenate([r * 4 + (x_at + ks) % 4 for r in rows]).astype(jnp.int32)
    gain_own = lax.dynamic_slice_in_dim(gain, (yl * 4 + x_at) * SHARE, SHARE, 0)

    xp, xq = x_own[:, :PW], x_own[:, PW:]
    got_p = [shift(xp, "x", k, 4) for k in (1, 2, 3)]
    got_q = swap(xq, "yl", 1, 2)
    scaled = (x_own.astype(F32) * gain_own).astype(BF).T.reshape(2, 2, 160, TOK)
    other = lax.dynamic_index_in_dim(scaled, 1 - yh, 0, False)
    straight = lax.dynamic_index_in_dim(other, core, 0, False)
    across = lax.dynamic_index_in_dim(other, 1 - core, 0, False)
    straight, across, got_p, got_q = lax.optimization_barrier((straight, across, got_p, got_q))
    p_here = jnp.concatenate([xp] + got_p, axis=1)
    q_here = jnp.concatenate([xq, got_q], axis=1)
    p_there = swap(p_here, "yl", 1, 2)
    q_there = [shift(q_here, "x", k, 4) for k in (1, 2, 3)]
    straight = swap(straight, "yh", 1, 2)
    across = lax.ppermute(across, ("yh", "core"), [(i, 3 - i) for i in range(4)])
    quarter = jnp.concatenate([straight, across], axis=1)

    weight = w_qkv.transpose(1, 0, 2)
    gains = gain.reshape(8, 1, SHARE)
    gain_p, gain_q = gains[:, :, :PW], gains[:, :, PW:]
    acc, squares = pl.pallas_call(
        project_first,
        out_shape=(
            jax.ShapeDtypeStruct((TOK, COLS), F32),
            jax.ShapeDtypeStruct((TOK, 128), F32),
        ),
        in_specs=[SM, VM, VM, VM, VM, ANY],
        out_specs=(VM, VM),
        scratch_shapes=[
            pltpu.VMEM((4 * PW, COLS), BF),
            pltpu.VMEM((2 * QW, COLS), BF),
            pltpu.SemaphoreType.DMA((6, 3)),
        ],
        compiler_params=limit(63),
        cost_estimate=SMALL,
        name="project_first",
    )(sources, p_here, q_here, gain_p, gain_q, weight)

    acc, quarter = lax.optimization_barrier((acc, quarter))
    quarter_there = swap(quarter, "yl", 1, 2)

    half = HD // 2
    angles = jnp.arange(TOK, dtype=F32)[:, None] * (
        10000.0 ** (-(2.0 * jnp.arange(half, dtype=F32)) / HD)
    )
    cosines, sines = jnp.cos(angles), jnp.sin(angles)
    cosines = jnp.concatenate([cosines, cosines], axis=1)
    sines = jnp.concatenate([-sines, sines], axis=1)
    d_packed, stats, row_dots = pl.pallas_call(
        attention,
        out_shape=(
            jax.ShapeDtypeStruct((TOK, COLS), BF),
            jax.ShapeDtypeStruct((TOK, HD), F32),
            jax.ShapeDtypeStruct((8, TOK), F32),
        ),
        in_specs=[SM, ANY, VM] + [ANY] * 4 + [VM] * 7 + [ANY],
        out_specs=(VM, VM, VM),
        scratch_shapes=[
            pltpu.VMEM((TOK, COLS), F32),
            pltpu.VMEM((TOK, COLS), F32),
            pltpu.VMEM((TOK, 4 * PW), BF),
            pltpu.VMEM((3, TOK, WIDE), BF),
            pltpu.VMEM((4 * PW, COLS), BF),
            pltpu.VMEM((3, 2 * QW, COLS), BF),
            pltpu.SemaphoreType.DMA((10, 3)),
            pltpu.SemaphoreType.DMA((5,)),
        ],
        compiler_params=limit(63),
        cost_estimate=SMALL,
        name="attention",
    )(
        sources, acc, squares, p_there, *q_there, gain_p, gain_q, cosines, sines,
        segments[:, None], segments[None, :], d_context, weight,
    )

    d_packed, quarter, quarter_there = lax.optimization_barrier((d_packed, quarter, quarter_there))
    far = [jnp.concatenate([quarter, quarter_there], axis=1)]
    from_yh = swap(d_packed, "yh", 1, 2)
    from_core = swap(d_packed, "core", 1, 2)
    far = far + [shift(far[0], "x", k, 4) for k in (1, 2, 3)]
    quarters = jnp.stack([yh * 2 + core, yh * 2 + 1 - core]).astype(jnp.int32)
    *pieces, gains_here, x_mine, x_theirs = pl.pallas_call(
        feature_gradient,
        out_shape=tuple(
            [jax.ShapeDtypeStruct((TOK, WIDE), BF)] * 4
            + [jax.ShapeDtypeStruct((TOK, 4 * PW), BF)] * 2
            + [jax.ShapeDtypeStruct((4, 8, SHARE), F32)]
            + [jax.ShapeDtypeStruct((8, 160, 384), BF)] * 2
        ),
        in_specs=[SM] * 3 + [VM] * 2 + [ANY] * 6 + [VM] * 2 + [ANY],
        out_specs=(ANY,) * 6 + (VM, ANY, ANY),
        scratch_shapes=[
            pltpu.VMEM((8, SHARE, COLS), BF),
            pltpu.VMEM((2, TOK, 4 * PW), BF),
            pltpu.VMEM((4, TOK, WIDE), BF),
            pltpu.VMEM((4, TOK, WIDE), BF),
            pltpu.VMEM((2, TOK, 4 * PW), BF),
            pltpu.VMEM((8, 160, 384), BF),
            pltpu.VMEM((8, 160, 384), BF),
            pltpu.SemaphoreType.DMA((8, 3)),
            pltpu.SemaphoreType.DMA((6,)),
            pltpu.SemaphoreType.DMA((8,)),
        ],
        compiler_params=limit(63),
        cost_estimate=SMALL,
        name="feature_gradient",
    )(
        targets, sources, quarters, d_packed, row_dots, p_here, p_there, q_here, *q_there, gain_p, gain_q, weight,
    )
    from_yh, from_core, far, x_theirs, gains_here = lax.optimization_barrier(
        (from_yh, from_core, far, x_theirs, gains_here)
    )
    small = [lax.dynamic_index_in_dim(gains_here, x_at ^ bit, 0, False) for bit in range(4)]
    small = small[:1] + [swap(small[bit], "x", bit, 4) for bit in (1, 2, 3)]
    from_both = swap(from_yh, "core", 1, 2)
    x_core = swap(x_theirs, "core", 1, 2)
    from_both, x_core, small, pieces = lax.optimization_barrier((from_both, x_core, small, pieces))
    small = (small[0] + small[1]) + (small[2] + small[3])

    z_at = lax.axis_index("z")
    owners = ((z_at + jnp.arange(8)) % 8).astype(jnp.int32)
    slots = ((sources - z_at) % 8).astype(jnp.int32)
    operands = (owners, slots, x_mine, x_core, *far, d_packed, from_core, from_yh, from_both)

    def rows_for(distances, name):
        return pl.pallas_call(
            functools.partial(weight_gradient, distances),
            out_shape=jax.ShapeDtypeStruct((len(distances), 160, COLS), BF),
            in_specs=[SM, SM] + [ANY] * 10,
            out_specs=ANY,
            scratch_shapes=[
                pltpu.VMEM((len(distances) * 160, 768), BF),
                pltpu.VMEM((8, 160, 640), BF),
                pltpu.VMEM((768, COLS), BF),
                pltpu.VMEM((640, COLS), BF),
                pltpu.VMEM((len(distances), 160, COLS), BF),
                pltpu.SemaphoreType.DMA((4,)),
                pltpu.SemaphoreType.DMA((len(distances), 2)),
                pltpu.SemaphoreType.DMA((8,)),
                pltpu.SemaphoreType.DMA((len(distances),)),
            ],
            compiler_params=limit(63),
            cost_estimate=SMALL,
            name=name,
        )(*operands)

    def plus(a, b):
        return (a.astype(F32) + b.astype(F32)).astype(BF)

    along_x = [shift(pieces[k], "x", k, 4) for k in (1, 2, 3)]
    along_y = swap(pieces[5], "yl", 1, 2)
    down = shift(rows_for((4,), "weight_gradient_far")[0], "z", 1, 8)
    rest = rows_for((3, 5, 2, 6, 1, 7, 0), "weight_gradient_rest")
    heard = [swap(small, "yl", 1, 2), swap(small, "yh", 1, 2)]
    heard.append(lax.ppermute(small, ("yh", "yl"), [(i, 3 - i) for i in range(4)]))
    down, heard, along_x[0], along_x[2], rest = lax.optimization_barrier(
        (down, heard, along_x[0], along_x[2], rest)
    )
    row_dot = small[2, :TOK] + heard[0][2, :TOK]
    shares = [lax.dynamic_index_in_dim(v, yl, 0, False) for v in (small, *heard)]
    share = (shares[0] + shares[1]) + (shares[2] + shares[3])
    down = shift(plus(rest[0], down), "z", 1, 8)
    up = shift(rest[1], "z", -1, 8)
    there = swap(share, "z", 1, 8)
    down, up, there, along_x, along_y = lax.optimization_barrier((down, up, there, along_x, along_y))
    share = share + there
    own_q, sent_q, own_p, *sent_p = pl.pallas_call(
        add_up,
        out_shape=(
            jax.ShapeDtypeStruct((TOK, QW), F32),
            jax.ShapeDtypeStruct((TOK, QW), BF),
            jax.ShapeDtypeStruct((TOK, PW), F32),
            jax.ShapeDtypeStruct((TOK, PW), BF),
            jax.ShapeDtypeStruct((TOK, PW), BF),
            jax.ShapeDtypeStruct((TOK, PW), BF),
        ),
        grid=(5,),
        in_specs=[rows_of(WIDE)] * 4 + [rows_of(4 * PW)] * 2,
        out_specs=(rows_of(QW), rows_of(QW)) + (rows_of(PW),) * 4,
        compiler_params=limit(16),
        cost_estimate=SMALL,
        name="add_up",
    )(pieces[0], *along_x, pieces[4], along_y)
    down = shift(plus(rest[2], down), "z", 1, 8)
    up = shift(plus(rest[3], up), "z", -1, 8)
    sent_q = swap(sent_q, "yl", 1, 2)
    sent_p = [shift(a, "x", k, 4) for k, a in zip((1, 2, 3), sent_p)]
    there = swap(share, "z", 2, 8)
    down, up, sent_q, sent_p, there = lax.optimization_barrier((down, up, sent_q, sent_p, there))
    share = share + there
    down = shift(plus(rest[4], down), "z", 1, 8)
    up = shift(plus(rest[5], up), "z", -1, 8)
    d_normed = jnp.concatenate(
        [sum((a.astype(F32) for a in sent_p), own_p), own_q + sent_q.astype(F32)], axis=1
    )
    row_dot = row_dot * stats[:, 0]
    input_gradient = (d_normed * gain_own - x_own.astype(F32) * row_dot[:, None]).astype(BF)
    share = share + swap(share, "z", 4, 8)
    gain_gradient = share + swap(share, "core", 1, 2)
    down, up, gain_gradient = lax.optimization_barrier((down, up, gain_gradient))
    d_weight = pl.pallas_call(
        finish,
        out_shape=jax.ShapeDtypeStruct((3, 160, HEADS * HD), BF),
        in_specs=[VM] * 3,
        out_specs=VM,
        compiler_params=limit(8),
        cost_estimate=SMALL,
        name="finish",
    )(rest[6], down, up)
    return input_gradient, gain_gradient, d_weight.transpose(1, 0, 2)


def solution(mesh):
    fine = Mesh(mesh.devices.reshape(8, 2, 2, 2, 4), ("z", "yh", "core", "yl", "x"))
    dp, tensor = ("z", "yh", "core"), ("yl", "x")
    in_specs = (P(dp, tensor), P(), P(None, None, tensor), P(dp), P(dp, tensor))
    out_specs = (P(dp, tensor), P(tensor), P(dp, None, tensor))
    return jax.shard_map(
        body, mesh=fine, in_specs=in_specs, out_specs=out_specs, check_vma=False
    )
```

```python
import functools

import jax
import jax.numpy as jnp
from jax import lax
from jax.experimental import pallas as pl
from jax.experimental.pallas import tpu as pltpu
from jax.sharding import Mesh, PartitionSpec as P

HD = 128
HEADS = 3
TOK = 320
D = 5120
COLS = 1152
SHARE = 640
PW = 256
WIDE = 768
QW = 384
BF = jnp.bfloat16
F32 = jnp.float32


def dot(a, b, dims):
    return lax.dot_general(a, b, (dims, ((), ())), preferred_element_type=F32)


NN = ((1,), (0,))
NT = ((1,), (1,))
TN = ((0,), (0,))


def square_sum(values):
    width = values.shape[1]
    squares = values * values
    total = squares[:, :128]
    for start in range(128, width, 128):
        total = total + squares[:, start : start + 128]
    return total


def absorb(x, gain_ref, places, w_slot, sums):
    width = x.shape[1] // len(places)
    values = x.astype(F32)
    gains = jnp.concatenate([gain_ref[t] for t in places], axis=1)
    sums = square_sum(values) if sums is None else sums + square_sum(values)
    return dot((values * gains).astype(BF), w_slot, NN), sums


def fetch(w_ref, place, first, count, slot, start, sems):
    return [
        pltpu.make_async_copy(
            w_ref.at[n, pl.ds(place * SHARE + first, count)],
            slot.at[pl.ds(start, count), pl.ds(n * HEADS * HD, HEADS * HD)],
            sems.at[n],
        )
        for n in range(3)
    ]


def project_first(place_ref, p_ref, q_ref, gp_ref, gq_ref, w_ref, acc_ref, sq_ref, wp, wq, sems):
    places_p = [place_ref[k] for k in range(4)]
    places_q = [place_ref[0], place_ref[4]]
    copies = []
    for i, t in enumerate(places_p):
        copies += fetch(w_ref, t, 0, PW, wp, i * PW, sems.at[i])
    for i, t in enumerate(places_q):
        copies += fetch(w_ref, t, PW, QW, wq, i * QW, sems.at[4 + i])
    for c in copies:
        c.start()
    for c in copies[:12]:
        c.wait()
    part, sums = absorb(p_ref[...], gp_ref, places_p, wp[...], None)
    acc_ref[...] = part
    for c in copies[12:]:
        c.wait()
    part, sums = absorb(q_ref[...], gq_ref, places_q, wq[...], sums)
    acc_ref[...] += part
    sq_ref[...] = sums


def split(values):
    high = values.astype(BF)
    return high, (values - high.astype(F32)).astype(BF)


def thirds(values):
    high, low = split(values)
    rest = values - high.astype(F32) - low.astype(F32)
    return high, low, rest.astype(BF)


def attention(
    place_ref, acc0_ref, sq0_ref, p_ref, q1_ref, q2_ref, q3_ref, gp_ref, gq_ref,
    cos_ref, sin_ref, seg_col_ref, seg_row_ref, dctx_ref, w_ref,
    dp_ref, stat_ref, lane_ref, acc, acc0, xp, xq, wp, wq, sems, x_sems,
):
    places_p = [place_ref[4 + k] for k in range(4)]
    places_q = [[place_ref[k], place_ref[4 + k]] for k in range(1, 4)]
    copies_p, copies_q = [], []
    for i, t in enumerate(places_p):
        copies_p += fetch(w_ref, t, 0, PW, wp, i * PW, sems.at[i])
    for g, pair in enumerate(places_q):
        for i, t in enumerate(pair):
            copies_q += fetch(w_ref, t, PW, QW, wq.at[g], i * QW, sems.at[4 + 2 * g + i])
    x_copies = [pltpu.make_async_copy(p_ref, xp, x_sems.at[0])]
    for g, x_ref in enumerate((q1_ref, q2_ref, q3_ref)):
        x_copies.append(pltpu.make_async_copy(x_ref, xq.at[g], x_sems.at[1 + g]))
    x_copies.append(pltpu.make_async_copy(acc0_ref, acc0, x_sems.at[4]))
    for c in x_copies[:1] + copies_p + x_copies[1:4] + copies_q + x_copies[4:]:
        c.start()
    sums = sq0_ref[...]
    for c in x_copies[:1] + copies_p:
        c.wait()
    part, sums = absorb(xp[...], gp_ref, places_p, wp[...], sums)
    acc[...] = part
    for g in range(3):
        for c in x_copies[1 + g : 2 + g] + copies_q[6 * g : 6 * g + 6]:
            c.wait()
        part, sums = absorb(xq[g], gq_ref, places_q[g], wq[g], sums)
        acc[...] += part
    x_copies[4].wait()
    acc[...] += acc0[...]
    mean_square = jnp.sum(sums, axis=1, keepdims=True) * (1.0 / D) + 1e-05
    inverse = lax.rsqrt(mean_square)
    cosines, sines = cos_ref[...], sin_ref[...]
    queries_at = lax.broadcasted_iota(jnp.int32, (TOK, TOK), 0)
    keys_at = lax.broadcasted_iota(jnp.int32, (TOK, TOK), 1)
    allowed = (seg_col_ref[...] == seg_row_ref[...]) & (keys_at <= queries_at)
    scale = HD ** (-0.5)
    row_dot = jnp.zeros((TOK, HD), F32)
    for h in range(HEADS):
        at = [slice(n * HEADS * HD + h * HD, n * HEADS * HD + (h + 1) * HD) for n in range(3)]
        raw = [acc[:, s] * inverse for s in at]
        q, k, v = (r.astype(BF) for r in raw)
        qf, kf = q.astype(F32), k.astype(F32)
        qr = qf * cosines + pltpu.roll(qf, HD // 2, 1) * sines
        kr = kf * cosines + pltpu.roll(kf, HD // 2, 1) * sines
        qh, ql = split(qr)
        kh, kl = split(kr)
        scores = (dot(qh, kh, NT) + (dot(qh, kl, NT) + dot(ql, kh, NT))) * scale
        scores = jnp.where(allowed, scores, -1e30)
        weights = jnp.exp(scores - jnp.max(scores, axis=1, keepdims=True))
        weights = weights / jnp.sum(weights, axis=1, keepdims=True)
        cotangent = dctx_ref[:, h * HD : (h + 1) * HD]
        d_weights = dot(cotangent, v, NT)
        d_scores = weights * (
            d_weights - jnp.sum(weights * d_weights, axis=1, keepdims=True)
        )
        d_scores = (d_scores * scale).astype(BF)
        dv = dot(weights.astype(BF), cotangent, TN)
        dqr = dot(d_scores, kh, NN)
        dkr = dot(d_scores, qh, TN)
        dq = dqr * cosines + pltpu.roll(dqr * sines, HD // 2, 1)
        dk = dkr * cosines + pltpu.roll(dkr * sines, HD // 2, 1)
        for s, r, g in zip(at, raw, (dq, dk, dv)):
            row_dot += r * g
            dp_ref[:, s] = (g * inverse).astype(BF)
    stat_ref[...] = jnp.broadcast_to(inverse * inverse, (TOK, HD))
    ones = jnp.ones((16, HD), BF)
    lane_ref[...] = sum(dot(ones, part, NT) for part in thirds(row_dot * (1.0 / D)))[:8]


def pick(
    place_ref, core_ref, ph_ref, pt_ref, q0_ref, q1_ref, q2_ref, q3_ref, gp_ref, gq_ref,
    mine_ref, theirs_ref, xp, xq, mine, theirs, x_sems, out_sems,
):
    x_copies = load_features((ph_ref, pt_ref), (q0_ref, q1_ref, q2_ref, q3_ref), xp, xq, x_sems)
    for c in x_copies:
        c.start()
    row = lax.broadcasted_iota(jnp.int32, (SHARE, SHARE), 0)
    place = jnp.where(row < 320, core_ref[0], 1 - core_ref[0]) * 160
    wanted = place + row + jnp.where(row % 320 < 160, 0, 160) - jnp.where(row < 320, 0, 320)
    unit = lax.broadcasted_iota(jnp.int32, (SHARE, SHARE), 1) == wanted
    unit = jnp.where(unit, 1.0, 0.0).astype(BF)
    mine[:, :, TOK:] = jnp.zeros((8, 320, 64), BF)
    theirs[:, :, TOK:] = jnp.zeros((8, 320, 64), BF)
    for c in x_copies:
        c.wait()
    left = []
    for dy in range(2):
        for k in range(4):
            n = dy * 4 + k
            t = place_ref[n]
            p_part = xp[dy, :, k * PW : (k + 1) * PW].astype(F32) * gp_ref[t]
            q_part = xq[k, :, dy * QW : (dy + 1) * QW].astype(F32) * gq_ref[t]
            part = jnp.concatenate([p_part.astype(BF), q_part.astype(BF)], axis=1)
            rows = dot(unit, part, NT).astype(BF)
            mine[n, :, :TOK] = rows[:320]
            theirs[n, :, :TOK] = rows[320:]
            for i, (source, target) in enumerate(((theirs, theirs_ref), (mine, mine_ref))):
                c = pltpu.make_async_copy(source.at[n], target.at[t], out_sems.at[n, i])
                c.start()
                left.append(c)
    for c in left:
        c.wait()


def load_features(p_refs, q_refs, xp, xq, sems):
    pairs = [(r, xp.at[i]) for i, r in enumerate(p_refs)] + [(r, xq.at[i]) for i, r in enumerate(q_refs)]
    return [pltpu.make_async_copy(r, slot, sems.at[i]) for i, (r, slot) in enumerate(pairs)]


def feature_gradient(
    place_ref, dp_ref, lane_ref, ph_ref, pt_ref, q0_ref, q1_ref, q2_ref, q3_ref,
    w_ref, qo0, qo1, qo2, qo3, po0, po1, gain_ref, ws, xp, xq, qs, ps, sems, x_sems, out_sems,
):
    order = [(k, dy) for k in (1, 3, 2, 0) for dy in (0, 1)]
    copies = []
    for n, (k, dy) in enumerate(order):
        copies.append(fetch(w_ref, place_ref[dy * 4 + k], 0, SHARE, ws.at[n], 0, sems.at[n]))
    x_copies = load_features((ph_ref, pt_ref), (q0_ref, q1_ref, q2_ref, q3_ref), xp, xq, x_sems)
    for c in copies[0] + x_copies + [c for group in copies[1:] for c in group]:
        c.start()
    gain_ref[:, 2:, :] = jnp.zeros((4, 6, SHARE), F32)
    for column in range(4):
        gain_ref[column, 2:3, :TOK] = lane_ref[0:1]
    dp = dp_ref[...]
    left = []

    def send(source, target, n):
        c = pltpu.make_async_copy(source, target, out_sems.at[n])
        c.start()
        left.append(c)

    for n, (k, dy) in enumerate(order):
        for c in copies[n]:
            c.wait()
        exact = dot(dp, ws[n], NT)
        if n == 0:
            for c in x_copies:
                c.wait()
        back = (4 - k) % 4
        column = place_ref[dy * 4 + k] & 3
        row = pl.ds(place_ref[dy * 4 + k] >> 2, 1)
        x_part = xp[dy, :, back * PW : (back + 1) * PW].astype(F32)
        gain_ref[column, row, :PW] = jnp.sum(exact[:, :PW] * x_part, axis=0, keepdims=True)
        x_part = xq[back, :, dy * QW : (dy + 1) * QW].astype(F32)
        gain_ref[column, row, PW:] = jnp.sum(exact[:, PW:] * x_part, axis=0, keepdims=True)
        ps[dy, :, k * PW : (k + 1) * PW] = exact[:, :PW].astype(BF)
        qs[k, :, dy * QW : (dy + 1) * QW] = exact[:, PW:].astype(BF)
        if dy == 1:
            send(qs.at[k], (qo0, qo1, qo2, qo3)[k], k)
    send(ps.at[1], po1, 5)
    send(ps.at[0], po0, 4)
    for c in left:
        c.wait()


def add_up(q0, q1, q2, q3, p0, p1, own_q, sent_q, own_p, sent1, sent2, sent3):
    total = (q0[...].astype(F32) + q1[...].astype(F32)) + (q2[...].astype(F32) + q3[...].astype(F32))
    own_q[...] = total[:, :QW]
    sent_q[...] = total[:, QW:].astype(BF)
    total = p0[...].astype(F32) + p1[...].astype(F32)
    own_p[...] = total[:, :PW]
    for k, ref in enumerate((sent1, sent2, sent3)):
        ref[...] = total[:, (k + 1) * PW : (k + 2) * PW].astype(BF)


def weight_gradient(
    distances, owner_ref, own_ref, core_ref, d0, d1, out_ref,
    x_rows, d_rows, result, sems, x_sems, out_sems,
):
    copies = [
        pltpu.make_async_copy(d0, d_rows.at[pl.ds(0, TOK)], sems.at[0]),
        pltpu.make_async_copy(d1, d_rows.at[pl.ds(384, TOK)], sems.at[1]),
    ]
    x_copies = []
    for i, r in enumerate(distances):
        t = owner_ref[r]
        x_copies += [
            pltpu.make_async_copy(own_ref.at[t], x_rows.at[i, :, pl.ds(0, 384)], x_sems.at[i, 0]),
            pltpu.make_async_copy(core_ref.at[t], x_rows.at[i, :, pl.ds(384, 384)], x_sems.at[i, 1]),
        ]
    for c in copies + x_copies:
        c.start()
    d_rows[TOK:384] = jnp.zeros((64, COLS), BF)
    d_rows[384 + TOK :] = jnp.zeros((64, COLS), BF)
    for c in copies:
        c.wait()
    left = []
    for i in range(len(distances)):
        for c in x_copies[2 * i : 2 * i + 2]:
            c.wait()
        result[i] = dot(x_rows[i], d_rows[...], NN).astype(BF)
        c = pltpu.make_async_copy(result.at[i], out_ref.at[i], out_sems.at[i])
        c.start()
        left.append(c)
    for c in left:
        c.wait()


def finish(kept_ref, got_ref, out_ref):
    total = kept_ref[...] + got_ref[...].astype(F32)
    for n in range(3):
        out_ref[n] = total[:, n * HEADS * HD : (n + 1) * HEADS * HD].astype(BF)


VM = pl.BlockSpec(memory_space=pltpu.VMEM)
SM = pl.BlockSpec(memory_space=pltpu.SMEM)
ANY = pl.BlockSpec(memory_space=pl.ANY)
SMALL = pl.CostEstimate(flops=1000, bytes_accessed=1000, transcendentals=0)


def rows_of(width):
    return pl.BlockSpec((64, width), lambda i: (i, 0))


def limit(mib):
    return pltpu.CompilerParams(vmem_limit_bytes=mib * 1024 * 1024)


def shift(values, axis, by, size):
    return lax.ppermute(values, axis, [(i, (i + by) % size) for i in range(size)])


def swap(values, axis, bit, size):
    return lax.ppermute(values, axis, [(i, i ^ bit) for i in range(size)])


def body(x_own, gain, w_qkv, segments, d_context):
    yh, core = lax.axis_index("yh"), lax.axis_index("core")
    yl, x_at = lax.axis_index("yl"), lax.axis_index("x")
    ks = jnp.arange(4, dtype=jnp.int32)
    rows = [yl, 1 - yl]
    sources = jnp.concatenate([r * 4 + (x_at - ks) % 4 for r in rows]).astype(jnp.int32)
    targets = jnp.concatenate([r * 4 + (x_at + ks) % 4 for r in rows]).astype(jnp.int32)
    gain_own = lax.dynamic_slice_in_dim(gain, (yl * 4 + x_at) * SHARE, SHARE, 0)

    xp, xq = x_own[:, :PW], x_own[:, PW:]
    got_p = [shift(xp, "x", k, 4) for k in (1, 2, 3)]
    got_q = swap(xq, "yl", 1, 2)
    p_here = jnp.concatenate([xp] + got_p, axis=1)
    q_here = jnp.concatenate([xq, got_q], axis=1)
    p_there = swap(p_here, "yl", 1, 2)
    q_there = [shift(q_here, "x", k, 4) for k in (1, 2, 3)]

    weight = w_qkv.transpose(1, 0, 2)
    gains = gain.reshape(8, 1, SHARE)
    gain_p, gain_q = gains[:, :, :PW], gains[:, :, PW:]
    acc, squares = pl.pallas_call(
        project_first,
        out_shape=(
            jax.ShapeDtypeStruct((TOK, COLS), F32),
            jax.ShapeDtypeStruct((TOK, 128), F32),
        ),
        in_specs=[SM, VM, VM, VM, VM, ANY],
        out_specs=(VM, VM),
        scratch_shapes=[
            pltpu.VMEM((4 * PW, COLS), BF),
            pltpu.VMEM((2 * QW, COLS), BF),
            pltpu.SemaphoreType.DMA((6, 3)),
        ],
        compiler_params=limit(63),
        cost_estimate=SMALL,
        name="project_first",
    )(sources, p_here, q_here, gain_p, gain_q, weight)


    half = HD // 2
    angles = jnp.arange(TOK, dtype=F32)[:, None] * (
        10000.0 ** (-(2.0 * jnp.arange(half, dtype=F32)) / HD)
    )
    cosines, sines = jnp.cos(angles), jnp.sin(angles)
    cosines = jnp.concatenate([cosines, cosines], axis=1)
    sines = jnp.concatenate([-sines, sines], axis=1)
    d_packed, stats, row_dots = pl.pallas_call(
        attention,
        out_shape=(
            jax.ShapeDtypeStruct((TOK, COLS), BF),
            jax.ShapeDtypeStruct((TOK, HD), F32),
            jax.ShapeDtypeStruct((8, TOK), F32),
        ),
        in_specs=[SM, ANY, VM] + [ANY] * 4 + [VM] * 7 + [ANY],
        out_specs=(VM, VM, VM),
        scratch_shapes=[
            pltpu.VMEM((TOK, COLS), F32),
            pltpu.VMEM((TOK, COLS), F32),
            pltpu.VMEM((TOK, 4 * PW), BF),
            pltpu.VMEM((3, TOK, WIDE), BF),
            pltpu.VMEM((4 * PW, COLS), BF),
            pltpu.VMEM((3, 2 * QW, COLS), BF),
            pltpu.SemaphoreType.DMA((10, 3)),
            pltpu.SemaphoreType.DMA((5,)),
        ],
        compiler_params=limit(63),
        cost_estimate=SMALL,
        name="attention",
    )(
        sources, acc, squares, p_there, *q_there, gain_p, gain_q, cosines, sines,
        segments[:, None], segments[None, :], d_context, weight,
    )

    from_core = swap(d_packed, "core", 1, 2)
    d_packed, row_dots, p_here = lax.optimization_barrier((d_packed, row_dots, p_here))
    features = (p_here, p_there, q_here, *q_there)
    x_scratch = [pltpu.VMEM((2, TOK, 4 * PW), BF), pltpu.VMEM((4, TOK, WIDE), BF)]
    x_mine, x_theirs = pl.pallas_call(
        pick,
        out_shape=(jax.ShapeDtypeStruct((8, 320, 384), BF),) * 2,
        in_specs=[SM] * 2 + [ANY] * 6 + [VM] * 2,
        out_specs=(ANY,) * 2,
        scratch_shapes=x_scratch
        + [
            pltpu.VMEM((8, 320, 384), BF),
            pltpu.VMEM((8, 320, 384), BF),
            pltpu.SemaphoreType.DMA((6,)),
            pltpu.SemaphoreType.DMA((8, 2)),
        ],
        compiler_params=limit(63),
        cost_estimate=SMALL,
        name="pick",
    )(sources, jnp.full((1,), core, jnp.int32), *features, gain_p, gain_q)
    x_core = swap(x_theirs, "core", 1, 2)

    z_at = lax.axis_index("z")
    owners = ((z_at + jnp.arange(8)) % 8).astype(jnp.int32)

    def rows_for(distances, name):
        count = len(distances)
        return pl.pallas_call(
            functools.partial(weight_gradient, distances),
            out_shape=jax.ShapeDtypeStruct((count, 320, COLS), BF),
            in_specs=[SM] + [ANY] * 4,
            out_specs=ANY,
            scratch_shapes=[
                pltpu.VMEM((count, 320, 768), BF),
                pltpu.VMEM((768, COLS), BF),
                pltpu.VMEM((count, 320, COLS), BF),
                pltpu.SemaphoreType.DMA((2,)),
                pltpu.SemaphoreType.DMA((count, 2)),
                pltpu.SemaphoreType.DMA((count,)),
            ],
            compiler_params=limit(63),
            cost_estimate=SMALL,
            name=name,
        )(owners, x_mine, x_core, d_packed, from_core)

    def plus(a, b):
        return (a.astype(F32) + b.astype(F32)).astype(BF)

    far_rows = rows_for((4,), "weight_gradient_far")[0]
    far_rows, d_here = lax.optimization_barrier((far_rows, d_packed))
    down = shift(far_rows, "z", 1, 8)
    middle_rows = rows_for((3, 5), "weight_gradient_middle")
    *pieces, gains_here = pl.pallas_call(
        feature_gradient,
        out_shape=tuple(
            [jax.ShapeDtypeStruct((TOK, WIDE), BF)] * 4
            + [jax.ShapeDtypeStruct((TOK, 4 * PW), BF)] * 2
            + [jax.ShapeDtypeStruct((4, 8, SHARE), F32)]
        ),
        in_specs=[SM] + [VM] * 2 + [ANY] * 7,
        out_specs=(ANY,) * 6 + (VM,),
        scratch_shapes=[
            pltpu.VMEM((8, SHARE, COLS), BF),
            *x_scratch,
            pltpu.VMEM((4, TOK, WIDE), BF),
            pltpu.VMEM((2, TOK, 4 * PW), BF),
            pltpu.SemaphoreType.DMA((8, 3)),
            pltpu.SemaphoreType.DMA((6,)),
            pltpu.SemaphoreType.DMA((6,)),
        ],
        compiler_params=limit(63),
        cost_estimate=SMALL,
        name="feature_gradient",
    )(targets, d_here, row_dots, *features, weight)
    down, gains_here, middle_rows = lax.optimization_barrier((down, gains_here, middle_rows))
    down = shift(plus(middle_rows[0], down), "z", 1, 8)
    up = shift(middle_rows[1], "z", -1, 8)
    small = [lax.dynamic_index_in_dim(gains_here, x_at ^ bit, 0, False) for bit in range(4)]
    small = small[:1] + [swap(small[bit], "x", bit, 4) for bit in (1, 2, 3)]
    small, pieces = lax.optimization_barrier((small, pieces))
    small = (small[0] + small[1]) + (small[2] + small[3])
    along_x = [shift(pieces[k], "x", k, 4) for k in (1, 2, 3)]
    along_y = swap(pieces[5], "yl", 1, 2)
    near_rows = rows_for((2, 6, 1, 7, 0), "weight_gradient_near")
    down, up, near_rows, along_x[0], along_x[2] = lax.optimization_barrier(
        (down, up, near_rows, along_x[0], along_x[2])
    )
    down = shift(plus(near_rows[0], down), "z", 1, 8)
    up = shift(plus(near_rows[1], up), "z", -1, 8)
    there = swap(small, "yl", 1, 2)
    row_dot = small[2, :TOK] + there[2, :TOK]
    share = lax.dynamic_index_in_dim(small, yl, 0, False) + lax.dynamic_index_in_dim(there, yl, 0, False)
    share = share + swap(share, "yh", 1, 2)
    down, up, along_x[1], along_y, share = lax.optimization_barrier(
        (down, up, along_x[1], along_y, share)
    )
    down = shift(plus(near_rows[2], down), "z", 1, 8)
    up = shift(plus(near_rows[3], up), "z", -1, 8)
    own_q, sent_q, own_p, *sent_p = pl.pallas_call(
        add_up,
        out_shape=(
            jax.ShapeDtypeStruct((TOK, QW), F32),
            jax.ShapeDtypeStruct((TOK, QW), BF),
            jax.ShapeDtypeStruct((TOK, PW), F32),
            jax.ShapeDtypeStruct((TOK, PW), BF),
            jax.ShapeDtypeStruct((TOK, PW), BF),
            jax.ShapeDtypeStruct((TOK, PW), BF),
        ),
        grid=(5,),
        in_specs=[rows_of(WIDE)] * 4 + [rows_of(4 * PW)] * 2,
        out_specs=(rows_of(QW), rows_of(QW)) + (rows_of(PW),) * 4,
        compiler_params=limit(16),
        cost_estimate=SMALL,
        name="add_up",
    )(pieces[0], *along_x, pieces[4], along_y)
    sent_q = swap(sent_q, "yl", 1, 2)
    sent_p = [shift(a, "x", k, 4) for k, a in zip((1, 2, 3), sent_p)]
    share = share + swap(share, "z", 1, 8)
    share = share + swap(share, "z", 2, 8)
    down, up, sent_q, sent_p, share = lax.optimization_barrier((down, up, sent_q, sent_p, share))
    total = near_rows[4].astype(F32) + (down.astype(F32) + up.astype(F32))
    kept = lax.dynamic_slice_in_dim(total, yh * 160, 160, 0)
    got = swap(lax.dynamic_slice_in_dim(total, (1 - yh) * 160, 160, 0).astype(BF), "yh", 1, 2)
    share = share + swap(share, "z", 4, 8)
    gain_gradient = share + swap(share, "core", 1, 2)
    d_normed = jnp.concatenate(
        [sum((a.astype(F32) for a in sent_p), own_p), own_q + sent_q.astype(F32)], axis=1
    )
    row_dot = row_dot * stats[:, 0]
    input_gradient = (d_normed * gain_own - x_own.astype(F32) * row_dot[:, None]).astype(BF)
    got, gain_gradient, input_gradient = lax.optimization_barrier((got, gain_gradient, input_gradient))
    d_weight = pl.pallas_call(
        finish,
        out_shape=jax.ShapeDtypeStruct((3, 160, HEADS * HD), BF),
        in_specs=[VM] * 2,
        out_specs=VM,
        compiler_params=limit(8),
        cost_estimate=SMALL,
        name="finish",
    )(kept, got)
    return input_gradient, gain_gradient, d_weight.transpose(1, 0, 2)


def solution(mesh):
    fine = Mesh(mesh.devices.reshape(8, 2, 2, 2, 4), ("z", "yh", "core", "yl", "x"))
    dp, tensor = ("z", "yh", "core"), ("yl", "x")
    in_specs = (P(dp, tensor), P(), P(None, None, tensor), P(dp), P(dp, tensor))
    out_specs = (P(dp, tensor), P(tensor), P(dp, None, tensor))
    return jax.shard_map(
        body, mesh=fine, in_specs=in_specs, out_specs=out_specs, check_vma=False
    )
```

```python
import functools

import jax
import jax.numpy as jnp
from jax import lax
from jax.experimental import pallas as pl
from jax.experimental.pallas import tpu as pltpu
from jax.sharding import Mesh, PartitionSpec as P

HD = 128
HEADS = 3
TOK = 320
D = 5120
COLS = 1152
SHARE = 640
PW = 256
WIDE = 768
QW = 384
BF = jnp.bfloat16
F32 = jnp.float32


def dot(a, b, dims):
    return lax.dot_general(a, b, (dims, ((), ())), preferred_element_type=F32)


NN = ((1,), (0,))
NT = ((1,), (1,))
TN = ((0,), (0,))


def square_sum(values):
    width = values.shape[1]
    squares = values * values
    total = squares[:, :128]
    for start in range(128, width, 128):
        total = total + squares[:, start : start + 128]
    return total


def absorb(x, gain_ref, places, w_slot, sums):
    width = x.shape[1] // len(places)
    values = x.astype(F32)
    gains = jnp.concatenate([gain_ref[t] for t in places], axis=1)
    sums = square_sum(values) if sums is None else sums + square_sum(values)
    return dot((values * gains).astype(BF), w_slot, NN), sums


def fetch(w_ref, place, first, count, slot, start, sems):
    return [
        pltpu.make_async_copy(
            w_ref.at[n, pl.ds(place * SHARE + first, count)],
            slot.at[pl.ds(start, count), pl.ds(n * HEADS * HD, HEADS * HD)],
            sems.at[n],
        )
        for n in range(3)
    ]


def project_first(place_ref, p_ref, q_ref, gp_ref, gq_ref, w_ref, acc_ref, sq_ref, wp, wq, sems):
    places_p = [place_ref[k] for k in range(4)]
    places_q = [place_ref[0], place_ref[4]]
    copies = []
    for i, t in enumerate(places_p):
        copies += fetch(w_ref, t, 0, PW, wp, i * PW, sems.at[i])
    for i, t in enumerate(places_q):
        copies += fetch(w_ref, t, PW, QW, wq, i * QW, sems.at[4 + i])
    for c in copies:
        c.start()
    for c in copies[:12]:
        c.wait()
    part, sums = absorb(p_ref[...], gp_ref, places_p, wp[...], None)
    acc_ref[...] = part
    for c in copies[12:]:
        c.wait()
    part, sums = absorb(q_ref[...], gq_ref, places_q, wq[...], sums)
    acc_ref[...] += part
    sq_ref[...] = sums


def split(values):
    high = values.astype(BF)
    return high, (values - high.astype(F32)).astype(BF)


def thirds(values):
    high, low = split(values)
    rest = values - high.astype(F32) - low.astype(F32)
    return high, low, rest.astype(BF)


def attention(
    place_ref, acc0_ref, sq0_ref, p_ref, q1_ref, q2_ref, q3_ref, gp_ref, gq_ref,
    cos_ref, sin_ref, seg_col_ref, seg_row_ref, dctx_ref, w_ref,
    dp_ref, stat_ref, lane_ref, acc, acc0, xp, xq, wp, wq, sems, x_sems,
):
    places_p = [place_ref[4 + k] for k in range(4)]
    places_q = [[place_ref[k], place_ref[4 + k]] for k in range(1, 4)]
    copies_p, copies_q = [], []
    for i, t in enumerate(places_p):
        copies_p += fetch(w_ref, t, 0, PW, wp, i * PW, sems.at[i])
    for g, pair in enumerate(places_q):
        for i, t in enumerate(pair):
            copies_q += fetch(w_ref, t, PW, QW, wq.at[g], i * QW, sems.at[4 + 2 * g + i])
    x_copies = [pltpu.make_async_copy(p_ref, xp, x_sems.at[0])]
    for g, x_ref in enumerate((q1_ref, q2_ref, q3_ref)):
        x_copies.append(pltpu.make_async_copy(x_ref, xq.at[g], x_sems.at[1 + g]))
    x_copies.append(pltpu.make_async_copy(acc0_ref, acc0, x_sems.at[4]))
    for c in x_copies[:1] + copies_p + x_copies[1:4] + copies_q + x_copies[4:]:
        c.start()
    sums = sq0_ref[...]
    for c in x_copies[:1] + copies_p:
        c.wait()
    part, sums = absorb(xp[...], gp_ref, places_p, wp[...], sums)
    acc[...] = part
    for g in range(3):
        for c in x_copies[1 + g : 2 + g] + copies_q[6 * g : 6 * g + 6]:
            c.wait()
        part, sums = absorb(xq[g], gq_ref, places_q[g], wq[g], sums)
        acc[...] += part
    x_copies[4].wait()
    acc[...] += acc0[...]
    mean_square = jnp.sum(sums, axis=1, keepdims=True) * (1.0 / D) + 1e-05
    inverse = lax.rsqrt(mean_square)
    cosines, sines = cos_ref[...], sin_ref[...]
    queries_at = lax.broadcasted_iota(jnp.int32, (TOK, TOK), 0)
    keys_at = lax.broadcasted_iota(jnp.int32, (TOK, TOK), 1)
    allowed = (seg_col_ref[...] == seg_row_ref[...]) & (keys_at <= queries_at)
    scale = HD ** (-0.5)
    row_dot = jnp.zeros((TOK, HD), F32)
    for h in range(HEADS):
        at = [slice(n * HEADS * HD + h * HD, n * HEADS * HD + (h + 1) * HD) for n in range(3)]
        raw = [acc[:, s] * inverse for s in at]
        q, k, v = (r.astype(BF) for r in raw)
        qf, kf = q.astype(F32), k.astype(F32)
        qr = qf * cosines + pltpu.roll(qf, HD // 2, 1) * sines
        kr = kf * cosines + pltpu.roll(kf, HD // 2, 1) * sines
        qh, ql = split(qr)
        kh, kl = split(kr)
        scores = (dot(qh, kh, NT) + (dot(qh, kl, NT) + dot(ql, kh, NT))) * scale
        scores = jnp.where(allowed, scores, -1e30)
        weights = jnp.exp(scores - jnp.max(scores, axis=1, keepdims=True))
        weights = weights / jnp.sum(weights, axis=1, keepdims=True)
        cotangent = dctx_ref[:, h * HD : (h + 1) * HD]
        d_weights = dot(cotangent, v, NT)
        d_scores = weights * (
            d_weights - jnp.sum(weights * d_weights, axis=1, keepdims=True)
        )
        d_scores = (d_scores * scale).astype(BF)
        dv = dot(weights.astype(BF), cotangent, TN)
        dqr = dot(d_scores, kh, NN)
        dkr = dot(d_scores, qh, TN)
        dq = dqr * cosines + pltpu.roll(dqr * sines, HD // 2, 1)
        dk = dkr * cosines + pltpu.roll(dkr * sines, HD // 2, 1)
        for s, r, g in zip(at, raw, (dq, dk, dv)):
            row_dot += r * g
            dp_ref[:, s] = (g * inverse).astype(BF)
    stat_ref[...] = jnp.broadcast_to(inverse * inverse, (TOK, HD))
    ones = jnp.ones((16, HD), BF)
    lane_ref[...] = sum(dot(ones, part, NT) for part in thirds(row_dot * (1.0 / D)))[:8]


def pick(place_ref, quarter_ref, xp_ref, xq_ref, gp_ref, gq_ref, mine_ref, theirs_ref):
    wanted = lax.broadcasted_iota(jnp.int32, (320, SHARE), 0)
    wanted = jnp.where(
        wanted < 160, wanted + 160 * quarter_ref[0], wanted - 160 + 160 * quarter_ref[1]
    )
    unit = lax.broadcasted_iota(jnp.int32, (320, SHARE), 1) == wanted
    unit = jnp.where(unit, 1.0, 0.0).astype(BF)
    for dy in range(2):
        for k in range(4):
            t = place_ref[dy * 4 + k]
            xp = xp_ref[dy, :, k * PW : (k + 1) * PW].astype(F32) * gp_ref[t]
            xq = xq_ref[k, :, dy * QW : (dy + 1) * QW].astype(F32) * gq_ref[t]
            rows = dot(unit[:, :PW], xp.astype(BF), NT) + dot(unit[:, PW:], xq.astype(BF), NT)
            rows = rows.astype(BF)
            mine_ref[t, :, :TOK] = rows[:160]
            mine_ref[t, :, TOK:] = jnp.zeros((160, 64), BF)
            theirs_ref[t, :, :TOK] = rows[160:]
            theirs_ref[t, :, TOK:] = jnp.zeros((160, 64), BF)


def feature_gradient(
    place_ref, source_ref, quarter_ref, dp_ref, lane_ref, ph_ref, pt_ref, q0_ref, q1_ref, q2_ref, q3_ref,
    gp_ref, gq_ref, w_ref, out_ref, gain_ref, mine_ref, theirs_ref,
    ws, xp, xq, result, mine, theirs, sems, x_sems, out_sems,
):
    order = [(k, dy) for k in (1, 3, 2, 0) for dy in (0, 1)]
    copies = []
    for n, (k, dy) in enumerate(order):
        copies.append(fetch(w_ref, place_ref[dy * 4 + k], 0, SHARE, ws.at[n], 0, sems.at[n]))
    x_copies = [
        pltpu.make_async_copy(ref, slot, x_sems.at[i])
        for i, (ref, slot) in enumerate(
            (
                (ph_ref, xp.at[0]), (pt_ref, xp.at[1]), (q0_ref, xq.at[0]),
                (q1_ref, xq.at[1]), (q2_ref, xq.at[2]), (q3_ref, xq.at[3]),
            )
        )
    ]
    for c in copies[0] + x_copies + [c for group in copies[1:] for c in group]:
        c.start()
    gain_ref[:, 2:, :] = jnp.zeros((4, 6, SHARE), F32)
    for column in range(4):
        gain_ref[column, 2:3, :TOK] = lane_ref[0:1]
    dp = dp_ref[...]
    left = []

    def send(source, target, n):
        c = pltpu.make_async_copy(source, target, out_sems.at[n])
        c.start()
        left.append(c)

    for n, (k, dy) in enumerate(order):
        for c in copies[n]:
            c.wait()
        exact = dot(dp, ws[n], NT)
        if n == 0:
            for c in x_copies:
                c.wait()
        back = (4 - k) % 4
        column = place_ref[dy * 4 + k] & 3
        row = pl.ds(place_ref[dy * 4 + k] >> 2, 1)
        x_part = xp[dy, :, back * PW : (back + 1) * PW].astype(F32)
        gain_ref[column, row, :PW] = jnp.sum(exact[:, :PW] * x_part, axis=0, keepdims=True)
        x_part = xq[back, :, dy * QW : (dy + 1) * QW].astype(F32)
        gain_ref[column, row, PW:] = jnp.sum(exact[:, PW:] * x_part, axis=0, keepdims=True)
        result[n] = exact.astype(BF)
        send(result.at[n], out_ref.at[place_ref[dy * 4 + k]], n)
        if n == 3:
            pick(source_ref, quarter_ref, xp, xq, gp_ref, gq_ref, mine, theirs)
            send(theirs, theirs_ref, 8)
            send(mine, mine_ref, 9)
    for c in left:
        c.wait()


def weight_gradient(
    distances, owner_ref, slot_ref, own_ref, core_ref, f0, f1, f2, f3, d0, d1, d2, d3, *rest
):
    out_refs, rest = rest[: len(distances)], rest[len(distances) :]
    near, far, d_near, d_far, result, sems, near_sems, far_sems, out_sems = rest
    d_copies = [
        pltpu.make_async_copy(d0, d_near.at[pl.ds(0, TOK)], sems.at[0]),
        pltpu.make_async_copy(d1, d_near.at[pl.ds(384, TOK)], sems.at[1]),
        pltpu.make_async_copy(d2, d_far.at[pl.ds(0, TOK)], sems.at[2]),
        pltpu.make_async_copy(d3, d_far.at[pl.ds(TOK, TOK)], sems.at[3]),
    ]
    copies = []
    for i, r in enumerate(distances):
        rows = pl.ds(i * 160, 160)
        t = owner_ref[r]
        copies += [
            pltpu.make_async_copy(own_ref.at[t], near.at[rows, pl.ds(0, 384)], near_sems.at[i, 0]),
            pltpu.make_async_copy(core_ref.at[t], near.at[rows, pl.ds(384, 384)], near_sems.at[i, 1]),
        ]
    for k, f in enumerate((f0, f1, f2, f3)):
        for dy in range(2):
            n = dy * 4 + k
            copies.append(
                pltpu.make_async_copy(f.at[:, pl.ds(dy * 640, 640)], far.at[slot_ref[n]], far_sems.at[n])
            )
    for c in d_copies + copies:
        c.start()
    d_near[TOK:384] = jnp.zeros((64, COLS), BF)
    d_near[384 + TOK :] = jnp.zeros((64, COLS), BF)
    for c in d_copies + copies:
        c.wait()
    at, left = 0, []
    while at < len(distances):
        count = min(2, len(distances) - at)
        group = distances[at : at + count]
        x_far = jnp.concatenate([far[r] for r in group], axis=0) if count > 1 else far[group[0]]
        total = dot(near[at * 160 : (at + count) * 160], d_near[...], NN) + dot(x_far, d_far[...], NN)
        for i in range(count):
            result[at + i] = total[i * 160 : (i + 1) * 160].astype(BF)
            c = pltpu.make_async_copy(result.at[at + i], out_refs[at + i], out_sems.at[at + i])
            c.start()
            left.append(c)
        at += count
    for c in left:
        c.wait()


def finish(own_ref, down_ref, up_ref, out_ref):
    total = own_ref[...].astype(F32) + (down_ref[...].astype(F32) + up_ref[...].astype(F32))
    for n in range(3):
        out_ref[n] = total[:, n * HEADS * HD : (n + 1) * HEADS * HD].astype(BF)


VM = pl.BlockSpec(memory_space=pltpu.VMEM)
SM = pl.BlockSpec(memory_space=pltpu.SMEM)
ANY = pl.BlockSpec(memory_space=pl.ANY)
SMALL = pl.CostEstimate(flops=1000, bytes_accessed=1000, transcendentals=0)


def limit(mib):
    return pltpu.CompilerParams(vmem_limit_bytes=mib * 1024 * 1024)


def shift(values, axis, by, size):
    return lax.ppermute(values, axis, [(i, (i + by) % size) for i in range(size)])


def swap(values, axis, bit, size):
    return lax.ppermute(values, axis, [(i, i ^ bit) for i in range(size)])


def body(x_own, gain, w_qkv, segments, d_context):
    yh, core = lax.axis_index("yh"), lax.axis_index("core")
    yl, x_at = lax.axis_index("yl"), lax.axis_index("x")
    ks = jnp.arange(4, dtype=jnp.int32)
    rows = [yl, 1 - yl]
    sources = jnp.concatenate([r * 4 + (x_at - ks) % 4 for r in rows]).astype(jnp.int32)
    targets = jnp.concatenate([r * 4 + (x_at + ks) % 4 for r in rows]).astype(jnp.int32)
    gain_own = lax.dynamic_slice_in_dim(gain, (yl * 4 + x_at) * SHARE, SHARE, 0)

    xp, xq = x_own[:, :PW], x_own[:, PW:]
    got_p = [shift(xp, "x", k, 4) for k in (1, 2, 3)]
    got_q = swap(xq, "yl", 1, 2)
    scaled = (x_own.astype(F32) * gain_own).astype(BF).T.reshape(2, 2, 160, TOK)
    other = lax.dynamic_index_in_dim(scaled, 1 - yh, 0, False)
    straight = lax.dynamic_index_in_dim(other, core, 0, False)
    across = lax.dynamic_index_in_dim(other, 1 - core, 0, False)
    straight, across, got_p, got_q = lax.optimization_barrier((straight, across, got_p, got_q))
    p_here = jnp.concatenate([xp] + got_p, axis=1)
    q_here = jnp.concatenate([xq, got_q], axis=1)
    p_there = swap(p_here, "yl", 1, 2)
    q_there = [shift(q_here, "x", k, 4) for k in (1, 2, 3)]
    straight = swap(straight, "yh", 1, 2)
    across = lax.ppermute(across, ("yh", "core"), [(i, 3 - i) for i in range(4)])
    quarter = jnp.concatenate([straight, across], axis=1)

    weight = w_qkv.transpose(1, 0, 2)
    gains = gain.reshape(8, 1, SHARE)
    gain_p, gain_q = gains[:, :, :PW], gains[:, :, PW:]
    acc, squares = pl.pallas_call(
        project_first,
        out_shape=(
            jax.ShapeDtypeStruct((TOK, COLS), F32),
            jax.ShapeDtypeStruct((TOK, 128), F32),
        ),
        in_specs=[SM, VM, VM, VM, VM, ANY],
        out_specs=(VM, VM),
        scratch_shapes=[
            pltpu.VMEM((4 * PW, COLS), BF),
            pltpu.VMEM((2 * QW, COLS), BF),
            pltpu.SemaphoreType.DMA((6, 3)),
        ],
        compiler_params=limit(63),
        cost_estimate=SMALL,
        name="project_first",
    )(sources, p_here, q_here, gain_p, gain_q, weight)

    acc, quarter = lax.optimization_barrier((acc, quarter))
    quarter_there = swap(quarter, "yl", 1, 2)

    half = HD // 2
    angles = jnp.arange(TOK, dtype=F32)[:, None] * (
        10000.0 ** (-(2.0 * jnp.arange(half, dtype=F32)) / HD)
    )
    cosines, sines = jnp.cos(angles), jnp.sin(angles)
    cosines = jnp.concatenate([cosines, cosines], axis=1)
    sines = jnp.concatenate([-sines, sines], axis=1)
    d_packed, stats, row_dots = pl.pallas_call(
        attention,
        out_shape=(
            jax.ShapeDtypeStruct((TOK, COLS), BF),
            jax.ShapeDtypeStruct((TOK, HD), F32),
            jax.ShapeDtypeStruct((8, TOK), F32),
        ),
        in_specs=[SM, ANY, VM] + [ANY] * 4 + [VM] * 7 + [ANY],
        out_specs=(VM, VM, VM),
        scratch_shapes=[
            pltpu.VMEM((TOK, COLS), F32),
            pltpu.VMEM((TOK, COLS), F32),
            pltpu.VMEM((TOK, 4 * PW), BF),
            pltpu.VMEM((3, TOK, WIDE), BF),
            pltpu.VMEM((4 * PW, COLS), BF),
            pltpu.VMEM((3, 2 * QW, COLS), BF),
            pltpu.SemaphoreType.DMA((10, 3)),
            pltpu.SemaphoreType.DMA((5,)),
        ],
        compiler_params=limit(63),
        cost_estimate=SMALL,
        name="attention",
    )(
        sources, acc, squares, p_there, *q_there, gain_p, gain_q, cosines, sines,
        segments[:, None], segments[None, :], d_context, weight,
    )

    d_packed, quarter, quarter_there = lax.optimization_barrier((d_packed, quarter, quarter_there))
    far = [jnp.concatenate([quarter, quarter_there], axis=1)]
    from_yh = swap(d_packed, "yh", 1, 2)
    from_core = swap(d_packed, "core", 1, 2)
    far = far + [shift(far[0], "x", k, 4) for k in (1, 2, 3)]
    quarters = jnp.stack([yh * 2 + core, yh * 2 + 1 - core]).astype(jnp.int32)
    shares, gains_here, x_mine, x_theirs = pl.pallas_call(
        feature_gradient,
        out_shape=tuple(
            [jax.ShapeDtypeStruct((8, TOK, SHARE), BF)]
            + [jax.ShapeDtypeStruct((4, 8, SHARE), F32)]
            + [jax.ShapeDtypeStruct((8, 160, 384), BF)] * 2
        ),
        in_specs=[SM] * 3 + [VM] * 2 + [ANY] * 6 + [VM] * 2 + [ANY],
        out_specs=(ANY, VM, ANY, ANY),
        scratch_shapes=[
            pltpu.VMEM((8, SHARE, COLS), BF),
            pltpu.VMEM((2, TOK, 4 * PW), BF),
            pltpu.VMEM((4, TOK, WIDE), BF),
            pltpu.VMEM((8, TOK, SHARE), BF),
            pltpu.VMEM((8, 160, 384), BF),
            pltpu.VMEM((8, 160, 384), BF),
            pltpu.SemaphoreType.DMA((8, 3)),
            pltpu.SemaphoreType.DMA((6,)),
            pltpu.SemaphoreType.DMA((10,)),
        ],
        compiler_params=limit(63),
        cost_estimate=SMALL,
        name="feature_gradient",
    )(
        targets, sources, quarters, d_packed, row_dots, p_here, p_there, q_here, *q_there, gain_p, gain_q, weight,
    )
    from_yh, from_core, far, x_theirs, gains_here, shares = lax.optimization_barrier(
        (from_yh, from_core, far, x_theirs, gains_here, shares)
    )
    small = [lax.dynamic_index_in_dim(gains_here, x_at ^ bit, 0, False) for bit in range(4)]
    small = small[:1] + [swap(small[bit], "x", bit, 4) for bit in (1, 2, 3)]
    from_both = swap(from_yh, "core", 1, 2)
    x_core = swap(x_theirs, "core", 1, 2)
    from_both, x_core, small = lax.optimization_barrier((from_both, x_core, small))
    small = (small[0] + small[1]) + (small[2] + small[3])

    z_at = lax.axis_index("z")
    owners = ((z_at + jnp.arange(8)) % 8).astype(jnp.int32)
    slots = ((sources - z_at) % 8).astype(jnp.int32)
    operands = (owners, slots, x_mine, x_core, *far, d_packed, from_core, from_yh, from_both)

    def rows_for(distances, name):
        call = pl.pallas_call(
            functools.partial(weight_gradient, distances),
            out_shape=(jax.ShapeDtypeStruct((160, COLS), BF),) * len(distances),
            in_specs=[SM, SM] + [ANY] * 10,
            out_specs=(ANY,) * len(distances),
            scratch_shapes=[
                pltpu.VMEM((len(distances) * 160, 768), BF),
                pltpu.VMEM((8, 160, 640), BF),
                pltpu.VMEM((768, COLS), BF),
                pltpu.VMEM((640, COLS), BF),
                pltpu.VMEM((len(distances), 160, COLS), BF),
                pltpu.SemaphoreType.DMA((4,)),
                pltpu.SemaphoreType.DMA((len(distances), 2)),
                pltpu.SemaphoreType.DMA((8,)),
                pltpu.SemaphoreType.DMA((len(distances),)),
            ],
            compiler_params=limit(63),
            cost_estimate=SMALL,
            name=name,
        )
        return list(call(*operands))

    def plus(a, b):
        return (a.astype(F32) + b.astype(F32)).astype(BF)

    d_normed = lax.psum_scatter(shares, ("yl", "x"), scatter_dimension=0, tiled=False)
    down = shift(rows_for((4,), "weight_gradient_far")[0], "z", 1, 8)
    rest = rows_for((3, 5, 2, 6, 1, 7, 0), "weight_gradient_rest")
    heard = [swap(small, "yl", 1, 2), swap(small, "yh", 1, 2)]
    heard.append(lax.ppermute(small, ("yh", "yl"), [(i, 3 - i) for i in range(4)]))
    down, heard, rest[-1] = lax.optimization_barrier((down, heard, rest[-1]))
    row_dot = small[2, :TOK] + heard[0][2, :TOK]
    parts = [lax.dynamic_index_in_dim(v, yl, 0, False) for v in (small, *heard)]
    share = (parts[0] + parts[1]) + (parts[2] + parts[3])
    up = rest[1]
    for step, bit in ((0, 1), (1, 2), (2, 4)):
        down = shift(plus(rest[2 * step], down), "z", 1, 8)
        up = shift(plus(rest[2 * step + 1], up) if step else up, "z", -1, 8)
        if step == 0:
            share = share + swap(share, "core", 1, 2)
        there = swap(share, "z", bit, 8)
        down, up, there = lax.optimization_barrier((down, up, there))
        share = share + there
    row_dot = row_dot * stats[:, 0]
    input_gradient = d_normed.astype(F32) * gain_own - x_own.astype(F32) * row_dot[:, None]
    d_weight = pl.pallas_call(
        finish,
        out_shape=jax.ShapeDtypeStruct((3, 160, HEADS * HD), BF),
        in_specs=[VM] * 3,
        out_specs=VM,
        compiler_params=limit(8),
        cost_estimate=SMALL,
        name="finish",
    )(rest[6], down, up)
    return input_gradient.astype(BF), share, d_weight.transpose(1, 0, 2)


def solution(mesh):
    fine = Mesh(mesh.devices.reshape(8, 2, 2, 2, 4), ("z", "yh", "core", "yl", "x"))
    dp, tensor = ("z", "yh", "core"), ("yl", "x")
    in_specs = (P(dp, tensor), P(), P(None, None, tensor), P(dp), P(dp, tensor))
    out_specs = (P(dp, tensor), P(tensor), P(dp, None, tensor))
    return jax.shard_map(
        body, mesh=fine, in_specs=in_specs, out_specs=out_specs, check_vma=False
    )
```

```python
import functools

import jax
import jax.numpy as jnp
from jax import lax
from jax.experimental import pallas as pl
from jax.experimental.pallas import tpu as pltpu
from jax.sharding import Mesh, PartitionSpec as P

HD = 128
HEADS = 3
TOK = 320
D = 5120
COLS = 1152
SHARE = 640
PW = 256
WIDE = 768
QW = 384
BF = jnp.bfloat16
F32 = jnp.float32


def dot(a, b, dims):
    return lax.dot_general(a, b, (dims, ((), ())), preferred_element_type=F32)


NN = ((1,), (0,))
NT = ((1,), (1,))
TN = ((0,), (0,))


def square_sum(values):
    width = values.shape[1]
    squares = values * values
    total = squares[:, :128]
    for start in range(128, width, 128):
        total = total + squares[:, start : start + 128]
    return total


def absorb(x, gain_ref, places, w_slot, sums):
    width = x.shape[1] // len(places)
    values = x.astype(F32)
    gains = jnp.concatenate([gain_ref[t] for t in places], axis=1)
    sums = square_sum(values) if sums is None else sums + square_sum(values)
    return dot((values * gains).astype(BF), w_slot, NN), sums


def fetch(w_ref, place, first, count, slot, start, sems):
    return [
        pltpu.make_async_copy(
            w_ref.at[n, pl.ds(place * SHARE + first, count)],
            slot.at[pl.ds(start, count), pl.ds(n * HEADS * HD, HEADS * HD)],
            sems.at[n],
        )
        for n in range(3)
    ]


def project_first(place_ref, p_ref, q_ref, gp_ref, gq_ref, w_ref, acc_ref, sq_ref, wp, wq, sems):
    places_p = [place_ref[k] for k in range(4)]
    places_q = [place_ref[0], place_ref[4]]
    copies = []
    for i, t in enumerate(places_p):
        copies += fetch(w_ref, t, 0, PW, wp, i * PW, sems.at[i])
    for i, t in enumerate(places_q):
        copies += fetch(w_ref, t, PW, QW, wq, i * QW, sems.at[4 + i])
    for c in copies:
        c.start()
    for c in copies[:12]:
        c.wait()
    part, sums = absorb(p_ref[...], gp_ref, places_p, wp[...], None)
    acc_ref[...] = part
    for c in copies[12:]:
        c.wait()
    part, sums = absorb(q_ref[...], gq_ref, places_q, wq[...], sums)
    acc_ref[...] += part
    sq_ref[...] = sums


def split(values):
    high = values.astype(BF)
    return high, (values - high.astype(F32)).astype(BF)


def thirds(values):
    high, low = split(values)
    rest = values - high.astype(F32) - low.astype(F32)
    return high, low, rest.astype(BF)


def attention(
    place_ref, acc0_ref, sq0_ref, p_ref, q1_ref, q2_ref, q3_ref, gp_ref, gq_ref,
    cos_ref, sin_ref, seg_col_ref, seg_row_ref, dctx_ref, w_ref,
    dp_ref, stat_ref, lane_ref, acc, acc0, xp, xq, wp, wq, sems, x_sems,
):
    places_p = [place_ref[4 + k] for k in range(4)]
    places_q = [[place_ref[k], place_ref[4 + k]] for k in range(1, 4)]
    copies_p, copies_q = [], []
    for i, t in enumerate(places_p):
        copies_p += fetch(w_ref, t, 0, PW, wp, i * PW, sems.at[i])
    for g, pair in enumerate(places_q):
        for i, t in enumerate(pair):
            copies_q += fetch(w_ref, t, PW, QW, wq.at[g], i * QW, sems.at[4 + 2 * g + i])
    x_copies = [pltpu.make_async_copy(p_ref, xp, x_sems.at[0])]
    for g, x_ref in enumerate((q1_ref, q2_ref, q3_ref)):
        x_copies.append(pltpu.make_async_copy(x_ref, xq.at[g], x_sems.at[1 + g]))
    x_copies.append(pltpu.make_async_copy(acc0_ref, acc0, x_sems.at[4]))
    for c in x_copies[:1] + copies_p + x_copies[1:4] + copies_q + x_copies[4:]:
        c.start()
    sums = sq0_ref[...]
    for c in x_copies[:1] + copies_p:
        c.wait()
    part, sums = absorb(xp[...], gp_ref, places_p, wp[...], sums)
    acc[...] = part
    for g in range(3):
        for c in x_copies[1 + g : 2 + g] + copies_q[6 * g : 6 * g + 6]:
            c.wait()
        part, sums = absorb(xq[g], gq_ref, places_q[g], wq[g], sums)
        acc[...] += part
    x_copies[4].wait()
    acc[...] += acc0[...]
    mean_square = jnp.sum(sums, axis=1, keepdims=True) * (1.0 / D) + 1e-05
    inverse = lax.rsqrt(mean_square)
    cosines, sines = cos_ref[...], sin_ref[...]
    queries_at = lax.broadcasted_iota(jnp.int32, (TOK, TOK), 0)
    keys_at = lax.broadcasted_iota(jnp.int32, (TOK, TOK), 1)
    allowed = (seg_col_ref[...] == seg_row_ref[...]) & (keys_at <= queries_at)
    scale = HD ** (-0.5)
    row_dot = jnp.zeros((TOK, HD), F32)
    for h in range(HEADS):
        at = [slice(n * HEADS * HD + h * HD, n * HEADS * HD + (h + 1) * HD) for n in range(3)]
        raw = [acc[:, s] * inverse for s in at]
        q, k, v = (r.astype(BF) for r in raw)
        qf, kf = q.astype(F32), k.astype(F32)
        qr = qf * cosines + pltpu.roll(qf, HD // 2, 1) * sines
        kr = kf * cosines + pltpu.roll(kf, HD // 2, 1) * sines
        qh, ql = split(qr)
        kh, kl = split(kr)
        scores = (dot(qh, kh, NT) + (dot(qh, kl, NT) + dot(ql, kh, NT))) * scale
        scores = jnp.where(allowed, scores, -1e30)
        weights = jnp.exp(scores - jnp.max(scores, axis=1, keepdims=True))
        weights = weights / jnp.sum(weights, axis=1, keepdims=True)
        cotangent = dctx_ref[:, h * HD : (h + 1) * HD]
        d_weights = dot(cotangent, v, NT)
        d_scores = weights * (
            d_weights - jnp.sum(weights * d_weights, axis=1, keepdims=True)
        )
        d_scores = (d_scores * scale).astype(BF)
        dv = dot(weights.astype(BF), cotangent, TN)
        dqr = dot(d_scores, kh, NN)
        dkr = dot(d_scores, qh, TN)
        dq = dqr * cosines + pltpu.roll(dqr * sines, HD // 2, 1)
        dk = dkr * cosines + pltpu.roll(dkr * sines, HD // 2, 1)
        for s, r, g in zip(at, raw, (dq, dk, dv)):
            row_dot += r * g
            dp_ref[:, s] = (g * inverse).astype(BF)
    stat_ref[...] = jnp.broadcast_to(inverse * inverse, (TOK, HD))
    ones = jnp.ones((16, HD), BF)
    lane_ref[...] = sum(dot(ones, part, NT) for part in thirds(row_dot * (1.0 / D)))[:8]


def pick(place_ref, quarter_ref, xp_ref, xq_ref, gp_ref, gq_ref, mine_ref, theirs_ref):
    wanted = lax.broadcasted_iota(jnp.int32, (320, SHARE), 0)
    wanted = jnp.where(
        wanted < 160, wanted + 160 * quarter_ref[0], wanted - 160 + 160 * quarter_ref[1]
    )
    unit = lax.broadcasted_iota(jnp.int32, (320, SHARE), 1) == wanted
    unit = jnp.where(unit, 1.0, 0.0).astype(BF)
    for dy in range(2):
        for k in range(4):
            t = place_ref[dy * 4 + k]
            xp = xp_ref[dy, :, k * PW : (k + 1) * PW].astype(F32) * gp_ref[t]
            xq = xq_ref[k, :, dy * QW : (dy + 1) * QW].astype(F32) * gq_ref[t]
            rows = dot(unit[:, :PW], xp.astype(BF), NT) + dot(unit[:, PW:], xq.astype(BF), NT)
            rows = rows.astype(BF)
            mine_ref[t, :, :TOK] = rows[:160]
            mine_ref[t, :, TOK:] = jnp.zeros((160, 64), BF)
            theirs_ref[t, :, :TOK] = rows[160:]
            theirs_ref[t, :, TOK:] = jnp.zeros((160, 64), BF)


def feature_gradient(
    place_ref, source_ref, quarter_ref, dp_ref, lane_ref, ph_ref, pt_ref, q0_ref, q1_ref, q2_ref, q3_ref,
    gp_ref, gq_ref, w_ref, out_ref, gain_ref, mine_ref, theirs_ref,
    ws, xp, xq, result, mine, theirs, sems, x_sems, out_sems,
):
    order = [(k, dy) for k in (1, 3, 2, 0) for dy in (0, 1)]
    copies = []
    for n, (k, dy) in enumerate(order):
        copies.append(fetch(w_ref, place_ref[dy * 4 + k], 0, SHARE, ws.at[n], 0, sems.at[n]))
    x_copies = [
        pltpu.make_async_copy(ref, slot, x_sems.at[i])
        for i, (ref, slot) in enumerate(
            (
                (ph_ref, xp.at[0]), (pt_ref, xp.at[1]), (q0_ref, xq.at[0]),
                (q1_ref, xq.at[1]), (q2_ref, xq.at[2]), (q3_ref, xq.at[3]),
            )
        )
    ]
    for c in copies[0] + x_copies + [c for group in copies[1:] for c in group]:
        c.start()
    gain_ref[:, 2:, :] = jnp.zeros((4, 6, SHARE), F32)
    for column in range(4):
        gain_ref[column, 2:3, :TOK] = lane_ref[0:1]
    dp = dp_ref[...]
    left = []

    def send(source, target, n):
        c = pltpu.make_async_copy(source, target, out_sems.at[n])
        c.start()
        left.append(c)

    for n, (k, dy) in enumerate(order):
        for c in copies[n]:
            c.wait()
        exact = dot(dp, ws[n], NT)
        if n == 0:
            for c in x_copies:
                c.wait()
        back = (4 - k) % 4
        column = place_ref[dy * 4 + k] & 3
        row = pl.ds(place_ref[dy * 4 + k] >> 2, 1)
        x_part = xp[dy, :, back * PW : (back + 1) * PW].astype(F32)
        gain_ref[column, row, :PW] = jnp.sum(exact[:, :PW] * x_part, axis=0, keepdims=True)
        x_part = xq[back, :, dy * QW : (dy + 1) * QW].astype(F32)
        gain_ref[column, row, PW:] = jnp.sum(exact[:, PW:] * x_part, axis=0, keepdims=True)
        result[n] = exact.astype(BF)
        send(result.at[n], out_ref.at[place_ref[dy * 4 + k]], n)
        if n == 3:
            pick(source_ref, quarter_ref, xp, xq, gp_ref, gq_ref, mine, theirs)
            send(theirs, theirs_ref, 8)
            send(mine, mine_ref, 9)
    for c in left:
        c.wait()


def weight_gradient(
    distances, owner_ref, slot_ref, own_ref, core_ref, f0, f1, f2, f3, d0, d1, d2, d3, *rest
):
    out_refs, rest = rest[: len(distances)], rest[len(distances) :]
    near, far, d_near, d_far, result, sems, near_sems, far_sems, out_sems = rest
    d_copies = [
        pltpu.make_async_copy(d0, d_near.at[pl.ds(0, TOK)], sems.at[0]),
        pltpu.make_async_copy(d1, d_near.at[pl.ds(384, TOK)], sems.at[1]),
        pltpu.make_async_copy(d2, d_far.at[pl.ds(0, TOK)], sems.at[2]),
        pltpu.make_async_copy(d3, d_far.at[pl.ds(TOK, TOK)], sems.at[3]),
    ]
    copies = []
    for i, r in enumerate(distances):
        rows = pl.ds(i * 160, 160)
        t = owner_ref[r]
        copies += [
            pltpu.make_async_copy(own_ref.at[t], near.at[rows, pl.ds(0, 384)], near_sems.at[i, 0]),
            pltpu.make_async_copy(core_ref.at[t], near.at[rows, pl.ds(384, 384)], near_sems.at[i, 1]),
        ]
    for k, f in enumerate((f0, f1, f2, f3)):
        for dy in range(2):
            n = dy * 4 + k
            copies.append(
                pltpu.make_async_copy(f.at[pl.ds(dy * 160, 160)], far.at[slot_ref[n]], far_sems.at[n])
            )
    for c in d_copies + copies:
        c.start()
    d_near[TOK:384] = jnp.zeros((64, COLS), BF)
    d_near[384 + TOK :] = jnp.zeros((64, COLS), BF)
    for c in d_copies + copies:
        c.wait()
    at, left = 0, []
    while at < len(distances):
        count = min(2, len(distances) - at)
        group = distances[at : at + count]
        x_far = jnp.concatenate([far[r] for r in group], axis=0) if count > 1 else far[group[0]]
        total = dot(near[at * 160 : (at + count) * 160], d_near[...], NN) + dot(x_far, d_far[...], NN)
        for i in range(count):
            result[at + i] = total[i * 160 : (i + 1) * 160].astype(BF)
            c = pltpu.make_async_copy(result.at[at + i], out_refs[at + i], out_sems.at[at + i])
            c.start()
            left.append(c)
        at += count
    for c in left:
        c.wait()


def finish(own_ref, down_ref, up_ref, out_ref):
    total = own_ref[...].astype(F32) + (down_ref[...].astype(F32) + up_ref[...].astype(F32))
    for n in range(3):
        out_ref[n] = total[:, n * HEADS * HD : (n + 1) * HEADS * HD].astype(BF)


VM = pl.BlockSpec(memory_space=pltpu.VMEM)
SM = pl.BlockSpec(memory_space=pltpu.SMEM)
ANY = pl.BlockSpec(memory_space=pl.ANY)
SMALL = pl.CostEstimate(flops=1000, bytes_accessed=1000, transcendentals=0)


def limit(mib):
    return pltpu.CompilerParams(vmem_limit_bytes=mib * 1024 * 1024)


def shift(values, axis, by, size):
    return lax.ppermute(values, axis, [(i, (i + by) % size) for i in range(size)])


def swap(values, axis, bit, size):
    return lax.ppermute(values, axis, [(i, i ^ bit) for i in range(size)])


def body(x_own, gain, w_qkv, segments, d_context):
    yh, core = lax.axis_index("yh"), lax.axis_index("core")
    yl, x_at = lax.axis_index("yl"), lax.axis_index("x")
    ks = jnp.arange(4, dtype=jnp.int32)
    rows = [yl, 1 - yl]
    sources = jnp.concatenate([r * 4 + (x_at - ks) % 4 for r in rows]).astype(jnp.int32)
    targets = jnp.concatenate([r * 4 + (x_at + ks) % 4 for r in rows]).astype(jnp.int32)
    gain_own = lax.dynamic_slice_in_dim(gain, (yl * 4 + x_at) * SHARE, SHARE, 0)

    xp, xq = x_own[:, :PW], x_own[:, PW:]
    got_p = [shift(xp, "x", k, 4) for k in (1, 2, 3)]
    got_q = swap(xq, "yl", 1, 2)
    scaled = (x_own.astype(F32) * gain_own).astype(BF).T.reshape(2, 2, 160, TOK)
    other = lax.dynamic_index_in_dim(scaled, 1 - yh, 0, False)
    other = jnp.stack([lax.dynamic_index_in_dim(other, c, 0, False) for c in (core, 1 - core)])
    other, got_p, got_q = lax.optimization_barrier((other, got_p, got_q))
    p_here = jnp.concatenate([xp] + got_p, axis=1)
    q_here = jnp.concatenate([xq, got_q], axis=1)
    p_there = swap(p_here, "yl", 1, 2)
    q_there = [shift(q_here, "x", k, 4) for k in (1, 2, 3)]
    other = swap(other, "yh", 1, 2)

    weight = w_qkv.transpose(1, 0, 2)
    gains = gain.reshape(8, 1, SHARE)
    gain_p, gain_q = gains[:, :, :PW], gains[:, :, PW:]
    acc, squares = pl.pallas_call(
        project_first,
        out_shape=(
            jax.ShapeDtypeStruct((TOK, COLS), F32),
            jax.ShapeDtypeStruct((TOK, 128), F32),
        ),
        in_specs=[SM, VM, VM, VM, VM, ANY],
        out_specs=(VM, VM),
        scratch_shapes=[
            pltpu.VMEM((4 * PW, COLS), BF),
            pltpu.VMEM((2 * QW, COLS), BF),
            pltpu.SemaphoreType.DMA((6, 3)),
        ],
        compiler_params=limit(63),
        cost_estimate=SMALL,
        name="project_first",
    )(sources, p_here, q_here, gain_p, gain_q, weight)

    acc, other = lax.optimization_barrier((acc, other))
    quarter = jnp.concatenate([other[0], swap(other[1], "core", 1, 2)], axis=1)
    acc, quarter = lax.optimization_barrier((acc, quarter))
    quarter_there = swap(quarter, "yl", 1, 2)

    half = HD // 2
    angles = jnp.arange(TOK, dtype=F32)[:, None] * (
        10000.0 ** (-(2.0 * jnp.arange(half, dtype=F32)) / HD)
    )
    cosines, sines = jnp.cos(angles), jnp.sin(angles)
    cosines = jnp.concatenate([cosines, cosines], axis=1)
    sines = jnp.concatenate([-sines, sines], axis=1)
    d_packed, stats, row_dots = pl.pallas_call(
        attention,
        out_shape=(
            jax.ShapeDtypeStruct((TOK, COLS), BF),
            jax.ShapeDtypeStruct((TOK, HD), F32),
            jax.ShapeDtypeStruct((8, TOK), F32),
        ),
        in_specs=[SM, ANY, VM] + [ANY] * 4 + [VM] * 7 + [ANY],
        out_specs=(VM, VM, VM),
        scratch_shapes=[
            pltpu.VMEM((TOK, COLS), F32),
            pltpu.VMEM((TOK, COLS), F32),
            pltpu.VMEM((TOK, 4 * PW), BF),
            pltpu.VMEM((3, TOK, WIDE), BF),
            pltpu.VMEM((4 * PW, COLS), BF),
            pltpu.VMEM((3, 2 * QW, COLS), BF),
            pltpu.SemaphoreType.DMA((10, 3)),
            pltpu.SemaphoreType.DMA((5,)),
        ],
        compiler_params=limit(63),
        cost_estimate=SMALL,
        name="attention",
    )(
        sources, acc, squares, p_there, *q_there, gain_p, gain_q, cosines, sines,
        segments[:, None], segments[None, :], d_context, weight,
    )

    d_packed, quarter, quarter_there = lax.optimization_barrier((d_packed, quarter, quarter_there))
    far = [jnp.concatenate([quarter, quarter_there], axis=0)]
    from_yh = swap(d_packed, "yh", 1, 2)
    from_core = swap(d_packed, "core", 1, 2)
    far = far + [shift(far[0], "x", k, 4) for k in (1, 2, 3)]
    quarters = jnp.stack([yh * 2 + core, yh * 2 + 1 - core]).astype(jnp.int32)
    shares, gains_here, x_mine, x_theirs = pl.pallas_call(
        feature_gradient,
        out_shape=tuple(
            [jax.ShapeDtypeStruct((8, TOK, SHARE), BF)]
            + [jax.ShapeDtypeStruct((4, 8, SHARE), F32)]
            + [jax.ShapeDtypeStruct((8, 160, 384), BF)] * 2
        ),
        in_specs=[SM] * 3 + [VM] * 2 + [ANY] * 6 + [VM] * 2 + [ANY],
        out_specs=(ANY, VM, ANY, ANY),
        scratch_shapes=[
            pltpu.VMEM((8, SHARE, COLS), BF),
            pltpu.VMEM((2, TOK, 4 * PW), BF),
            pltpu.VMEM((4, TOK, WIDE), BF),
            pltpu.VMEM((8, TOK, SHARE), BF),
            pltpu.VMEM((8, 160, 384), BF),
            pltpu.VMEM((8, 160, 384), BF),
            pltpu.SemaphoreType.DMA((8, 3)),
            pltpu.SemaphoreType.DMA((6,)),
            pltpu.SemaphoreType.DMA((10,)),
        ],
        compiler_params=limit(63),
        cost_estimate=SMALL,
        name="feature_gradient",
    )(
        targets, sources, quarters, d_packed, row_dots, p_here, p_there, q_here, *q_there, gain_p, gain_q, weight,
    )
    from_yh, from_core, far, x_theirs, gains_here = lax.optimization_barrier(
        (from_yh, from_core, far, x_theirs, gains_here)
    )
    small = [lax.dynamic_index_in_dim(gains_here, x_at ^ bit, 0, False) for bit in range(4)]
    small = small[:1] + [swap(small[bit], "x", bit, 4) for bit in (1, 2, 3)]
    from_both = swap(from_yh, "core", 1, 2)
    x_core = swap(x_theirs, "core", 1, 2)
    from_both, x_core, small = lax.optimization_barrier((from_both, x_core, small))
    small = (small[0] + small[1]) + (small[2] + small[3])

    z_at = lax.axis_index("z")
    owners = ((z_at + jnp.arange(8)) % 8).astype(jnp.int32)
    slots = ((sources - z_at) % 8).astype(jnp.int32)
    operands = (owners, slots, x_mine, x_core, *far, d_packed, from_core, from_yh, from_both)

    def rows_for(distances, name):
        call = pl.pallas_call(
            functools.partial(weight_gradient, distances),
            out_shape=(jax.ShapeDtypeStruct((160, COLS), BF),) * len(distances),
            in_specs=[SM, SM] + [ANY] * 10,
            out_specs=(ANY,) * len(distances),
            scratch_shapes=[
                pltpu.VMEM((len(distances) * 160, 768), BF),
                pltpu.VMEM((8, 160, 640), BF),
                pltpu.VMEM((768, COLS), BF),
                pltpu.VMEM((640, COLS), BF),
                pltpu.VMEM((len(distances), 160, COLS), BF),
                pltpu.SemaphoreType.DMA((4,)),
                pltpu.SemaphoreType.DMA((len(distances), 2)),
                pltpu.SemaphoreType.DMA((8,)),
                pltpu.SemaphoreType.DMA((len(distances),)),
            ],
            compiler_params=limit(63),
            cost_estimate=SMALL,
            name=name,
        )
        return list(call(*operands))

    def plus(a, b):
        return (a.astype(F32) + b.astype(F32)).astype(BF)

    heard = [swap(small, "yl", 1, 2), swap(small, "yh", 1, 2)]
    heard.append(lax.ppermute(small, ("yh", "yl"), [(i, 3 - i) for i in range(4)]))
    far_rows = rows_for((4,), "weight_gradient_far")[0]
    far_rows, heard, shares = lax.optimization_barrier((far_rows, heard, shares))
    row_dot = small[2, :TOK] + heard[0][2, :TOK]
    parts = [lax.dynamic_index_in_dim(v, yl, 0, False) for v in (small, *heard)]
    share = (parts[0] + parts[1]) + (parts[2] + parts[3])
    d_normed = lax.psum_scatter(shares, ("yl", "x"), scatter_dimension=0, tiled=False)
    down = shift(far_rows, "z", 1, 8)
    there = swap(share, "z", 1, 8)
    rest = rows_for((3, 5), "weight_gradient_middle")
    down, there, rest[0] = lax.optimization_barrier((down, there, rest[0]))
    share = share + there
    up = rest[1]
    for step, bit in ((0, 2), (1, 4), (2, None)):
        down = shift(plus(rest[2 * step], down), "z", 1, 8)
        up = shift(plus(rest[2 * step + 1], up) if step else up, "z", -1, 8)
        if step == 0:
            rest += rows_for((2, 6, 1, 7, 0), "weight_gradient_near")
        there = swap(share, "core", 1, 2) if bit is None else swap(share, "z", bit, 8)
        down, up, there, rest[2] = lax.optimization_barrier((down, up, there, rest[2]))
        share = share + there
    row_dot = row_dot * stats[:, 0]
    input_gradient = d_normed.astype(F32) * gain_own - x_own.astype(F32) * row_dot[:, None]
    d_weight = pl.pallas_call(
        finish,
        out_shape=jax.ShapeDtypeStruct((3, 160, HEADS * HD), BF),
        in_specs=[VM] * 3,
        out_specs=VM,
        compiler_params=limit(8),
        cost_estimate=SMALL,
        name="finish",
    )(rest[6], down, up)
    return input_gradient.astype(BF), share, d_weight.transpose(1, 0, 2)


def solution(mesh):
    fine = Mesh(mesh.devices.reshape(8, 2, 2, 2, 4), ("z", "yh", "core", "yl", "x"))
    dp, tensor = ("z", "yh", "core"), ("yl", "x")
    in_specs = (P(dp, tensor), P(), P(None, None, tensor), P(dp), P(dp, tensor))
    out_specs = (P(dp, tensor), P(tensor), P(dp, None, tensor))
    return jax.shard_map(
        body, mesh=fine, in_specs=in_specs, out_specs=out_specs, check_vma=False
    )
```

```python
import functools

import jax
import jax.numpy as jnp
from jax import lax
from jax.experimental import pallas as pl
from jax.experimental.pallas import tpu as pltpu
from jax.sharding import Mesh, PartitionSpec as P

HD = 128
HEADS = 3
TOK = 320
D = 5120
COLS = 1152
SHARE = 640
PW = 256
WIDE = 768
QW = 384
BF = jnp.bfloat16
F32 = jnp.float32


def dot(a, b, dims):
    return lax.dot_general(a, b, (dims, ((), ())), preferred_element_type=F32)


NN = ((1,), (0,))
NT = ((1,), (1,))
TN = ((0,), (0,))


def square_sum(values):
    width = values.shape[1]
    squares = values * values
    total = squares[:, :128]
    for start in range(128, width, 128):
        total = total + squares[:, start : start + 128]
    return total


def absorb(x, gain_ref, places, w_slot, sums):
    width = x.shape[1] // len(places)
    values = x.astype(F32)
    gains = jnp.concatenate([gain_ref[t] for t in places], axis=1)
    sums = square_sum(values) if sums is None else sums + square_sum(values)
    return dot((values * gains).astype(BF), w_slot, NN), sums


def fetch(w_ref, place, first, count, slot, start, sems):
    return [
        pltpu.make_async_copy(
            w_ref.at[n, pl.ds(place * SHARE + first, count)],
            slot.at[pl.ds(start, count), pl.ds(n * HEADS * HD, HEADS * HD)],
            sems.at[n],
        )
        for n in range(3)
    ]


def project_first(place_ref, p_ref, q_ref, gp_ref, gq_ref, w_ref, acc_ref, sq_ref, wp, wq, sems):
    places_p = [place_ref[k] for k in range(4)]
    places_q = [place_ref[0], place_ref[4]]
    copies = []
    for i, t in enumerate(places_p):
        copies += fetch(w_ref, t, 0, PW, wp, i * PW, sems.at[i])
    for i, t in enumerate(places_q):
        copies += fetch(w_ref, t, PW, QW, wq, i * QW, sems.at[4 + i])
    for c in copies:
        c.start()
    for c in copies[:12]:
        c.wait()
    part, sums = absorb(p_ref[...], gp_ref, places_p, wp[...], None)
    acc_ref[...] = part
    for c in copies[12:]:
        c.wait()
    part, sums = absorb(q_ref[...], gq_ref, places_q, wq[...], sums)
    acc_ref[...] += part
    sq_ref[...] = sums


def split(values):
    high = values.astype(BF)
    return high, (values - high.astype(F32)).astype(BF)


def thirds(values):
    high, low = split(values)
    rest = values - high.astype(F32) - low.astype(F32)
    return high, low, rest.astype(BF)


def attention(
    place_ref, acc0_ref, sq0_ref, p_ref, q1_ref, q2_ref, q3_ref, gp_ref, gq_ref,
    cos_ref, sin_ref, seg_col_ref, seg_row_ref, dctx_ref, w_ref,
    dp_ref, stat_ref, lane_ref, acc, acc0, xp, xq, wp, wq, sems, x_sems,
):
    places_p = [place_ref[4 + k] for k in range(4)]
    places_q = [[place_ref[k], place_ref[4 + k]] for k in range(1, 4)]
    copies_p, copies_q = [], []
    for i, t in enumerate(places_p):
        copies_p += fetch(w_ref, t, 0, PW, wp, i * PW, sems.at[i])
    for g, pair in enumerate(places_q):
        for i, t in enumerate(pair):
            copies_q += fetch(w_ref, t, PW, QW, wq.at[g], i * QW, sems.at[4 + 2 * g + i])
    x_copies = [pltpu.make_async_copy(p_ref, xp, x_sems.at[0])]
    for g, x_ref in enumerate((q1_ref, q2_ref, q3_ref)):
        x_copies.append(pltpu.make_async_copy(x_ref, xq.at[g], x_sems.at[1 + g]))
    x_copies.append(pltpu.make_async_copy(acc0_ref, acc0, x_sems.at[4]))
    for c in x_copies[:1] + copies_p + x_copies[1:4] + copies_q + x_copies[4:]:
        c.start()
    sums = sq0_ref[...]
    for c in x_copies[:1] + copies_p:
        c.wait()
    part, sums = absorb(xp[...], gp_ref, places_p, wp[...], sums)
    acc[...] = part
    for g in range(3):
        for c in x_copies[1 + g : 2 + g] + copies_q[6 * g : 6 * g + 6]:
            c.wait()
        part, sums = absorb(xq[g], gq_ref, places_q[g], wq[g], sums)
        acc[...] += part
    x_copies[4].wait()
    acc[...] += acc0[...]
    mean_square = jnp.sum(sums, axis=1, keepdims=True) * (1.0 / D) + 1e-05
    inverse = lax.rsqrt(mean_square)
    cosines, sines = cos_ref[...], sin_ref[...]
    queries_at = lax.broadcasted_iota(jnp.int32, (TOK, TOK), 0)
    keys_at = lax.broadcasted_iota(jnp.int32, (TOK, TOK), 1)
    allowed = (seg_col_ref[...] == seg_row_ref[...]) & (keys_at <= queries_at)
    scale = HD ** (-0.5)
    row_dot = jnp.zeros((TOK, HD), F32)
    for h in range(HEADS):
        at = [slice(n * HEADS * HD + h * HD, n * HEADS * HD + (h + 1) * HD) for n in range(3)]
        raw = [acc[:, s] * inverse for s in at]
        q, k, v = (r.astype(BF) for r in raw)
        qf, kf = q.astype(F32), k.astype(F32)
        qr = qf * cosines + pltpu.roll(qf, HD // 2, 1) * sines
        kr = kf * cosines + pltpu.roll(kf, HD // 2, 1) * sines
        qh, ql = split(qr)
        kh, kl = split(kr)
        scores = (dot(qh, kh, NT) + (dot(qh, kl, NT) + dot(ql, kh, NT))) * scale
        scores = jnp.where(allowed, scores, -1e30)
        weights = jnp.exp(scores - jnp.max(scores, axis=1, keepdims=True))
        weights = weights / jnp.sum(weights, axis=1, keepdims=True)
        cotangent = dctx_ref[:, h * HD : (h + 1) * HD]
        d_weights = dot(cotangent, v, NT)
        d_scores = weights * (
            d_weights - jnp.sum(weights * d_weights, axis=1, keepdims=True)
        )
        d_scores = (d_scores * scale).astype(BF)
        dv = dot(weights.astype(BF), cotangent, TN)
        dqr = dot(d_scores, kh, NN)
        dkr = dot(d_scores, qh, TN)
        dq = dqr * cosines + pltpu.roll(dqr * sines, HD // 2, 1)
        dk = dkr * cosines + pltpu.roll(dkr * sines, HD // 2, 1)
        for s, r, g in zip(at, raw, (dq, dk, dv)):
            row_dot += r * g
            dp_ref[:, s] = (g * inverse).astype(BF)
    stat_ref[...] = jnp.broadcast_to(inverse * inverse, (TOK, HD))
    ones = jnp.ones((16, HD), BF)
    lane_ref[...] = sum(dot(ones, part, NT) for part in thirds(row_dot * (1.0 / D)))[:8]


def pick(place_ref, quarter_ref, xp_ref, xq_ref, gp_ref, gq_ref, mine_ref, theirs_ref):
    wanted = lax.broadcasted_iota(jnp.int32, (320, SHARE), 0)
    wanted = jnp.where(
        wanted < 160, wanted + 160 * quarter_ref[0], wanted - 160 + 160 * quarter_ref[1]
    )
    unit = lax.broadcasted_iota(jnp.int32, (320, SHARE), 1) == wanted
    unit = jnp.where(unit, 1.0, 0.0).astype(BF)
    for dy in range(2):
        for k in range(4):
            t = place_ref[dy * 4 + k]
            xp = xp_ref[dy, :, k * PW : (k + 1) * PW].astype(F32) * gp_ref[t]
            xq = xq_ref[k, :, dy * QW : (dy + 1) * QW].astype(F32) * gq_ref[t]
            rows = dot(unit[:, :PW], xp.astype(BF), NT) + dot(unit[:, PW:], xq.astype(BF), NT)
            rows = rows.astype(BF)
            mine_ref[t, :, :TOK] = rows[:160]
            mine_ref[t, :, TOK:] = jnp.zeros((160, 64), BF)
            theirs_ref[t, :, :TOK] = rows[160:]
            theirs_ref[t, :, TOK:] = jnp.zeros((160, 64), BF)


def feature_gradient(
    place_ref, source_ref, quarter_ref, dp_ref, ph_ref, pt_ref, q0_ref, q1_ref, q2_ref, q3_ref,
    gp_ref, gq_ref, w_ref, out_ref, gain_ref, mine_ref, theirs_ref,
    ws, xp, xq, result, mine, theirs, sems, x_sems, out_sems,
):
    order = [(k, dy) for k in (1, 3, 2, 0) for dy in (0, 1)]
    copies = []
    for n, (k, dy) in enumerate(order):
        copies.append(fetch(w_ref, place_ref[dy * 4 + k], 0, SHARE, ws.at[n], 0, sems.at[n]))
    x_copies = [
        pltpu.make_async_copy(ref, slot, x_sems.at[i])
        for i, (ref, slot) in enumerate(
            (
                (ph_ref, xp.at[0]), (pt_ref, xp.at[1]), (q0_ref, xq.at[0]),
                (q1_ref, xq.at[1]), (q2_ref, xq.at[2]), (q3_ref, xq.at[3]),
            )
        )
    ]
    for c in copies[0] + x_copies + [c for group in copies[1:] for c in group]:
        c.start()
    dp = dp_ref[...]
    left = []

    def send(source, target, n):
        c = pltpu.make_async_copy(source, target, out_sems.at[n])
        c.start()
        left.append(c)

    for n, (k, dy) in enumerate(order):
        for c in copies[n]:
            c.wait()
        exact = dot(dp, ws[n], NT)
        if n == 0:
            for c in x_copies:
                c.wait()
        back = (4 - k) % 4
        row = pl.ds(place_ref[dy * 4 + k], 1)
        x_part = xp[dy, :, back * PW : (back + 1) * PW].astype(F32)
        gain_ref[row, :PW] = jnp.sum(exact[:, :PW] * x_part, axis=0, keepdims=True)
        x_part = xq[back, :, dy * QW : (dy + 1) * QW].astype(F32)
        gain_ref[row, PW:] = jnp.sum(exact[:, PW:] * x_part, axis=0, keepdims=True)
        result[n] = exact.astype(BF)
        send(result.at[n], out_ref.at[place_ref[dy * 4 + k]], n)
        if n == 3:
            pick(source_ref, quarter_ref, xp, xq, gp_ref, gq_ref, mine, theirs)
            send(theirs, theirs_ref, 8)
            send(mine, mine_ref, 9)
    for c in left:
        c.wait()


def weight_gradient(
    distances, owner_ref, slot_ref, own_ref, core_ref, f0, f1, f2, f3, d0, d1, d2, d3, *rest
):
    out_refs, rest = rest[: len(distances)], rest[len(distances) :]
    near, far, d_near, d_far, result, sems, near_sems, far_sems, out_sems = rest
    d_copies = [
        pltpu.make_async_copy(d0, d_near.at[pl.ds(0, TOK)], sems.at[0]),
        pltpu.make_async_copy(d1, d_near.at[pl.ds(384, TOK)], sems.at[1]),
        pltpu.make_async_copy(d2, d_far.at[pl.ds(0, TOK)], sems.at[2]),
        pltpu.make_async_copy(d3, d_far.at[pl.ds(TOK, TOK)], sems.at[3]),
    ]
    copies = []
    for i, r in enumerate(distances):
        rows = pl.ds(i * 160, 160)
        t = owner_ref[r]
        copies += [
            pltpu.make_async_copy(own_ref.at[t], near.at[rows, pl.ds(0, 384)], near_sems.at[i, 0]),
            pltpu.make_async_copy(core_ref.at[t], near.at[rows, pl.ds(384, 384)], near_sems.at[i, 1]),
        ]
    wanted = []
    for k, f in enumerate((f0, f1, f2, f3)):
        for dy in range(2):
            n = dy * 4 + k
            hit = slot_ref[n] == distances[0]
            for r in distances[1:]:
                hit = hit | (slot_ref[n] == r)
            c = pltpu.make_async_copy(f.at[pl.ds(dy * 160, 160)], far.at[slot_ref[n]], far_sems.at[n])
            wanted.append((hit, c))
    for c in d_copies + copies:
        c.start()
    for hit, c in wanted:
        pl.when(hit)(c.start)
    d_near[TOK:384] = jnp.zeros((64, COLS), BF)
    d_near[384 + TOK :] = jnp.zeros((64, COLS), BF)
    for c in d_copies + copies:
        c.wait()
    for hit, c in wanted:
        pl.when(hit)(c.wait)
    at, left = 0, []
    while at < len(distances):
        count = min(2, len(distances) - at)
        group = distances[at : at + count]
        x_far = jnp.concatenate([far[r] for r in group], axis=0) if count > 1 else far[group[0]]
        total = dot(near[at * 160 : (at + count) * 160], d_near[...], NN) + dot(x_far, d_far[...], NN)
        for i in range(count):
            result[at + i] = total[i * 160 : (i + 1) * 160].astype(BF)
            c = pltpu.make_async_copy(result.at[at + i], out_refs[at + i], out_sems.at[at + i])
            c.start()
            left.append(c)
        at += count
    for c in left:
        c.wait()


def finish(own_ref, down_ref, up_ref, out_ref):
    total = own_ref[...].astype(F32) + (down_ref[...].astype(F32) + up_ref[...].astype(F32))
    for n in range(3):
        out_ref[n] = total[:, n * HEADS * HD : (n + 1) * HEADS * HD].astype(BF)


VM = pl.BlockSpec(memory_space=pltpu.VMEM)
SM = pl.BlockSpec(memory_space=pltpu.SMEM)
ANY = pl.BlockSpec(memory_space=pl.ANY)
SMALL = pl.CostEstimate(flops=1000, bytes_accessed=1000, transcendentals=0)


def limit(mib):
    return pltpu.CompilerParams(vmem_limit_bytes=mib * 1024 * 1024)


def shift(values, axis, by, size):
    return lax.ppermute(values, axis, [(i, (i + by) % size) for i in range(size)])


def swap(values, axis, bit, size):
    return lax.ppermute(values, axis, [(i, i ^ bit) for i in range(size)])


def body(x_own, gain, w_qkv, segments, d_context):
    yh, core = lax.axis_index("yh"), lax.axis_index("core")
    yl, x_at = lax.axis_index("yl"), lax.axis_index("x")
    ks = jnp.arange(4, dtype=jnp.int32)
    rows = [yl, 1 - yl]
    sources = jnp.concatenate([r * 4 + (x_at - ks) % 4 for r in rows]).astype(jnp.int32)
    targets = jnp.concatenate([r * 4 + (x_at + ks) % 4 for r in rows]).astype(jnp.int32)
    gain_own = lax.dynamic_slice_in_dim(gain, (yl * 4 + x_at) * SHARE, SHARE, 0)

    xp, xq = x_own[:, :PW], x_own[:, PW:]
    got_p = [shift(xp, "x", k, 4) for k in (1, 2, 3)]
    got_q = swap(xq, "yl", 1, 2)
    scaled = (x_own.astype(F32) * gain_own).astype(BF).T.reshape(2, 2, 160, TOK)
    other = lax.dynamic_index_in_dim(scaled, 1 - yh, 0, False)
    other = jnp.stack([lax.dynamic_index_in_dim(other, c, 0, False) for c in (core, 1 - core)])
    other, got_p, got_q = lax.optimization_barrier((other, got_p, got_q))
    p_here = jnp.concatenate([xp] + got_p, axis=1)
    q_here = jnp.concatenate([xq, got_q], axis=1)
    p_there = swap(p_here, "yl", 1, 2)
    q_there = [shift(q_here, "x", k, 4) for k in (1, 2, 3)]
    other = swap(other, "yh", 1, 2)

    weight = w_qkv.transpose(1, 0, 2)
    gains = gain.reshape(8, 1, SHARE)
    gain_p, gain_q = gains[:, :, :PW], gains[:, :, PW:]
    acc, squares = pl.pallas_call(
        project_first,
        out_shape=(
            jax.ShapeDtypeStruct((TOK, COLS), F32),
            jax.ShapeDtypeStruct((TOK, 128), F32),
        ),
        in_specs=[SM, VM, VM, VM, VM, ANY],
        out_specs=(VM, VM),
        scratch_shapes=[
            pltpu.VMEM((4 * PW, COLS), BF),
            pltpu.VMEM((2 * QW, COLS), BF),
            pltpu.SemaphoreType.DMA((6, 3)),
        ],
        compiler_params=limit(63),
        cost_estimate=SMALL,
        name="project_first",
    )(sources, p_here, q_here, gain_p, gain_q, weight)

    acc, other = lax.optimization_barrier((acc, other))
    quarter = jnp.concatenate([other[0], swap(other[1], "core", 1, 2)], axis=1)
    acc, quarter = lax.optimization_barrier((acc, quarter))
    quarter_there = swap(quarter, "yl", 1, 2)

    half = HD // 2
    angles = jnp.arange(TOK, dtype=F32)[:, None] * (
        10000.0 ** (-(2.0 * jnp.arange(half, dtype=F32)) / HD)
    )
    cosines, sines = jnp.cos(angles), jnp.sin(angles)
    cosines = jnp.concatenate([cosines, cosines], axis=1)
    sines = jnp.concatenate([-sines, sines], axis=1)
    d_packed, stats, row_dots = pl.pallas_call(
        attention,
        out_shape=(
            jax.ShapeDtypeStruct((TOK, COLS), BF),
            jax.ShapeDtypeStruct((TOK, HD), F32),
            jax.ShapeDtypeStruct((8, TOK), F32),
        ),
        in_specs=[SM, ANY, VM] + [ANY] * 4 + [VM] * 7 + [ANY],
        out_specs=(VM, VM, VM),
        scratch_shapes=[
            pltpu.VMEM((TOK, COLS), F32),
            pltpu.VMEM((TOK, COLS), F32),
            pltpu.VMEM((TOK, 4 * PW), BF),
            pltpu.VMEM((3, TOK, WIDE), BF),
            pltpu.VMEM((4 * PW, COLS), BF),
            pltpu.VMEM((3, 2 * QW, COLS), BF),
            pltpu.SemaphoreType.DMA((10, 3)),
            pltpu.SemaphoreType.DMA((5,)),
        ],
        compiler_params=limit(63),
        cost_estimate=SMALL,
        name="attention",
    )(
        sources, acc, squares, p_there, *q_there, gain_p, gain_q, cosines, sines,
        segments[:, None], segments[None, :], d_context, weight,
    )

    d_packed, quarter, quarter_there = lax.optimization_barrier((d_packed, quarter, quarter_there))
    far = [jnp.concatenate([quarter, quarter_there], axis=0)]
    from_yh = swap(d_packed, "yh", 1, 2)
    from_core = swap(d_packed, "core", 1, 2)
    far = far + [shift(far[0], "x", k, 4) for k in (1, 2, 3)]
    quarters = jnp.stack([yh * 2 + core, yh * 2 + 1 - core]).astype(jnp.int32)
    shares, gains_here, x_mine, x_theirs = pl.pallas_call(
        feature_gradient,
        out_shape=tuple(
            [jax.ShapeDtypeStruct((8, TOK, SHARE), BF)]
            + [jax.ShapeDtypeStruct((8, SHARE), F32)]
            + [jax.ShapeDtypeStruct((8, 160, 384), BF)] * 2
        ),
        in_specs=[SM] * 3 + [VM] + [ANY] * 6 + [VM] * 2 + [ANY],
        out_specs=(ANY, VM, ANY, ANY),
        scratch_shapes=[
            pltpu.VMEM((8, SHARE, COLS), BF),
            pltpu.VMEM((2, TOK, 4 * PW), BF),
            pltpu.VMEM((4, TOK, WIDE), BF),
            pltpu.VMEM((8, TOK, SHARE), BF),
            pltpu.VMEM((8, 160, 384), BF),
            pltpu.VMEM((8, 160, 384), BF),
            pltpu.SemaphoreType.DMA((8, 3)),
            pltpu.SemaphoreType.DMA((6,)),
            pltpu.SemaphoreType.DMA((10,)),
        ],
        compiler_params=limit(63),
        cost_estimate=SMALL,
        name="feature_gradient",
    )(
        targets, sources, quarters, d_packed, p_here, p_there, q_here, *q_there, gain_p, gain_q, weight,
    )
    from_yh, from_core, far, x_theirs, gains, shares = lax.optimization_barrier(
        (from_yh, from_core, far, x_theirs, gains_here, shares)
    )
    d_normed = lax.psum_scatter(shares, ("yl", "x"), scatter_dimension=0, tiled=False)
    from_both = swap(from_yh, "core", 1, 2)
    x_core = swap(x_theirs, "core", 1, 2)
    from_both, x_core, gains = lax.optimization_barrier((from_both, x_core, gains))

    z_at = lax.axis_index("z")
    owners = ((z_at + jnp.arange(8)) % 8).astype(jnp.int32)
    slots = ((sources - z_at) % 8).astype(jnp.int32)
    operands = (owners, slots, x_mine, x_core, *far, d_packed, from_core, from_yh, from_both)

    def rows_for(distances, name):
        call = pl.pallas_call(
            functools.partial(weight_gradient, distances),
            out_shape=(jax.ShapeDtypeStruct((160, COLS), BF),) * len(distances),
            in_specs=[SM, SM] + [ANY] * 10,
            out_specs=(ANY,) * len(distances),
            scratch_shapes=[
                pltpu.VMEM((len(distances) * 160, 768), BF),
                pltpu.VMEM((8, 160, 640), BF),
                pltpu.VMEM((768, COLS), BF),
                pltpu.VMEM((640, COLS), BF),
                pltpu.VMEM((len(distances), 160, COLS), BF),
                pltpu.SemaphoreType.DMA((4,)),
                pltpu.SemaphoreType.DMA((len(distances), 2)),
                pltpu.SemaphoreType.DMA((8,)),
                pltpu.SemaphoreType.DMA((len(distances),)),
            ],
            compiler_params=limit(32),
            cost_estimate=SMALL,
            name=name,
        )
        return list(call(*operands))

    def plus(a, b):
        return (a.astype(F32) + b.astype(F32)).astype(BF)

    there = swap(gains, "z", 1, 8)
    far_rows = rows_for((4,), "weight_gradient_far")[0]
    far_rows, there = lax.optimization_barrier((far_rows, there))
    gains = gains + there
    down = shift(far_rows, "z", 1, 8)
    there = swap(gains, "z", 2, 8)
    rest = rows_for((3, 5), "weight_gradient_middle")
    down, there, rest[0] = lax.optimization_barrier((down, there, rest[0]))
    gains = gains + there
    down = shift(plus(rest[0], down), "z", 1, 8)
    up = shift(rest[1], "z", -1, 8)
    there = swap(gains, "z", 4, 8)
    rest += rows_for((2, 6, 1, 7, 0), "weight_gradient_near")
    down, up, there, rest[2] = lax.optimization_barrier((down, up, there, rest[2]))
    gains = (gains + there).reshape(2, 4, SHARE)
    down = shift(plus(rest[2], down), "z", 1, 8)
    up = shift(plus(rest[3], up), "z", -1, 8)
    row_dots = jnp.pad(row_dots[:1], ((0, 0), (0, SHARE - TOK)))
    empty = jnp.zeros((5, SHARE), F32)
    small = [
        jnp.concatenate([lax.dynamic_index_in_dim(gains, x_at ^ bit, 1, False), row_dots, empty])
        for bit in range(4)
    ]
    small = small[:1] + [swap(small[bit], "x", bit, 4) for bit in (1, 2, 3)]
    down, up, small = lax.optimization_barrier((down, up, small))
    small = (small[0] + small[1]) + (small[2] + small[3])
    down = shift(plus(rest[4], down), "z", 1, 8)
    up = shift(plus(rest[5], up), "z", -1, 8)
    heard = [swap(small, "yl", 1, 2), swap(small, "yh", 1, 2)]
    heard.append(lax.ppermute(small, ("yh", "yl"), [(i, 3 - i) for i in range(4)]))
    row_dot = small[2, :TOK] + heard[0][2, :TOK]
    parts = [lax.dynamic_index_in_dim(v, yl, 0, False) for v in (small, *heard)]
    share = (parts[0] + parts[1]) + (parts[2] + parts[3])
    share = share + swap(share, "core", 1, 2)
    down, up, share = lax.optimization_barrier((down, up, share))
    row_dot = row_dot * stats[:, 0]
    input_gradient = d_normed.astype(F32) * gain_own - x_own.astype(F32) * row_dot[:, None]
    d_weight = pl.pallas_call(
        finish,
        out_shape=jax.ShapeDtypeStruct((3, 160, HEADS * HD), BF),
        in_specs=[VM] * 3,
        out_specs=VM,
        compiler_params=limit(8),
        cost_estimate=SMALL,
        name="finish",
    )(rest[6], down, up)
    return input_gradient.astype(BF), share, d_weight.transpose(1, 0, 2)


def solution(mesh):
    fine = Mesh(mesh.devices.reshape(8, 2, 2, 2, 4), ("z", "yh", "core", "yl", "x"))
    dp, tensor = ("z", "yh", "core"), ("yl", "x")
    in_specs = (P(dp, tensor), P(), P(None, None, tensor), P(dp), P(dp, tensor))
    out_specs = (P(dp, tensor), P(tensor), P(dp, None, tensor))
    return jax.shard_map(
        body, mesh=fine, in_specs=in_specs, out_specs=out_specs, check_vma=False
    )
```

```python
import functools

import jax
import jax.numpy as jnp
from jax import lax
from jax.experimental import pallas as pl
from jax.experimental.pallas import tpu as pltpu
from jax.sharding import Mesh, PartitionSpec as P

HD = 128
HEADS = 3
TOK = 320
D = 5120
COLS = 1152
SHARE = 640
PW = 256
WIDE = 768
QW = 384
BF = jnp.bfloat16
F32 = jnp.float32


def dot(a, b, dims):
    return lax.dot_general(a, b, (dims, ((), ())), preferred_element_type=F32)


NN = ((1,), (0,))
NT = ((1,), (1,))
TN = ((0,), (0,))


def square_sum(values):
    width = values.shape[1]
    squares = values * values
    total = squares[:, :128]
    for start in range(128, width, 128):
        total = total + squares[:, start : start + 128]
    return total


def absorb(x, gain_ref, places, w_slot, sums):
    width = x.shape[1] // len(places)
    values = x.astype(F32)
    gains = jnp.concatenate([gain_ref[t] for t in places], axis=1)
    sums = square_sum(values) if sums is None else sums + square_sum(values)
    return dot((values * gains).astype(BF), w_slot, NN), sums


def fetch(w_ref, place, first, count, slot, start, sems):
    return [
        pltpu.make_async_copy(
            w_ref.at[n, pl.ds(place * SHARE + first, count)],
            slot.at[pl.ds(start, count), pl.ds(n * HEADS * HD, HEADS * HD)],
            sems.at[n],
        )
        for n in range(3)
    ]


def project_first(place_ref, p_ref, q_ref, gp_ref, gq_ref, w_ref, acc_ref, sq_ref, wp, wq, sems):
    places_p = [place_ref[k] for k in range(4)]
    places_q = [place_ref[0], place_ref[4]]
    copies = []
    for i, t in enumerate(places_p):
        copies += fetch(w_ref, t, 0, PW, wp, i * PW, sems.at[i])
    for i, t in enumerate(places_q):
        copies += fetch(w_ref, t, PW, QW, wq, i * QW, sems.at[4 + i])
    for c in copies:
        c.start()
    for c in copies[:12]:
        c.wait()
    part, sums = absorb(p_ref[...], gp_ref, places_p, wp[...], None)
    acc_ref[...] = part
    for c in copies[12:]:
        c.wait()
    part, sums = absorb(q_ref[...], gq_ref, places_q, wq[...], sums)
    acc_ref[...] += part
    sq_ref[...] = sums


def project_second(
    place_ref, acc_ref, sq_ref, q2_ref, q3_ref, gq_ref, w_ref, out_ref, sq_out_ref, xq, wq, sems, x_sems
):
    places = [[place_ref[k], place_ref[4 + k]] for k in (2, 3)]
    copies = []
    for g, pair in enumerate(places):
        group = [pltpu.make_async_copy((q2_ref, q3_ref)[g], xq.at[g], x_sems.at[g])]
        for i, t in enumerate(pair):
            group += fetch(w_ref, t, PW, QW, wq.at[g], i * QW, sems.at[2 * g + i])
        copies.append(group)
    for c in copies[0] + copies[1]:
        c.start()
    out_ref[...] = acc_ref[...]
    sums = sq_ref[...]
    for g in range(2):
        for c in copies[g]:
            c.wait()
        part, sums = absorb(xq[g], gq_ref, places[g], wq[g], sums)
        out_ref[...] += part
    sq_out_ref[...] = sums


def split(values):
    high = values.astype(BF)
    return high, (values - high.astype(F32)).astype(BF)


def thirds(values):
    high, low = split(values)
    rest = values - high.astype(F32) - low.astype(F32)
    return high, low, rest.astype(BF)


def attention(
    place_ref, acc0_ref, sq0_ref, p_ref, q1_ref, gp_ref, gq_ref,
    cos_ref, sin_ref, seg_col_ref, seg_row_ref, dctx_ref, w_ref,
    dp_ref, stat_ref, lane_ref, acc, acc0, xp, xq, wp, wq, sems, x_sems,
):
    places_p = [place_ref[4 + k] for k in range(4)]
    places_q = [place_ref[1], place_ref[5]]
    copies_p = [pltpu.make_async_copy(p_ref, xp, x_sems.at[0])]
    copies_q = [pltpu.make_async_copy(q1_ref, xq, x_sems.at[1])]
    for i, t in enumerate(places_q):
        copies_q += fetch(w_ref, t, PW, QW, wq, i * QW, sems.at[i])
    for i, t in enumerate(places_p):
        copies_p += fetch(w_ref, t, 0, PW, wp, i * PW, sems.at[2 + i])
    last = pltpu.make_async_copy(acc0_ref, acc0, x_sems.at[2])
    for c in copies_q + copies_p + [last]:
        c.start()
    for c in copies_q:
        c.wait()
    part, sums = absorb(xq[...], gq_ref, places_q, wq[...], sq0_ref[...])
    acc[...] = part
    for c in copies_p + [last]:
        c.wait()
    part, sums = absorb(xp[...], gp_ref, places_p, wp[...], sums)
    acc[...] += acc0[...] + part
    mean_square = jnp.sum(sums, axis=1, keepdims=True) * (1.0 / D) + 1e-05
    inverse = lax.rsqrt(mean_square)
    cosines, sines = cos_ref[...], sin_ref[...]
    queries_at = lax.broadcasted_iota(jnp.int32, (TOK, TOK), 0)
    keys_at = lax.broadcasted_iota(jnp.int32, (TOK, TOK), 1)
    allowed = (seg_col_ref[...] == seg_row_ref[...]) & (keys_at <= queries_at)
    scale = HD ** (-0.5)
    row_dot = jnp.zeros((TOK, HD), F32)
    for h in range(HEADS):
        at = [slice(n * HEADS * HD + h * HD, n * HEADS * HD + (h + 1) * HD) for n in range(3)]
        raw = [acc[:, s] * inverse for s in at]
        q, k, v = (r.astype(BF) for r in raw)
        qf, kf = q.astype(F32), k.astype(F32)
        qr = qf * cosines + pltpu.roll(qf, HD // 2, 1) * sines
        kr = kf * cosines + pltpu.roll(kf, HD // 2, 1) * sines
        qh, ql = split(qr)
        kh, kl = split(kr)
        scores = (dot(qh, kh, NT) + (dot(qh, kl, NT) + dot(ql, kh, NT))) * scale
        scores = jnp.where(allowed, scores, -1e30)
        weights = jnp.exp(scores - jnp.max(scores, axis=1, keepdims=True))
        weights = weights / jnp.sum(weights, axis=1, keepdims=True)
        cotangent = dctx_ref[:, h * HD : (h + 1) * HD]
        d_weights = dot(cotangent, v, NT)
        d_scores = weights * (
            d_weights - jnp.sum(weights * d_weights, axis=1, keepdims=True)
        )
        d_scores = (d_scores * scale).astype(BF)
        dv = dot(weights.astype(BF), cotangent, TN)
        dqr = dot(d_scores, kh, NN)
        dkr = dot(d_scores, qh, TN)
        dq = dqr * cosines + pltpu.roll(dqr * sines, HD // 2, 1)
        dk = dkr * cosines + pltpu.roll(dkr * sines, HD // 2, 1)
        for s, r, g in zip(at, raw, (dq, dk, dv)):
            row_dot += r * g
            dp_ref[:, s] = (g * inverse).astype(BF)
    stat_ref[...] = jnp.broadcast_to(inverse * inverse, (TOK, HD))
    ones = jnp.ones((16, HD), BF)
    lane_ref[...] = sum(dot(ones, part, NT) for part in thirds(row_dot * (1.0 / D)))[:8]


def pick(place_ref, quarter_ref, xp_ref, xq_ref, gp_ref, gq_ref, mine_ref, theirs_ref):
    wanted = lax.broadcasted_iota(jnp.int32, (320, SHARE), 0)
    wanted = jnp.where(
        wanted < 160, wanted + 160 * quarter_ref[0], wanted - 160 + 160 * quarter_ref[1]
    )
    unit = lax.broadcasted_iota(jnp.int32, (320, SHARE), 1) == wanted
    unit = jnp.where(unit, 1.0, 0.0).astype(BF)
    for dy in range(2):
        for k in range(4):
            t = place_ref[dy * 4 + k]
            xp = xp_ref[dy, :, k * PW : (k + 1) * PW].astype(F32) * gp_ref[t]
            xq = xq_ref[k, :, dy * QW : (dy + 1) * QW].astype(F32) * gq_ref[t]
            rows = dot(unit[:, :PW], xp.astype(BF), NT) + dot(unit[:, PW:], xq.astype(BF), NT)
            rows = rows.astype(BF)
            mine_ref[t, :, :TOK] = rows[:160]
            mine_ref[t, :, TOK:] = jnp.zeros((160, 64), BF)
            theirs_ref[t, :, :TOK] = rows[160:]
            theirs_ref[t, :, TOK:] = jnp.zeros((160, 64), BF)


def feature_gradient(
    place_ref, source_ref, quarter_ref, dp_ref, ph_ref, pt_ref, q0_ref, q1_ref, q2_ref, q3_ref,
    gp_ref, gq_ref, w_ref, out_ref, gain_ref, mine_ref, theirs_ref,
    ws, xp, xq, result, mine, theirs, sems, x_sems, out_sems,
):
    order = [(k, dy) for k in (1, 3, 2, 0) for dy in (0, 1)]
    copies = []
    for n, (k, dy) in enumerate(order):
        copies.append(fetch(w_ref, place_ref[dy * 4 + k], 0, SHARE, ws.at[n], 0, sems.at[n]))
    x_copies = [
        pltpu.make_async_copy(ref, slot, x_sems.at[i])
        for i, (ref, slot) in enumerate(
            (
                (ph_ref, xp.at[0]), (pt_ref, xp.at[1]), (q0_ref, xq.at[0]),
                (q1_ref, xq.at[1]), (q2_ref, xq.at[2]), (q3_ref, xq.at[3]),
            )
        )
    ]
    for c in copies[0] + x_copies + [c for group in copies[1:] for c in group]:
        c.start()
    dp = dp_ref[...]
    left = []

    def send(source, target, n):
        c = pltpu.make_async_copy(source, target, out_sems.at[n])
        c.start()
        left.append(c)

    for n, (k, dy) in enumerate(order):
        for c in copies[n]:
            c.wait()
        exact = dot(dp, ws[n], NT)
        if n == 0:
            for c in x_copies:
                c.wait()
        back = (4 - k) % 4
        row = pl.ds(place_ref[dy * 4 + k], 1)
        x_part = xp[dy, :, back * PW : (back + 1) * PW].astype(F32)
        gain_ref[row, :PW] = jnp.sum(exact[:, :PW] * x_part, axis=0, keepdims=True)
        x_part = xq[back, :, dy * QW : (dy + 1) * QW].astype(F32)
        gain_ref[row, PW:] = jnp.sum(exact[:, PW:] * x_part, axis=0, keepdims=True)
        result[n] = exact.astype(BF)
        send(result.at[n], out_ref.at[place_ref[dy * 4 + k]], n)
        if n == 3:
            pick(source_ref, quarter_ref, xp, xq, gp_ref, gq_ref, mine, theirs)
            send(theirs, theirs_ref, 8)
            send(mine, mine_ref, 9)
    for c in left:
        c.wait()


def weight_gradient(
    distances, owner_ref, slot_ref, own_ref, core_ref, f0, f1, f2, f3, d0, d1, d2, d3, *rest
):
    out_refs, rest = rest[: len(distances)], rest[len(distances) :]
    near, far, d_near, d_far, result, sems, near_sems, far_sems, out_sems = rest
    d_copies = [
        pltpu.make_async_copy(d0, d_near.at[pl.ds(0, TOK)], sems.at[0]),
        pltpu.make_async_copy(d1, d_near.at[pl.ds(384, TOK)], sems.at[1]),
        pltpu.make_async_copy(d2, d_far.at[pl.ds(0, TOK)], sems.at[2]),
        pltpu.make_async_copy(d3, d_far.at[pl.ds(TOK, TOK)], sems.at[3]),
    ]
    copies = []
    for i, r in enumerate(distances):
        rows = pl.ds(i * 160, 160)
        t = owner_ref[r]
        copies += [
            pltpu.make_async_copy(own_ref.at[t], near.at[rows, pl.ds(0, 384)], near_sems.at[i, 0]),
            pltpu.make_async_copy(core_ref.at[t], near.at[rows, pl.ds(384, 384)], near_sems.at[i, 1]),
        ]
    wanted = []
    for k, f in enumerate((f0, f1, f2, f3)):
        for dy in range(2):
            n = dy * 4 + k
            hit = slot_ref[n] == distances[0]
            for r in distances[1:]:
                hit = hit | (slot_ref[n] == r)
            c = pltpu.make_async_copy(f.at[pl.ds(dy * 160, 160)], far.at[slot_ref[n]], far_sems.at[n])
            wanted.append((hit, c))
    for c in d_copies + copies:
        c.start()
    for hit, c in wanted:
        pl.when(hit)(c.start)
    d_near[TOK:384] = jnp.zeros((64, COLS), BF)
    d_near[384 + TOK :] = jnp.zeros((64, COLS), BF)
    for c in d_copies + copies:
        c.wait()
    for hit, c in wanted:
        pl.when(hit)(c.wait)
    at, left = 0, []
    while at < len(distances):
        count = min(2, len(distances) - at)
        group = distances[at : at + count]
        x_far = jnp.concatenate([far[r] for r in group], axis=0) if count > 1 else far[group[0]]
        total = dot(near[at * 160 : (at + count) * 160], d_near[...], NN) + dot(x_far, d_far[...], NN)
        for i in range(count):
            result[at + i] = total[i * 160 : (i + 1) * 160].astype(BF)
            c = pltpu.make_async_copy(result.at[at + i], out_refs[at + i], out_sems.at[at + i])
            c.start()
            left.append(c)
        at += count
    for c in left:
        c.wait()


def finish(own_ref, down_ref, up_ref, out_ref):
    total = own_ref[...].astype(F32) + (down_ref[...].astype(F32) + up_ref[...].astype(F32))
    for n in range(3):
        out_ref[n] = total[:, n * HEADS * HD : (n + 1) * HEADS * HD].astype(BF)


VM = pl.BlockSpec(memory_space=pltpu.VMEM)
SM = pl.BlockSpec(memory_space=pltpu.SMEM)
ANY = pl.BlockSpec(memory_space=pl.ANY)
SMALL = pl.CostEstimate(flops=1000, bytes_accessed=1000, transcendentals=0)


def limit(mib):
    return pltpu.CompilerParams(vmem_limit_bytes=mib * 1024 * 1024)


def shift(values, axis, by, size):
    return lax.ppermute(values, axis, [(i, (i + by) % size) for i in range(size)])


def swap(values, axis, bit, size):
    return lax.ppermute(values, axis, [(i, i ^ bit) for i in range(size)])


def body(x_own, gain, w_qkv, segments, d_context):
    yh, core = lax.axis_index("yh"), lax.axis_index("core")
    yl, x_at = lax.axis_index("yl"), lax.axis_index("x")
    ks = jnp.arange(4, dtype=jnp.int32)
    rows = [yl, 1 - yl]
    sources = jnp.concatenate([r * 4 + (x_at - ks) % 4 for r in rows]).astype(jnp.int32)
    targets = jnp.concatenate([r * 4 + (x_at + ks) % 4 for r in rows]).astype(jnp.int32)
    gain_own = lax.dynamic_slice_in_dim(gain, (yl * 4 + x_at) * SHARE, SHARE, 0)

    xp, xq = x_own[:, :PW], x_own[:, PW:]
    got_p = [shift(xp, "x", k, 4) for k in (1, 2, 3)]
    got_q = swap(xq, "yl", 1, 2)
    scaled = (x_own.astype(F32) * gain_own).astype(BF).T.reshape(2, 2, 160, TOK)
    other = lax.dynamic_index_in_dim(scaled, 1 - yh, 0, False)
    other = jnp.stack([lax.dynamic_index_in_dim(other, c, 0, False) for c in (core, 1 - core)])
    other, got_p, got_q = lax.optimization_barrier((other, got_p, got_q))
    p_here = jnp.concatenate([xp] + got_p, axis=1)
    q_here = jnp.concatenate([xq, got_q], axis=1)
    p_there = swap(p_here, "yl", 1, 2)
    q_there = [shift(q_here, "x", k, 4) for k in (1, 2, 3)]
    other = swap(other, "yh", 1, 2)

    weight = w_qkv.transpose(1, 0, 2)
    gains = gain.reshape(8, 1, SHARE)
    gain_p, gain_q = gains[:, :, :PW], gains[:, :, PW:]
    acc, squares = pl.pallas_call(
        project_first,
        out_shape=(
            jax.ShapeDtypeStruct((TOK, COLS), F32),
            jax.ShapeDtypeStruct((TOK, 128), F32),
        ),
        in_specs=[SM, VM, VM, VM, VM, ANY],
        out_specs=(VM, VM),
        scratch_shapes=[
            pltpu.VMEM((4 * PW, COLS), BF),
            pltpu.VMEM((2 * QW, COLS), BF),
            pltpu.SemaphoreType.DMA((6, 3)),
        ],
        compiler_params=limit(63),
        cost_estimate=SMALL,
        name="project_first",
    )(sources, p_here, q_here, gain_p, gain_q, weight)

    acc, other = lax.optimization_barrier((acc, other))
    quarter = jnp.concatenate([other[0], swap(other[1], "core", 1, 2)], axis=1)
    acc, quarter = lax.optimization_barrier((acc, quarter))
    quarter_there = swap(quarter, "yl", 1, 2)

    acc, squares = pl.pallas_call(
        project_second,
        out_shape=(
            jax.ShapeDtypeStruct((TOK, COLS), F32),
            jax.ShapeDtypeStruct((TOK, 128), F32),
        ),
        in_specs=[SM, VM, VM, ANY, ANY, VM, ANY],
        out_specs=(VM, VM),
        scratch_shapes=[
            pltpu.VMEM((2, TOK, WIDE), BF),
            pltpu.VMEM((2, WIDE, COLS), BF),
            pltpu.SemaphoreType.DMA((4, 3)),
            pltpu.SemaphoreType.DMA((2,)),
        ],
        compiler_params=limit(63),
        cost_estimate=SMALL,
        name="project_second",
    )(sources, acc, squares, q_there[1], q_there[2], gain_q, weight)

    half = HD // 2
    angles = jnp.arange(TOK, dtype=F32)[:, None] * (
        10000.0 ** (-(2.0 * jnp.arange(half, dtype=F32)) / HD)
    )
    cosines, sines = jnp.cos(angles), jnp.sin(angles)
    cosines = jnp.concatenate([cosines, cosines], axis=1)
    sines = jnp.concatenate([-sines, sines], axis=1)
    d_packed, stats, row_dots = pl.pallas_call(
        attention,
        out_shape=(
            jax.ShapeDtypeStruct((TOK, COLS), BF),
            jax.ShapeDtypeStruct((TOK, HD), F32),
            jax.ShapeDtypeStruct((8, TOK), F32),
        ),
        in_specs=[SM, ANY, VM] + [ANY] * 2 + [VM] * 7 + [ANY],
        out_specs=(VM, VM, VM),
        scratch_shapes=[
            pltpu.VMEM((TOK, COLS), F32),
            pltpu.VMEM((TOK, COLS), F32),
            pltpu.VMEM((TOK, 4 * PW), BF),
            pltpu.VMEM((TOK, WIDE), BF),
            pltpu.VMEM((4 * PW, COLS), BF),
            pltpu.VMEM((WIDE, COLS), BF),
            pltpu.SemaphoreType.DMA((6, 3)),
            pltpu.SemaphoreType.DMA((3,)),
        ],
        compiler_params=limit(63),
        cost_estimate=SMALL,
        name="attention",
    )(
        sources, acc, squares, p_there, q_there[0], gain_p, gain_q, cosines, sines,
        segments[:, None], segments[None, :], d_context, weight,
    )

    d_packed, quarter, quarter_there = lax.optimization_barrier((d_packed, quarter, quarter_there))
    far = [jnp.concatenate([quarter, quarter_there], axis=0)]
    from_yh = swap(d_packed, "yh", 1, 2)
    from_core = swap(d_packed, "core", 1, 2)
    far = far + [shift(far[0], "x", k, 4) for k in (1, 2, 3)]
    quarters = jnp.stack([yh * 2 + core, yh * 2 + 1 - core]).astype(jnp.int32)
    shares, gains_here, x_mine, x_theirs = pl.pallas_call(
        feature_gradient,
        out_shape=tuple(
            [jax.ShapeDtypeStruct((8, TOK, SHARE), BF)]
            + [jax.ShapeDtypeStruct((8, SHARE), F32)]
            + [jax.ShapeDtypeStruct((8, 160, 384), BF)] * 2
        ),
        in_specs=[SM] * 3 + [VM] + [ANY] * 6 + [VM] * 2 + [ANY],
        out_specs=(ANY, VM, ANY, ANY),
        scratch_shapes=[
            pltpu.VMEM((8, SHARE, COLS), BF),
            pltpu.VMEM((2, TOK, 4 * PW), BF),
            pltpu.VMEM((4, TOK, WIDE), BF),
            pltpu.VMEM((8, TOK, SHARE), BF),
            pltpu.VMEM((8, 160, 384), BF),
            pltpu.VMEM((8, 160, 384), BF),
            pltpu.SemaphoreType.DMA((8, 3)),
            pltpu.SemaphoreType.DMA((6,)),
            pltpu.SemaphoreType.DMA((10,)),
        ],
        compiler_params=limit(63),
        cost_estimate=SMALL,
        name="feature_gradient",
    )(
        targets, sources, quarters, d_packed, p_here, p_there, q_here, *q_there, gain_p, gain_q, weight,
    )
    from_yh, from_core, far, x_theirs, gains, shares = lax.optimization_barrier(
        (from_yh, from_core, far, x_theirs, gains_here, shares)
    )
    d_normed = lax.psum_scatter(shares, ("yl", "x"), scatter_dimension=0, tiled=False)
    from_both = swap(from_yh, "core", 1, 2)
    x_core = swap(x_theirs, "core", 1, 2)
    from_both, x_core, gains = lax.optimization_barrier((from_both, x_core, gains))

    z_at = lax.axis_index("z")
    owners = ((z_at + jnp.arange(8)) % 8).astype(jnp.int32)
    slots = ((sources - z_at) % 8).astype(jnp.int32)
    operands = (owners, slots, x_mine, x_core, *far, d_packed, from_core, from_yh, from_both)

    def rows_for(distances, name):
        call = pl.pallas_call(
            functools.partial(weight_gradient, distances),
            out_shape=(jax.ShapeDtypeStruct((160, COLS), BF),) * len(distances),
            in_specs=[SM, SM] + [ANY] * 10,
            out_specs=(ANY,) * len(distances),
            scratch_shapes=[
                pltpu.VMEM((len(distances) * 160, 768), BF),
                pltpu.VMEM((8, 160, 640), BF),
                pltpu.VMEM((768, COLS), BF),
                pltpu.VMEM((640, COLS), BF),
                pltpu.VMEM((len(distances), 160, COLS), BF),
                pltpu.SemaphoreType.DMA((4,)),
                pltpu.SemaphoreType.DMA((len(distances), 2)),
                pltpu.SemaphoreType.DMA((8,)),
                pltpu.SemaphoreType.DMA((len(distances),)),
            ],
            compiler_params=limit(32),
            cost_estimate=SMALL,
            name=name,
        )
        return list(call(*operands))

    def plus(a, b):
        return (a.astype(F32) + b.astype(F32)).astype(BF)

    there = swap(gains, "z", 1, 8)
    far_rows = rows_for((4,), "weight_gradient_far")[0]
    far_rows, there = lax.optimization_barrier((far_rows, there))
    gains = gains + there
    down = shift(far_rows, "z", 1, 8)
    heard = [swap(gains, "z", bit, 8) for bit in (2, 4, 6)]
    rest = rows_for((3, 5), "weight_gradient_middle")
    down, heard, rest[0] = lax.optimization_barrier((down, heard, rest[0]))
    gains = ((gains + heard[0]) + (heard[1] + heard[2])).reshape(2, 4, SHARE)
    down = shift(plus(rest[0], down), "z", 1, 8)
    up = shift(rest[1], "z", -1, 8)
    row_dots = jnp.pad(row_dots[:1], ((0, 0), (0, SHARE - TOK)))
    empty = jnp.zeros((5, SHARE), F32)
    small = [
        jnp.concatenate([lax.dynamic_index_in_dim(gains, x_at ^ bit, 1, False), row_dots, empty])
        for bit in range(4)
    ]
    small = small[:1] + [swap(small[bit], "x", bit, 4) for bit in (1, 2, 3)]
    rest += rows_for((2, 6), "weight_gradient_near")
    down, up, small, rest[2] = lax.optimization_barrier((down, up, small, rest[2]))
    small = (small[0] + small[1]) + (small[2] + small[3])
    down = shift(plus(rest[2], down), "z", 1, 8)
    up = shift(plus(rest[3], up), "z", -1, 8)
    heard = [swap(small, "yl", 1, 2), swap(small, "yh", 1, 2)]
    heard.append(lax.ppermute(small, ("yh", "yl"), [(i, 3 - i) for i in range(4)]))
    rest += rows_for((1, 7, 0), "weight_gradient_nearest")
    down, up, heard, rest[4] = lax.optimization_barrier((down, up, heard, rest[4]))
    row_dot = small[2, :TOK] + heard[0][2, :TOK]
    parts = [lax.dynamic_index_in_dim(v, yl, 0, False) for v in (small, *heard)]
    share = (parts[0] + parts[1]) + (parts[2] + parts[3])
    down = shift(plus(rest[4], down), "z", 1, 8)
    up = shift(plus(rest[5], up), "z", -1, 8)
    share = share + swap(share, "core", 1, 2)
    down, up, share = lax.optimization_barrier((down, up, share))
    row_dot = row_dot * stats[:, 0]
    input_gradient = d_normed.astype(F32) * gain_own - x_own.astype(F32) * row_dot[:, None]
    d_weight = pl.pallas_call(
        finish,
        out_shape=jax.ShapeDtypeStruct((3, 160, HEADS * HD), BF),
        in_specs=[VM] * 3,
        out_specs=VM,
        compiler_params=limit(8),
        cost_estimate=SMALL,
        name="finish",
    )(rest[6], down, up)
    return input_gradient.astype(BF), share, d_weight.transpose(1, 0, 2)


def solution(mesh):
    fine = Mesh(mesh.devices.reshape(8, 2, 2, 2, 4), ("z", "yh", "core", "yl", "x"))
    dp, tensor = ("z", "yh", "core"), ("yl", "x")
    in_specs = (P(dp, tensor), P(), P(None, None, tensor), P(dp), P(dp, tensor))
    out_specs = (P(dp, tensor), P(tensor), P(dp, None, tensor))
    return jax.shard_map(
        body, mesh=fine, in_specs=in_specs, out_specs=out_specs, check_vma=False
    )
```

```python
import functools

import jax
import jax.numpy as jnp
from jax import lax
from jax.experimental import pallas as pl
from jax.experimental.pallas import tpu as pltpu
from jax.sharding import Mesh, PartitionSpec as P

HD = 128
HEADS = 3
TOK = 320
D = 5120
COLS = 1152
SHARE = 640
PW = 256
WIDE = 768
QW = 384
BF = jnp.bfloat16
F32 = jnp.float32


def dot(a, b, dims):
    return lax.dot_general(a, b, (dims, ((), ())), preferred_element_type=F32)


NN = ((1,), (0,))
NT = ((1,), (1,))
TN = ((0,), (0,))


def square_sum(values):
    width = values.shape[1]
    squares = values * values
    total = squares[:, :128]
    for start in range(128, width, 128):
        total = total + squares[:, start : start + 128]
    return total


def absorb(x, gain_ref, places, w_slot, sums):
    width = x.shape[1] // len(places)
    values = x.astype(F32)
    gains = jnp.concatenate([gain_ref[t] for t in places], axis=1)
    sums = square_sum(values) if sums is None else sums + square_sum(values)
    return dot((values * gains).astype(BF), w_slot, NN), sums


def fetch(w_ref, place, first, count, slot, start, sems):
    return [
        pltpu.make_async_copy(
            w_ref.at[n, pl.ds(place * SHARE + first, count)],
            slot.at[pl.ds(start, count), pl.ds(n * HEADS * HD, HEADS * HD)],
            sems.at[n],
        )
        for n in range(3)
    ]


def project_first(place_ref, p_ref, q_ref, gp_ref, gq_ref, w_ref, acc_ref, sq_ref, wp, wq, sems):
    places_p = [place_ref[k] for k in range(4)]
    places_q = [place_ref[0], place_ref[4]]
    copies = []
    for i, t in enumerate(places_p):
        copies += fetch(w_ref, t, 0, PW, wp, i * PW, sems.at[i])
    for i, t in enumerate(places_q):
        copies += fetch(w_ref, t, PW, QW, wq, i * QW, sems.at[4 + i])
    for c in copies:
        c.start()
    for c in copies[:12]:
        c.wait()
    part, sums = absorb(p_ref[...], gp_ref, places_p, wp[...], None)
    acc_ref[...] = part
    for c in copies[12:]:
        c.wait()
    part, sums = absorb(q_ref[...], gq_ref, places_q, wq[...], sums)
    acc_ref[...] += part
    sq_ref[...] = sums


def split(values):
    high = values.astype(BF)
    return high, (values - high.astype(F32)).astype(BF)


def thirds(values):
    high, low = split(values)
    rest = values - high.astype(F32) - low.astype(F32)
    return high, low, rest.astype(BF)


def attention(
    place_ref, acc0_ref, sq0_ref, p_ref, q1_ref, q2_ref, q3_ref, gp_ref, gq_ref,
    cos_ref, sin_ref, seg_col_ref, seg_row_ref, dctx_ref, w_ref, here_ref, there_ref,
    dp_ref, stat_ref, lane_ref, far_ref, acc, acc0, xp, xq, wp, wq, far, sems, x_sems, far_sems,
):
    places_p = [place_ref[4 + k] for k in range(4)]
    places_q = [[place_ref[k], place_ref[4 + k]] for k in range(1, 4)]
    copies_p, copies_q = [], []
    for i, t in enumerate(places_p):
        copies_p += fetch(w_ref, t, 0, PW, wp, i * PW, sems.at[i])
    for g, pair in enumerate(places_q):
        for i, t in enumerate(pair):
            copies_q += fetch(w_ref, t, PW, QW, wq.at[g], i * QW, sems.at[4 + 2 * g + i])
    x_copies = [pltpu.make_async_copy(p_ref, xp, x_sems.at[0])]
    for g, x_ref in enumerate((q1_ref, q2_ref, q3_ref)):
        x_copies.append(pltpu.make_async_copy(x_ref, xq.at[g], x_sems.at[1 + g]))
    x_copies.append(pltpu.make_async_copy(acc0_ref, acc0, x_sems.at[4]))
    for c in x_copies[:1] + copies_p + x_copies[1:4] + copies_q + x_copies[4:]:
        c.start()
    far_in = [
        pltpu.make_async_copy(ref, far.at[pl.ds(i * 160, 160)], far_sems.at[i])
        for i, ref in enumerate((here_ref, there_ref))
    ]
    far_out = pltpu.make_async_copy(far, far_ref, far_sems.at[2])
    for c in far_in:
        c.start()
    sums = sq0_ref[...]
    for c in x_copies[:1] + copies_p:
        c.wait()
    part, sums = absorb(xp[...], gp_ref, places_p, wp[...], sums)
    acc[...] = part
    for g in range(3):
        for c in x_copies[1 + g : 2 + g] + copies_q[6 * g : 6 * g + 6]:
            c.wait()
        part, sums = absorb(xq[g], gq_ref, places_q[g], wq[g], sums)
        acc[...] += part
    x_copies[4].wait()
    acc[...] += acc0[...]
    for c in far_in:
        c.wait()
    far_out.start()
    mean_square = jnp.sum(sums, axis=1, keepdims=True) * (1.0 / D) + 1e-05
    inverse = lax.rsqrt(mean_square)
    cosines, sines = cos_ref[...], sin_ref[...]
    queries_at = lax.broadcasted_iota(jnp.int32, (TOK, TOK), 0)
    keys_at = lax.broadcasted_iota(jnp.int32, (TOK, TOK), 1)
    allowed = (seg_col_ref[...] == seg_row_ref[...]) & (keys_at <= queries_at)
    scale = HD ** (-0.5)
    row_dot = jnp.zeros((TOK, HD), F32)
    for h in range(HEADS):
        at = [slice(n * HEADS * HD + h * HD, n * HEADS * HD + (h + 1) * HD) for n in range(3)]
        raw = [acc[:, s] * inverse for s in at]
        q, k, v = (r.astype(BF) for r in raw)
        qf, kf = q.astype(F32), k.astype(F32)
        qr = qf * cosines + pltpu.roll(qf, HD // 2, 1) * sines
        kr = kf * cosines + pltpu.roll(kf, HD // 2, 1) * sines
        qh, ql = split(qr)
        kh, kl = split(kr)
        scores = (dot(qh, kh, NT) + (dot(qh, kl, NT) + dot(ql, kh, NT))) * scale
        scores = jnp.where(allowed, scores, -1e30)
        weights = jnp.exp(scores - jnp.max(scores, axis=1, keepdims=True))
        weights = weights / jnp.sum(weights, axis=1, keepdims=True)
        cotangent = dctx_ref[:, h * HD : (h + 1) * HD]
        d_weights = dot(cotangent, v, NT)
        d_scores = weights * (
            d_weights - jnp.sum(weights * d_weights, axis=1, keepdims=True)
        )
        d_scores = (d_scores * scale).astype(BF)
        dv = dot(weights.astype(BF), cotangent, TN)
        dqr = dot(d_scores, kh, NN)
        dkr = dot(d_scores, qh, TN)
        dq = dqr * cosines + pltpu.roll(dqr * sines, HD // 2, 1)
        dk = dkr * cosines + pltpu.roll(dkr * sines, HD // 2, 1)
        for s, r, g in zip(at, raw, (dq, dk, dv)):
            row_dot += r * g
            dp_ref[:, s] = (g * inverse).astype(BF)
    stat_ref[...] = jnp.broadcast_to(inverse * inverse, (TOK, HD))
    ones = jnp.ones((16, HD), BF)
    lane_ref[...] = sum(dot(ones, part, NT) for part in thirds(row_dot * (1.0 / D)))[:8]
    far_out.wait()


def pick(place_ref, quarter_ref, xp_ref, xq_ref, gp_ref, gq_ref, mine_ref, theirs_ref):
    wanted = lax.broadcasted_iota(jnp.int32, (320, SHARE), 0)
    wanted = jnp.where(
        wanted < 160, wanted + 160 * quarter_ref[0], wanted - 160 + 160 * quarter_ref[1]
    )
    unit = lax.broadcasted_iota(jnp.int32, (320, SHARE), 1) == wanted
    unit = jnp.where(unit, 1.0, 0.0).astype(BF)
    for dy in range(2):
        for k in range(4):
            t = place_ref[dy * 4 + k]
            xp = xp_ref[dy, :, k * PW : (k + 1) * PW].astype(F32) * gp_ref[t]
            xq = xq_ref[k, :, dy * QW : (dy + 1) * QW].astype(F32) * gq_ref[t]
            rows = dot(unit[:, :PW], xp.astype(BF), NT) + dot(unit[:, PW:], xq.astype(BF), NT)
            rows = rows.astype(BF)
            mine_ref[t, :, :TOK] = rows[:160]
            mine_ref[t, :, TOK:] = jnp.zeros((160, 64), BF)
            theirs_ref[t, :, :TOK] = rows[160:]
            theirs_ref[t, :, TOK:] = jnp.zeros((160, 64), BF)


def feature_gradient(
    place_ref, source_ref, quarter_ref, dp_ref, ph_ref, pt_ref, q0_ref, q1_ref, q2_ref, q3_ref,
    gp_ref, gq_ref, w_ref, out_ref, gain_ref, mine_ref, theirs_ref,
    ws, xp, xq, result, mine, theirs, sems, x_sems, out_sems,
):
    order = [(k, dy) for k in (1, 3, 2, 0) for dy in (0, 1)]
    copies = []
    for n, (k, dy) in enumerate(order):
        copies.append(fetch(w_ref, place_ref[dy * 4 + k], 0, SHARE, ws.at[n], 0, sems.at[n]))
    x_copies = [
        pltpu.make_async_copy(ref, slot, x_sems.at[i])
        for i, (ref, slot) in enumerate(
            (
                (ph_ref, xp.at[0]), (pt_ref, xp.at[1]), (q0_ref, xq.at[0]),
                (q1_ref, xq.at[1]), (q2_ref, xq.at[2]), (q3_ref, xq.at[3]),
            )
        )
    ]
    for c in copies[0] + x_copies + [c for group in copies[1:] for c in group]:
        c.start()
    dp = dp_ref[...]
    left = []

    def send(source, target, n):
        c = pltpu.make_async_copy(source, target, out_sems.at[n])
        c.start()
        left.append(c)

    for n, (k, dy) in enumerate(order):
        for c in copies[n]:
            c.wait()
        exact = dot(dp, ws[n], NT)
        if n == 0:
            for c in x_copies:
                c.wait()
        back = (4 - k) % 4
        row = pl.ds(place_ref[dy * 4 + k], 1)
        x_part = xp[dy, :, back * PW : (back + 1) * PW].astype(F32)
        gain_ref[row, :PW] = jnp.sum(exact[:, :PW] * x_part, axis=0, keepdims=True)
        x_part = xq[back, :, dy * QW : (dy + 1) * QW].astype(F32)
        gain_ref[row, PW:] = jnp.sum(exact[:, PW:] * x_part, axis=0, keepdims=True)
        result[n] = exact.astype(BF)
        send(result.at[n], out_ref.at[place_ref[dy * 4 + k]], n)
        if n == 3:
            pick(source_ref, quarter_ref, xp, xq, gp_ref, gq_ref, mine, theirs)
            send(theirs, theirs_ref, 8)
            send(mine, mine_ref, 9)
    for c in left:
        c.wait()


def weight_gradient(
    distances, owner_ref, slot_ref, own_ref, core_ref, f0, f1, f2, f3, d0, d1, d2, d3, *rest
):
    out_refs, token_ref, rest = rest[: len(distances)], rest[len(distances)], rest[len(distances) + 1 :]
    token_ref[...] = jnp.zeros((8, 128), F32)
    near, far, d_near, d_far, result, sems, near_sems, far_sems, out_sems = rest
    d_copies = [
        pltpu.make_async_copy(d0, d_near.at[pl.ds(0, TOK)], sems.at[0]),
        pltpu.make_async_copy(d1, d_near.at[pl.ds(384, TOK)], sems.at[1]),
        pltpu.make_async_copy(d2, d_far.at[pl.ds(0, TOK)], sems.at[2]),
        pltpu.make_async_copy(d3, d_far.at[pl.ds(TOK, TOK)], sems.at[3]),
    ]
    copies = []
    for i, r in enumerate(distances):
        rows = pl.ds(i * 160, 160)
        t = owner_ref[r]
        copies += [
            pltpu.make_async_copy(own_ref.at[t], near.at[rows, pl.ds(0, 384)], near_sems.at[i, 0]),
            pltpu.make_async_copy(core_ref.at[t], near.at[rows, pl.ds(384, 384)], near_sems.at[i, 1]),
        ]
    wanted = []
    for k, f in enumerate((f0, f1, f2, f3)):
        for dy in range(2):
            n = dy * 4 + k
            hit = slot_ref[n] == distances[0]
            for r in distances[1:]:
                hit = hit | (slot_ref[n] == r)
            c = pltpu.make_async_copy(f.at[pl.ds(dy * 160, 160)], far.at[slot_ref[n]], far_sems.at[n])
            wanted.append((hit, c))
    for c in d_copies + copies:
        c.start()
    for hit, c in wanted:
        pl.when(hit)(c.start)
    d_near[TOK:384] = jnp.zeros((64, COLS), BF)
    d_near[384 + TOK :] = jnp.zeros((64, COLS), BF)
    for c in d_copies + copies:
        c.wait()
    for hit, c in wanted:
        pl.when(hit)(c.wait)
    at, left = 0, []
    while at < len(distances):
        count = min(2, len(distances) - at)
        group = distances[at : at + count]
        x_far = jnp.concatenate([far[r] for r in group], axis=0) if count > 1 else far[group[0]]
        total = dot(near[at * 160 : (at + count) * 160], d_near[...], NN) + dot(x_far, d_far[...], NN)
        for i in range(count):
            result[at + i] = total[i * 160 : (i + 1) * 160].astype(BF)
            c = pltpu.make_async_copy(result.at[at + i], out_refs[at + i], out_sems.at[at + i])
            c.start()
            left.append(c)
        at += count
    for c in left:
        c.wait()


def finish(own_ref, down_ref, up_ref, out_ref):
    total = own_ref[...].astype(F32) + (down_ref[...].astype(F32) + up_ref[...].astype(F32))
    for n in range(3):
        out_ref[n] = total[:, n * HEADS * HD : (n + 1) * HEADS * HD].astype(BF)


VM = pl.BlockSpec(memory_space=pltpu.VMEM)
SM = pl.BlockSpec(memory_space=pltpu.SMEM)
ANY = pl.BlockSpec(memory_space=pl.ANY)
SMALL = pl.CostEstimate(flops=1000, bytes_accessed=1000, transcendentals=0)


def limit(mib):
    return pltpu.CompilerParams(vmem_limit_bytes=mib * 1024 * 1024)


def shift(values, axis, by, size):
    return lax.ppermute(values, axis, [(i, (i + by) % size) for i in range(size)])


def swap(values, axis, bit, size):
    return lax.ppermute(values, axis, [(i, i ^ bit) for i in range(size)])


def body(x_own, gain, w_qkv, segments, d_context):
    yh, core = lax.axis_index("yh"), lax.axis_index("core")
    yl, x_at = lax.axis_index("yl"), lax.axis_index("x")
    ks = jnp.arange(4, dtype=jnp.int32)
    rows = [yl, 1 - yl]
    sources = jnp.concatenate([r * 4 + (x_at - ks) % 4 for r in rows]).astype(jnp.int32)
    targets = jnp.concatenate([r * 4 + (x_at + ks) % 4 for r in rows]).astype(jnp.int32)
    gain_own = lax.dynamic_slice_in_dim(gain, (yl * 4 + x_at) * SHARE, SHARE, 0)

    xp, xq = x_own[:, :PW], x_own[:, PW:]
    got_p = [shift(xp, "x", k, 4) for k in (1, 2, 3)]
    got_q = swap(xq, "yl", 1, 2)
    scaled = (x_own.astype(F32) * gain_own).astype(BF).T.reshape(2, 2, 160, TOK)
    other = lax.dynamic_index_in_dim(scaled, 1 - yh, 0, False)
    other = jnp.stack([lax.dynamic_index_in_dim(other, c, 0, False) for c in (core, 1 - core)])
    other, got_p, got_q = lax.optimization_barrier((other, got_p, got_q))
    p_here = jnp.concatenate([xp] + got_p, axis=1)
    q_here = jnp.concatenate([xq, got_q], axis=1)
    p_there = swap(p_here, "yl", 1, 2)
    q_there = [shift(q_here, "x", k, 4) for k in (1, 2, 3)]
    other = swap(other, "yh", 1, 2)

    weight = w_qkv.transpose(1, 0, 2)
    gains = gain.reshape(8, 1, SHARE)
    gain_p, gain_q = gains[:, :, :PW], gains[:, :, PW:]
    acc, squares = pl.pallas_call(
        project_first,
        out_shape=(
            jax.ShapeDtypeStruct((TOK, COLS), F32),
            jax.ShapeDtypeStruct((TOK, 128), F32),
        ),
        in_specs=[SM, VM, VM, VM, VM, ANY],
        out_specs=(VM, VM),
        scratch_shapes=[
            pltpu.VMEM((4 * PW, COLS), BF),
            pltpu.VMEM((2 * QW, COLS), BF),
            pltpu.SemaphoreType.DMA((6, 3)),
        ],
        compiler_params=limit(63),
        cost_estimate=SMALL,
        name="project_first",
    )(sources, p_here, q_here, gain_p, gain_q, weight)

    acc, other = lax.optimization_barrier((acc, other))
    quarter = jnp.concatenate([other[0], swap(other[1], "core", 1, 2)], axis=1)
    acc, quarter = lax.optimization_barrier((acc, quarter))
    quarter_there = swap(quarter, "yl", 1, 2)

    half = HD // 2
    angles = jnp.arange(TOK, dtype=F32)[:, None] * (
        10000.0 ** (-(2.0 * jnp.arange(half, dtype=F32)) / HD)
    )
    cosines, sines = jnp.cos(angles), jnp.sin(angles)
    cosines = jnp.concatenate([cosines, cosines], axis=1)
    sines = jnp.concatenate([-sines, sines], axis=1)
    d_packed, stats, row_dots, far_own = pl.pallas_call(
        attention,
        out_shape=(
            jax.ShapeDtypeStruct((TOK, COLS), BF),
            jax.ShapeDtypeStruct((TOK, HD), F32),
            jax.ShapeDtypeStruct((8, TOK), F32),
            jax.ShapeDtypeStruct((320, 640), BF),
        ),
        in_specs=[SM, ANY, VM] + [ANY] * 4 + [VM] * 7 + [ANY] * 3,
        out_specs=(VM, VM, VM, ANY),
        scratch_shapes=[
            pltpu.VMEM((TOK, COLS), F32),
            pltpu.VMEM((TOK, COLS), F32),
            pltpu.VMEM((TOK, 4 * PW), BF),
            pltpu.VMEM((3, TOK, WIDE), BF),
            pltpu.VMEM((4 * PW, COLS), BF),
            pltpu.VMEM((3, 2 * QW, COLS), BF),
            pltpu.VMEM((320, 640), BF),
            pltpu.SemaphoreType.DMA((10, 3)),
            pltpu.SemaphoreType.DMA((5,)),
            pltpu.SemaphoreType.DMA((3,)),
        ],
        compiler_params=limit(63),
        cost_estimate=SMALL,
        name="attention",
    )(
        sources, acc, squares, p_there, *q_there, gain_p, gain_q, cosines, sines,
        segments[:, None], segments[None, :], d_context, weight, quarter, quarter_there,
    )

    far = [far_own]
    from_yh = swap(d_packed, "yh", 1, 2)
    from_core = swap(d_packed, "core", 1, 2)
    far = far + [shift(far[0], "x", k, 4) for k in (1, 2, 3)]
    quarters = jnp.stack([yh * 2 + core, yh * 2 + 1 - core]).astype(jnp.int32)
    shares, gains_here, x_mine, x_theirs = pl.pallas_call(
        feature_gradient,
        out_shape=tuple(
            [jax.ShapeDtypeStruct((8, TOK, SHARE), BF)]
            + [jax.ShapeDtypeStruct((8, SHARE), F32)]
            + [jax.ShapeDtypeStruct((8, 160, 384), BF)] * 2
        ),
        in_specs=[SM] * 3 + [VM] + [ANY] * 6 + [VM] * 2 + [ANY],
        out_specs=(ANY, VM, ANY, ANY),
        scratch_shapes=[
            pltpu.VMEM((8, SHARE, COLS), BF),
            pltpu.VMEM((2, TOK, 4 * PW), BF),
            pltpu.VMEM((4, TOK, WIDE), BF),
            pltpu.VMEM((8, TOK, SHARE), BF),
            pltpu.VMEM((8, 160, 384), BF),
            pltpu.VMEM((8, 160, 384), BF),
            pltpu.SemaphoreType.DMA((8, 3)),
            pltpu.SemaphoreType.DMA((6,)),
            pltpu.SemaphoreType.DMA((10,)),
        ],
        compiler_params=limit(63),
        cost_estimate=SMALL,
        name="feature_gradient",
    )(
        targets, sources, quarters, d_packed, p_here, p_there, q_here, *q_there, gain_p, gain_q, weight,
    )
    from_yh, from_core, far, x_theirs, gains, shares = lax.optimization_barrier(
        (from_yh, from_core, far, x_theirs, gains_here, shares)
    )
    d_normed = lax.psum_scatter(shares, ("yl", "x"), scatter_dimension=0, tiled=False)
    from_both = swap(from_yh, "core", 1, 2)
    x_core = swap(x_theirs, "core", 1, 2)
    there = swap(gains, "core", 1, 2)
    from_both, x_core, there = lax.optimization_barrier((from_both, x_core, there))
    gains = gains + there

    z_at = lax.axis_index("z")
    owners = ((z_at + jnp.arange(8)) % 8).astype(jnp.int32)
    slots = ((sources - z_at) % 8).astype(jnp.int32)
    operands = (owners, slots, x_mine, x_core, *far, d_packed, from_core, from_yh, from_both)

    def rows_for(distances, name):
        call = pl.pallas_call(
            functools.partial(weight_gradient, distances),
            out_shape=(jax.ShapeDtypeStruct((160, COLS), BF),) * len(distances)
            + (jax.ShapeDtypeStruct((8, 128), F32),),
            in_specs=[SM, SM] + [ANY] * 10,
            out_specs=(ANY,) * len(distances) + (VM,),
            scratch_shapes=[
                pltpu.VMEM((len(distances) * 160, 768), BF),
                pltpu.VMEM((8, 160, 640), BF),
                pltpu.VMEM((768, COLS), BF),
                pltpu.VMEM((640, COLS), BF),
                pltpu.VMEM((len(distances), 160, COLS), BF),
                pltpu.SemaphoreType.DMA((4,)),
                pltpu.SemaphoreType.DMA((len(distances), 2)),
                pltpu.SemaphoreType.DMA((8,)),
                pltpu.SemaphoreType.DMA((len(distances),)),
            ],
            compiler_params=limit(32),
            cost_estimate=SMALL,
            name=name,
        )
        return list(call(*operands))

    def plus(a, b):
        return (a.astype(F32) + b.astype(F32)).astype(BF)

    there = swap(gains, "z", 1, 8)
    far_rows, _ = rows_for((4,), "weight_gradient_far")
    far_rows, there = lax.optimization_barrier((far_rows, there))
    gains = gains + there
    down = shift(far_rows, "z", 1, 8)
    there = swap(gains, "z", 2, 8)
    *rest, token = rows_for((3, 5), "weight_gradient_middle")
    down, there, token = lax.optimization_barrier((down, there, token))
    gains = gains + there
    down = shift(plus(rest[0], down), "z", 1, 8)
    up = shift(rest[1], "z", -1, 8)
    *near_rows, token = rows_for((2, 6, 1, 7, 0), "weight_gradient_near")
    rest += near_rows
    gains = gains + token[0, 0]
    there = swap(gains, "z", 4, 8)
    down, up, there = lax.optimization_barrier((down, up, there))
    gains = (gains + there).reshape(2, 4, SHARE)
    down = shift(plus(rest[2], down), "z", 1, 8)
    up = shift(plus(rest[3], up), "z", -1, 8)
    row_dots = jnp.pad(row_dots[:1], ((0, 0), (0, SHARE - TOK)))
    empty = jnp.zeros((5, SHARE), F32)
    small = [
        jnp.concatenate([lax.dynamic_index_in_dim(gains, x_at ^ bit, 1, False), row_dots, empty])
        for bit in range(4)
    ]
    small = small[:1] + [swap(small[bit], "x", bit, 4) for bit in (1, 2, 3)]
    down, up, small = lax.optimization_barrier((down, up, small))
    small = (small[0] + small[1]) + (small[2] + small[3])
    down = shift(plus(rest[4], down), "z", 1, 8)
    up = shift(plus(rest[5], up), "z", -1, 8)
    there = swap(small, "yl", 1, 2)
    row_dot = small[2, :TOK] + there[2, :TOK]
    share = lax.dynamic_index_in_dim(small, yl, 0, False) + lax.dynamic_index_in_dim(there, yl, 0, False)
    share = share + swap(share, "yh", 1, 2)
    down, up, share = lax.optimization_barrier((down, up, share))
    row_dot = row_dot * stats[:, 0]
    input_gradient = d_normed.astype(F32) * gain_own - x_own.astype(F32) * row_dot[:, None]
    d_weight = pl.pallas_call(
        finish,
        out_shape=jax.ShapeDtypeStruct((3, 160, HEADS * HD), BF),
        in_specs=[VM] * 3,
        out_specs=VM,
        compiler_params=limit(8),
        cost_estimate=SMALL,
        name="finish",
    )(rest[6], down, up)
    return input_gradient.astype(BF), share, d_weight.transpose(1, 0, 2)


def solution(mesh):
    fine = Mesh(mesh.devices.reshape(8, 2, 2, 2, 4), ("z", "yh", "core", "yl", "x"))
    dp, tensor = ("z", "yh", "core"), ("yl", "x")
    in_specs = (P(dp, tensor), P(), P(None, None, tensor), P(dp), P(dp, tensor))
    out_specs = (P(dp, tensor), P(tensor), P(dp, None, tensor))
    return jax.shard_map(
        body, mesh=fine, in_specs=in_specs, out_specs=out_specs, check_vma=False
    )
```

```python
import functools

import jax
import jax.numpy as jnp
from jax import lax
from jax.experimental import pallas as pl
from jax.experimental.pallas import tpu as pltpu
from jax.sharding import Mesh, PartitionSpec as P

HD = 128
HEADS = 3
TOK = 320
D = 5120
COLS = 1152
SHARE = 640
PW = 256
WIDE = 768
QW = 384
BF = jnp.bfloat16
F32 = jnp.float32


def dot(a, b, dims):
    return lax.dot_general(a, b, (dims, ((), ())), preferred_element_type=F32)


NN = ((1,), (0,))
NT = ((1,), (1,))
TN = ((0,), (0,))


def square_sum(values):
    width = values.shape[1]
    squares = values * values
    total = squares[:, :128]
    for start in range(128, width, 128):
        total = total + squares[:, start : start + 128]
    return total


def absorb(x, gain_ref, places, w_slot, sums):
    width = x.shape[1] // len(places)
    values = x.astype(F32)
    gains = jnp.concatenate([gain_ref[t] for t in places], axis=1)
    sums = square_sum(values) if sums is None else sums + square_sum(values)
    return dot((values * gains).astype(BF), w_slot, NN), sums


def fetch(w_ref, place, first, count, slot, start, sems):
    return [
        pltpu.make_async_copy(
            w_ref.at[n, pl.ds(place * SHARE + first, count)],
            slot.at[pl.ds(start, count), pl.ds(n * HEADS * HD, HEADS * HD)],
            sems.at[n],
        )
        for n in range(3)
    ]


def project_first(place_ref, p_ref, q_ref, gp_ref, gq_ref, w_ref, acc_ref, sq_ref, wp, wq, sems):
    places_p = [place_ref[k] for k in range(4)]
    places_q = [place_ref[0], place_ref[4]]
    copies = []
    for i, t in enumerate(places_p):
        copies += fetch(w_ref, t, 0, PW, wp, i * PW, sems.at[i])
    for i, t in enumerate(places_q):
        copies += fetch(w_ref, t, PW, QW, wq, i * QW, sems.at[4 + i])
    for c in copies:
        c.start()
    for c in copies[:12]:
        c.wait()
    part, sums = absorb(p_ref[...], gp_ref, places_p, wp[...], None)
    acc_ref[...] = part
    for c in copies[12:]:
        c.wait()
    part, sums = absorb(q_ref[...], gq_ref, places_q, wq[...], sums)
    acc_ref[...] += part
    sq_ref[...] = sums


def split(values):
    high = values.astype(BF)
    return high, (values - high.astype(F32)).astype(BF)


def thirds(values):
    high, low = split(values)
    rest = values - high.astype(F32) - low.astype(F32)
    return high, low, rest.astype(BF)


def attention(
    place_ref, acc0_ref, sq0_ref, p_ref, q1_ref, q2_ref, q3_ref, gp_ref, gq_ref,
    cos_ref, sin_ref, seg_col_ref, seg_row_ref, dctx_ref, w_ref, here_ref, there_ref,
    dp_ref, stat_ref, lane_ref, far_ref, acc, acc0, xp, xq, wp, wq, far, sems, x_sems, far_sems,
):
    places_p = [place_ref[4 + k] for k in range(4)]
    places_q = [[place_ref[k], place_ref[4 + k]] for k in range(1, 4)]
    copies_p, copies_q = [], []
    for i, t in enumerate(places_p):
        copies_p += fetch(w_ref, t, 0, PW, wp, i * PW, sems.at[i])
    for g, pair in enumerate(places_q):
        for i, t in enumerate(pair):
            copies_q += fetch(w_ref, t, PW, QW, wq.at[g], i * QW, sems.at[4 + 2 * g + i])
    x_copies = [pltpu.make_async_copy(p_ref, xp, x_sems.at[0])]
    for g, x_ref in enumerate((q1_ref, q2_ref, q3_ref)):
        x_copies.append(pltpu.make_async_copy(x_ref, xq.at[g], x_sems.at[1 + g]))
    x_copies.append(pltpu.make_async_copy(acc0_ref, acc0, x_sems.at[4]))
    for c in x_copies[:1] + copies_p + x_copies[1:4] + copies_q + x_copies[4:]:
        c.start()
    far_in = [
        pltpu.make_async_copy(ref, far.at[pl.ds(i * 160, 160)], far_sems.at[i])
        for i, ref in enumerate((here_ref, there_ref))
    ]
    far_out = pltpu.make_async_copy(far, far_ref, far_sems.at[2])
    for c in far_in:
        c.start()
    sums = sq0_ref[...]
    for c in x_copies[:1] + copies_p:
        c.wait()
    part, sums = absorb(xp[...], gp_ref, places_p, wp[...], sums)
    acc[...] = part
    for g in range(3):
        for c in x_copies[1 + g : 2 + g] + copies_q[6 * g : 6 * g + 6]:
            c.wait()
        part, sums = absorb(xq[g], gq_ref, places_q[g], wq[g], sums)
        acc[...] += part
    x_copies[4].wait()
    acc[...] += acc0[...]
    for c in far_in:
        c.wait()
    far_out.start()
    mean_square = jnp.sum(sums, axis=1, keepdims=True) * (1.0 / D) + 1e-05
    inverse = lax.rsqrt(mean_square)
    cosines, sines = cos_ref[...], sin_ref[...]
    queries_at = lax.broadcasted_iota(jnp.int32, (TOK, TOK), 0)
    keys_at = lax.broadcasted_iota(jnp.int32, (TOK, TOK), 1)
    allowed = (seg_col_ref[...] == seg_row_ref[...]) & (keys_at <= queries_at)
    scale = HD ** (-0.5)
    row_dot = jnp.zeros((TOK, HD), F32)
    for h in range(HEADS):
        at = [slice(n * HEADS * HD + h * HD, n * HEADS * HD + (h + 1) * HD) for n in range(3)]
        raw = [acc[:, s] * inverse for s in at]
        q, k, v = (r.astype(BF) for r in raw)
        qf, kf = q.astype(F32), k.astype(F32)
        qr = qf * cosines + pltpu.roll(qf, HD // 2, 1) * sines
        kr = kf * cosines + pltpu.roll(kf, HD // 2, 1) * sines
        qh, ql = split(qr)
        kh, kl = split(kr)
        scores = (dot(qh, kh, NT) + (dot(qh, kl, NT) + dot(ql, kh, NT))) * scale
        scores = jnp.where(allowed, scores, -1e30)
        weights = jnp.exp(scores - jnp.max(scores, axis=1, keepdims=True))
        weights = weights / jnp.sum(weights, axis=1, keepdims=True)
        cotangent = dctx_ref[:, h * HD : (h + 1) * HD]
        d_weights = dot(cotangent, v, NT)
        d_scores = weights * (
            d_weights - jnp.sum(weights * d_weights, axis=1, keepdims=True)
        )
        d_scores = (d_scores * scale).astype(BF)
        dv = dot(weights.astype(BF), cotangent, TN)
        dqr = dot(d_scores, kh, NN)
        dkr = dot(d_scores, qh, TN)
        dq = dqr * cosines + pltpu.roll(dqr * sines, HD // 2, 1)
        dk = dkr * cosines + pltpu.roll(dkr * sines, HD // 2, 1)
        for s, r, g in zip(at, raw, (dq, dk, dv)):
            row_dot += r * g
            dp_ref[:, s] = (g * inverse).astype(BF)
    stat_ref[...] = jnp.broadcast_to(inverse * inverse, (TOK, HD))
    ones = jnp.ones((16, HD), BF)
    lane_ref[...] = sum(dot(ones, part, NT) for part in thirds(row_dot * (1.0 / D)))[:8]
    far_out.wait()


def pick(place_ref, quarter_ref, xp_ref, xq_ref, gp_ref, gq_ref, mine_ref, theirs_ref):
    wanted = lax.broadcasted_iota(jnp.int32, (320, SHARE), 0)
    wanted = jnp.where(
        wanted < 160, wanted + 160 * quarter_ref[0], wanted - 160 + 160 * quarter_ref[1]
    )
    unit = lax.broadcasted_iota(jnp.int32, (320, SHARE), 1) == wanted
    unit = jnp.where(unit, 1.0, 0.0).astype(BF)
    for dy in range(2):
        for k in range(4):
            t = place_ref[dy * 4 + k]
            xp = xp_ref[dy, :, k * PW : (k + 1) * PW].astype(F32) * gp_ref[t]
            xq = xq_ref[k, :, dy * QW : (dy + 1) * QW].astype(F32) * gq_ref[t]
            rows = dot(unit[:, :PW], xp.astype(BF), NT) + dot(unit[:, PW:], xq.astype(BF), NT)
            rows = rows.astype(BF)
            mine_ref[t, :, :TOK] = rows[:160]
            mine_ref[t, :, TOK:] = jnp.zeros((160, 64), BF)
            theirs_ref[t, :, :TOK] = rows[160:]
            theirs_ref[t, :, TOK:] = jnp.zeros((160, 64), BF)


def feature_gradient(
    place_ref, source_ref, quarter_ref, dp_ref, ph_ref, pt_ref, q0_ref, q1_ref, q2_ref, q3_ref,
    gp_ref, gq_ref, w_ref, out_ref, gain_ref, mine_ref, theirs_ref,
    ws, xp, xq, result, mine, theirs, sems, x_sems, out_sems,
):
    order = [(k, dy) for k in (1, 3, 2, 0) for dy in (0, 1)]
    copies = []
    for n, (k, dy) in enumerate(order):
        copies.append(fetch(w_ref, place_ref[dy * 4 + k], 0, SHARE, ws.at[n], 0, sems.at[n]))
    x_copies = [
        pltpu.make_async_copy(ref, slot, x_sems.at[i])
        for i, (ref, slot) in enumerate(
            (
                (ph_ref, xp.at[0]), (pt_ref, xp.at[1]), (q0_ref, xq.at[0]),
                (q1_ref, xq.at[1]), (q2_ref, xq.at[2]), (q3_ref, xq.at[3]),
            )
        )
    ]
    for c in copies[0] + x_copies + [c for group in copies[1:] for c in group]:
        c.start()
    dp = dp_ref[...]
    left = []

    def send(source, target, n):
        c = pltpu.make_async_copy(source, target, out_sems.at[n])
        c.start()
        left.append(c)

    for n, (k, dy) in enumerate(order):
        for c in copies[n]:
            c.wait()
        exact = dot(dp, ws[n], NT)
        if n == 0:
            for c in x_copies:
                c.wait()
        back = (4 - k) % 4
        row = pl.ds(place_ref[dy * 4 + k], 1)
        x_part = xp[dy, :, back * PW : (back + 1) * PW].astype(F32)
        gain_ref[row, :PW] = jnp.sum(exact[:, :PW] * x_part, axis=0, keepdims=True)
        x_part = xq[back, :, dy * QW : (dy + 1) * QW].astype(F32)
        gain_ref[row, PW:] = jnp.sum(exact[:, PW:] * x_part, axis=0, keepdims=True)
        result[n] = exact.astype(BF)
        send(result.at[n], out_ref.at[place_ref[dy * 4 + k]], n)
        if n == 3:
            pick(source_ref, quarter_ref, xp, xq, gp_ref, gq_ref, mine, theirs)
            send(theirs, theirs_ref, 8)
            send(mine, mine_ref, 9)
    for c in left:
        c.wait()


def weight_gradient(
    distances, owner_ref, slot_ref, own_ref, core_ref, f0, f1, f2, f3, d0, d1, d2, d3, *rest
):
    out_refs, rest = rest[: len(distances)], rest[len(distances) :]
    near, far, d_near, d_far, result, sems, near_sems, far_sems, out_sems = rest
    d_copies = [
        pltpu.make_async_copy(d0, d_near.at[pl.ds(0, TOK)], sems.at[0]),
        pltpu.make_async_copy(d1, d_near.at[pl.ds(384, TOK)], sems.at[1]),
        pltpu.make_async_copy(d2, d_far.at[pl.ds(0, TOK)], sems.at[2]),
        pltpu.make_async_copy(d3, d_far.at[pl.ds(TOK, TOK)], sems.at[3]),
    ]
    copies = []
    for i, r in enumerate(distances):
        rows = pl.ds(i * 160, 160)
        t = owner_ref[r]
        copies += [
            pltpu.make_async_copy(own_ref.at[t], near.at[rows, pl.ds(0, 384)], near_sems.at[i, 0]),
            pltpu.make_async_copy(core_ref.at[t], near.at[rows, pl.ds(384, 384)], near_sems.at[i, 1]),
        ]
    wanted = []
    for k, f in enumerate((f0, f1, f2, f3)):
        for dy in range(2):
            n = dy * 4 + k
            hit = slot_ref[n] == distances[0]
            for r in distances[1:]:
                hit = hit | (slot_ref[n] == r)
            c = pltpu.make_async_copy(f.at[pl.ds(dy * 160, 160)], far.at[slot_ref[n]], far_sems.at[n])
            wanted.append((hit, c))
    for c in d_copies + copies:
        c.start()
    for hit, c in wanted:
        pl.when(hit)(c.start)
    d_near[TOK:384] = jnp.zeros((64, COLS), BF)
    d_near[384 + TOK :] = jnp.zeros((64, COLS), BF)
    for c in d_copies + copies:
        c.wait()
    for hit, c in wanted:
        pl.when(hit)(c.wait)
    at, left = 0, []
    while at < len(distances):
        count = min(2, len(distances) - at)
        group = distances[at : at + count]
        x_far = jnp.concatenate([far[r] for r in group], axis=0) if count > 1 else far[group[0]]
        total = dot(near[at * 160 : (at + count) * 160], d_near[...], NN) + dot(x_far, d_far[...], NN)
        for i in range(count):
            result[at + i] = total[i * 160 : (i + 1) * 160].astype(BF)
            c = pltpu.make_async_copy(result.at[at + i], out_refs[at + i], out_sems.at[at + i])
            c.start()
            left.append(c)
        at += count
    for c in left:
        c.wait()


def finish(own_ref, down_ref, up_ref, out_ref):
    total = own_ref[...].astype(F32) + (down_ref[...].astype(F32) + up_ref[...].astype(F32))
    for n in range(3):
        out_ref[n] = total[:, n * HEADS * HD : (n + 1) * HEADS * HD].astype(BF)


VM = pl.BlockSpec(memory_space=pltpu.VMEM)
SM = pl.BlockSpec(memory_space=pltpu.SMEM)
ANY = pl.BlockSpec(memory_space=pl.ANY)
SMALL = pl.CostEstimate(flops=1000, bytes_accessed=1000, transcendentals=0)


def limit(mib):
    return pltpu.CompilerParams(vmem_limit_bytes=mib * 1024 * 1024)


def shift(values, axis, by, size):
    return lax.ppermute(values, axis, [(i, (i + by) % size) for i in range(size)])


def swap(values, axis, bit, size):
    return lax.ppermute(values, axis, [(i, i ^ bit) for i in range(size)])


def body(x_own, gain, w_qkv, segments, d_context):
    yh, core = lax.axis_index("yh"), lax.axis_index("core")
    yl, x_at = lax.axis_index("yl"), lax.axis_index("x")
    ks = jnp.arange(4, dtype=jnp.int32)
    rows = [yl, 1 - yl]
    sources = jnp.concatenate([r * 4 + (x_at - ks) % 4 for r in rows]).astype(jnp.int32)
    targets = jnp.concatenate([r * 4 + (x_at + ks) % 4 for r in rows]).astype(jnp.int32)
    gain_own = lax.dynamic_slice_in_dim(gain, (yl * 4 + x_at) * SHARE, SHARE, 0)

    xp, xq = x_own[:, :PW], x_own[:, PW:]
    got_p = [shift(xp, "x", k, 4) for k in (1, 2, 3)]
    got_q = swap(xq, "yl", 1, 2)
    scaled = (x_own.astype(F32) * gain_own).astype(BF).T.reshape(2, 2, 160, TOK)
    other = lax.dynamic_index_in_dim(scaled, 1 - yh, 0, False)
    other = jnp.stack([lax.dynamic_index_in_dim(other, c, 0, False) for c in (core, 1 - core)])
    other, got_p, got_q = lax.optimization_barrier((other, got_p, got_q))
    p_here = jnp.concatenate([xp] + got_p, axis=1)
    q_here = jnp.concatenate([xq, got_q], axis=1)
    p_there = swap(p_here, "yl", 1, 2)
    q_there = [shift(q_here, "x", k, 4) for k in (1, 2, 3)]
    other = swap(other, "yh", 1, 2)

    weight = w_qkv.transpose(1, 0, 2)
    gains = gain.reshape(8, 1, SHARE)
    gain_p, gain_q = gains[:, :, :PW], gains[:, :, PW:]
    acc, squares = pl.pallas_call(
        project_first,
        out_shape=(
            jax.ShapeDtypeStruct((TOK, COLS), F32),
            jax.ShapeDtypeStruct((TOK, 128), F32),
        ),
        in_specs=[SM, VM, VM, VM, VM, ANY],
        out_specs=(VM, VM),
        scratch_shapes=[
            pltpu.VMEM((4 * PW, COLS), BF),
            pltpu.VMEM((2 * QW, COLS), BF),
            pltpu.SemaphoreType.DMA((6, 3)),
        ],
        compiler_params=limit(63),
        cost_estimate=SMALL,
        name="project_first",
    )(sources, p_here, q_here, gain_p, gain_q, weight)

    acc, other = lax.optimization_barrier((acc, other))
    quarter = jnp.concatenate([other[0], swap(other[1], "core", 1, 2)], axis=1)
    acc, quarter = lax.optimization_barrier((acc, quarter))
    quarter_there = swap(quarter, "yl", 1, 2)

    half = HD // 2
    angles = jnp.arange(TOK, dtype=F32)[:, None] * (
        10000.0 ** (-(2.0 * jnp.arange(half, dtype=F32)) / HD)
    )
    cosines, sines = jnp.cos(angles), jnp.sin(angles)
    cosines = jnp.concatenate([cosines, cosines], axis=1)
    sines = jnp.concatenate([-sines, sines], axis=1)
    d_packed, stats, row_dots, far_own = pl.pallas_call(
        attention,
        out_shape=(
            jax.ShapeDtypeStruct((TOK, COLS), BF),
            jax.ShapeDtypeStruct((TOK, HD), F32),
            jax.ShapeDtypeStruct((8, TOK), F32),
            jax.ShapeDtypeStruct((320, 640), BF),
        ),
        in_specs=[SM, ANY, VM] + [ANY] * 4 + [VM] * 7 + [ANY] * 3,
        out_specs=(VM, VM, VM, ANY),
        scratch_shapes=[
            pltpu.VMEM((TOK, COLS), F32),
            pltpu.VMEM((TOK, COLS), F32),
            pltpu.VMEM((TOK, 4 * PW), BF),
            pltpu.VMEM((3, TOK, WIDE), BF),
            pltpu.VMEM((4 * PW, COLS), BF),
            pltpu.VMEM((3, 2 * QW, COLS), BF),
            pltpu.VMEM((320, 640), BF),
            pltpu.SemaphoreType.DMA((10, 3)),
            pltpu.SemaphoreType.DMA((5,)),
            pltpu.SemaphoreType.DMA((3,)),
        ],
        compiler_params=limit(63),
        cost_estimate=SMALL,
        name="attention",
    )(
        sources, acc, squares, p_there, *q_there, gain_p, gain_q, cosines, sines,
        segments[:, None], segments[None, :], d_context, weight, quarter, quarter_there,
    )

    far = [far_own]
    from_yh = swap(d_packed, "yh", 1, 2)
    from_core = swap(d_packed, "core", 1, 2)
    far = far + [shift(far[0], "x", k, 4) for k in (1, 2, 3)]
    quarters = jnp.stack([yh * 2 + core, yh * 2 + 1 - core]).astype(jnp.int32)
    shares, gains_here, x_mine, x_theirs = pl.pallas_call(
        feature_gradient,
        out_shape=tuple(
            [jax.ShapeDtypeStruct((8, TOK, SHARE), BF)]
            + [jax.ShapeDtypeStruct((8, SHARE), F32)]
            + [jax.ShapeDtypeStruct((8, 160, 384), BF)] * 2
        ),
        in_specs=[SM] * 3 + [VM] + [ANY] * 6 + [VM] * 2 + [ANY],
        out_specs=(ANY, VM, ANY, ANY),
        scratch_shapes=[
            pltpu.VMEM((8, SHARE, COLS), BF),
            pltpu.VMEM((2, TOK, 4 * PW), BF),
            pltpu.VMEM((4, TOK, WIDE), BF),
            pltpu.VMEM((8, TOK, SHARE), BF),
            pltpu.VMEM((8, 160, 384), BF),
            pltpu.VMEM((8, 160, 384), BF),
            pltpu.SemaphoreType.DMA((8, 3)),
            pltpu.SemaphoreType.DMA((6,)),
            pltpu.SemaphoreType.DMA((10,)),
        ],
        compiler_params=limit(63),
        cost_estimate=SMALL,
        name="feature_gradient",
    )(
        targets, sources, quarters, d_packed, p_here, p_there, q_here, *q_there, gain_p, gain_q, weight,
    )
    from_yh, from_core, far, x_theirs, gains, shares = lax.optimization_barrier(
        (from_yh, from_core, far, x_theirs, gains_here, shares)
    )
    d_normed = lax.psum_scatter(shares, ("yl", "x"), scatter_dimension=0, tiled=False)
    from_both = swap(from_yh, "core", 1, 2)
    x_core = swap(x_theirs, "core", 1, 2)
    from_both, x_core, gains = lax.optimization_barrier((from_both, x_core, gains))

    z_at = lax.axis_index("z")
    owners = ((z_at + jnp.arange(8)) % 8).astype(jnp.int32)
    slots = ((sources - z_at) % 8).astype(jnp.int32)
    operands = (owners, slots, x_mine, x_core, *far, d_packed, from_core, from_yh, from_both)

    def rows_for(distances, name):
        call = pl.pallas_call(
            functools.partial(weight_gradient, distances),
            out_shape=(jax.ShapeDtypeStruct((160, COLS), BF),) * len(distances),
            in_specs=[SM, SM] + [ANY] * 10,
            out_specs=(ANY,) * len(distances),
            scratch_shapes=[
                pltpu.VMEM((len(distances) * 160, 768), BF),
                pltpu.VMEM((8, 160, 640), BF),
                pltpu.VMEM((768, COLS), BF),
                pltpu.VMEM((640, COLS), BF),
                pltpu.VMEM((len(distances), 160, COLS), BF),
                pltpu.SemaphoreType.DMA((4,)),
                pltpu.SemaphoreType.DMA((len(distances), 2)),
                pltpu.SemaphoreType.DMA((8,)),
                pltpu.SemaphoreType.DMA((len(distances),)),
            ],
            compiler_params=limit(32),
            cost_estimate=SMALL,
            name=name,
        )
        return list(call(*operands))

    def plus(a, b):
        return (a.astype(F32) + b.astype(F32)).astype(BF)

    there = swap(gains, "z", 1, 8)
    far_rows = rows_for((4,), "weight_gradient_far")[0]
    far_rows, there = lax.optimization_barrier((far_rows, there))
    gains = gains + there
    down = shift(far_rows, "z", 1, 8)
    there = swap(gains, "z", 2, 8)
    rest = rows_for((3, 5), "weight_gradient_middle")
    down, there, rest[0] = lax.optimization_barrier((down, there, rest[0]))
    gains = gains + there
    down = shift(plus(rest[0], down), "z", 1, 8)
    up = shift(rest[1], "z", -1, 8)
    there = swap(gains, "z", 4, 8)
    rest += rows_for((2, 6, 1, 7, 0), "weight_gradient_near")
    down, up, there, rest[2] = lax.optimization_barrier((down, up, there, rest[2]))
    gains = (gains + there).reshape(2, 4, SHARE)
    down = shift(plus(rest[2], down), "z", 1, 8)
    up = shift(plus(rest[3], up), "z", -1, 8)
    row_dots = jnp.pad(row_dots[:1], ((0, 0), (0, SHARE - TOK)))
    empty = jnp.zeros((5, SHARE), F32)
    small = [
        jnp.concatenate([lax.dynamic_index_in_dim(gains, x_at ^ bit, 1, False), row_dots, empty])
        for bit in range(4)
    ]
    small = small[:1] + [swap(small[bit], "x", bit, 4) for bit in (1, 2, 3)]
    down, up, small = lax.optimization_barrier((down, up, small))
    small = (small[0] + small[1]) + (small[2] + small[3])
    down = shift(plus(rest[4], down), "z", 1, 8)
    up = shift(plus(rest[5], up), "z", -1, 8)
    there = swap(small, "yl", 1, 2)
    row_dot = small[2, :TOK] + there[2, :TOK]
    share = lax.dynamic_index_in_dim(small, yl, 0, False) + lax.dynamic_index_in_dim(there, yl, 0, False)
    share = share + swap(share, "yh", 1, 2)
    share = share + swap(share, "core", 1, 2)
    down, up, share = lax.optimization_barrier((down, up, share))
    row_dot = row_dot * stats[:, 0]
    input_gradient = d_normed.astype(F32) * gain_own - x_own.astype(F32) * row_dot[:, None]
    d_weight = pl.pallas_call(
        finish,
        out_shape=jax.ShapeDtypeStruct((3, 160, HEADS * HD), BF),
        in_specs=[VM] * 3,
        out_specs=VM,
        compiler_params=limit(8),
        cost_estimate=SMALL,
        name="finish",
    )(rest[6], down, up)
    return input_gradient.astype(BF), share, d_weight.transpose(1, 0, 2)


def solution(mesh):
    fine = Mesh(mesh.devices.reshape(8, 2, 2, 2, 4), ("z", "yh", "core", "yl", "x"))
    dp, tensor = ("z", "yh", "core"), ("yl", "x")
    in_specs = (P(dp, tensor), P(), P(None, None, tensor), P(dp), P(dp, tensor))
    out_specs = (P(dp, tensor), P(tensor), P(dp, None, tensor))
    return jax.shard_map(
        body, mesh=fine, in_specs=in_specs, out_specs=out_specs, check_vma=False
    )
```
